256 devices in a mesh: cells: 64 (over z, x, core), genes: 4 (over y).
Axes of the slice: x: 4, y: 4, z: 8, core: 2. Of those that a mesh axis runs over, the one named last changes fastest.
Arguments:
- expression: bfloat16 [65536, 2048], P('cells', 'genes'), may hold values from -6 to 6
- affinity: bfloat16 [512, 12, 128, 128], P('cells'), may hold values from -0.15625 to 0.15625
- near_blocks: int32 [512, 4], P('cells'), may hold values from 0 to 511, as said below
- far_blocks: int32 [512, 8], P('cells'), may hold values from 0 to 511, as said below
- far_count: int32 [512], P('cells'), may hold values from 1 to 8, as said below
Outputs:
- smoothed: bfloat16 [65536, 2048], P('cells', 'genes')
- covariance: float32 [2048, 2048], P('cells', 'genes')
The draws below stay inside these ranges and needn't reach their ends.
Inputs may be any that keep to these rules, and one draw needn't show every extreme that they name: near_blocks[b, 0] = b, and every entry names a block of the same shard of 8 consecutive blocks as b. `far_blocks`: over the 8 x 8 entries of the blocks of one shard, every shard owns exactly 1 of the named blocks; a block may be named more than once. `far_count`: in every draw some shard has all its counts equal to 8.
All inputs are finite; a program needn't handle non-finite values.
Results may differ from the reference program's by a relative error of at most 0.0049.
Values may be sent and summed in bfloat16 or wider, within the bound.
A program may use at most 192 MiB of HBM per device.

```python
import jax
import jax.numpy as jnp
from jax import lax

G = 2048
BL = 128
BLK_DEV = 8
LOC = 4
FAR = 8
STEPS = 2
BLOCKS = 512
CELLS = 65536


def draw_near_blocks(key, part):
    key = jax.random.fold_in(key, 13)
    numbers = jnp.arange(BLOCKS, dtype=jnp.int32)
    base = numbers // BLK_DEV * BLK_DEV
    picks = jax.random.randint(key, (BLOCKS, LOC), 0, BLK_DEV, dtype=jnp.int32)
    result = base[:, None] + picks
    result = result.at[:, 0].set(numbers)
    return result.astype(jnp.int32)


def draw_far_blocks(key, part):
    key = jax.random.fold_in(key, 11)
    shard_total = BLOCKS // BLK_DEV
    keys = jax.random.split(key, shard_total + 1)
    perms = jax.vmap(lambda single: jax.random.permutation(single, shard_total))(keys[:shard_total])
    positions = jnp.arange(BLK_DEV * FAR, dtype=jnp.int32) % shard_total
    owners = perms[:, positions].astype(jnp.int32)
    picks = jax.random.randint(keys[shard_total], (shard_total, BLK_DEV * FAR), 0, BLK_DEV, dtype=jnp.int32)
    leading = (jnp.arange(BLK_DEV * FAR, dtype=jnp.int32) < shard_total)[None, :]
    picks = jnp.where(leading & (owners == 0), 0, picks)
    picks = jnp.where(leading & (owners == shard_total - 1), BLK_DEV - 1, picks)
    return (owners * BLK_DEV + picks).reshape(BLOCKS, FAR).astype(jnp.int32)


def draw_far_count(key, part):
    key = jax.random.fold_in(key, 12)
    shard_total = BLOCKS // BLK_DEV
    first_key, second_key = jax.random.split(key)
    full_shard = jax.random.randint(first_key, (), 0, shard_total, dtype=jnp.int32)
    counts = jax.random.randint(second_key, (shard_total, BLK_DEV), 1, FAR + 1, dtype=jnp.int32)
    shards = jnp.arange(shard_total, dtype=jnp.int32)[:, None]
    counts = jnp.where(shards == full_shard, FAR, counts)
    return counts.reshape(BLOCKS).astype(jnp.int32)


def shard_levels(key, extent, cuts, least, high):
    loudness, own = 1.0, jax.random.fold_in(key, 6)
    for axis_at, parts in cuts:
        steps = jnp.exp(jax.random.uniform(jax.random.fold_in(own, axis_at), (parts,), jnp.float32, least / len(cuts), high / len(cuts)))
        loudness = loudness * jnp.repeat(steps, extent[axis_at] // parts).reshape([-1 if axis == axis_at else 1 for axis in range(len(extent))])
    return loudness


def centred(rng, shape, spread, bound, cuts=(), held_as=jnp.bfloat16):
    values = jax.random.normal(rng, shape, jnp.float32) * spread
    if len(cuts) > 0:
        values = shard_levels(rng, shape, cuts, -0.22, 0.18) * values
    return jnp.clip(values, min=-bound, max=bound).astype(held_as)


def setup_inputs(seed: int = 0) -> dict:
    key_list = jax.random.split(jax.random.key(seed), 6)
    return {
        "expression": centred(key_list[0], (CELLS, G), 1.0, 6.0, ((0, 64), (1, 4))),
        "affinity": centred(key_list[1], (BLOCKS, LOC + FAR, BL, BL), (BL * (LOC + FAR)) ** -0.5, 0.15625, ((0, 64),)),
        "near_blocks": draw_near_blocks(jax.random.fold_in(key_list[5], 71), 0),
        "far_blocks": draw_far_blocks(jax.random.fold_in(key_list[5], 71), 0),
        "far_count": draw_far_count(jax.random.fold_in(key_list[5], 71), 0),
    }


def reference(expression, affinity, near_blocks, far_blocks, far_count):
    nblocks = near_blocks.shape[0]
    shard_total = nblocks // BLK_DEV
    live_slots = jnp.arange(FAR, dtype=jnp.int32)[None, :] < far_count[:, None]
    slot_mask = jnp.concatenate([jnp.ones((nblocks, LOC), dtype=bool), live_slots], axis=1)
    weights = jnp.where(slot_mask[:, :, None, None], affinity, jnp.zeros_like(affinity))
    block_lists = jnp.concatenate([near_blocks, far_blocks], axis=1).astype(jnp.int32)
    current = expression
    for iteration in range(STEPS):
        blocks = current.reshape(nblocks, BL, G)

        def one_shard(shard_index):
            first = (shard_index * BLK_DEV).astype(jnp.int32)
            shard_weights = lax.dynamic_slice_in_dim(weights, first, BLK_DEV, 0).astype(jnp.float32)
            shard_lists = lax.dynamic_slice_in_dim(block_lists, first, BLK_DEV, 0)
            neighbours = blocks[shard_lists].astype(jnp.float32)
            return jnp.einsum("bkij,bkjg->big", shard_weights, neighbours)

        smoothed_blocks = lax.map(one_shard, jnp.arange(shard_total, dtype=jnp.int32))
        current = smoothed_blocks.reshape(nblocks * BL, G).astype(jnp.bfloat16)
    covariance = jnp.dot(current.T, current, preferred_element_type=jnp.float32) / (nblocks * BL)
    return current, covariance
```

```python
import functools

import jax
import jax.numpy as jnp
from jax import lax
from jax.experimental import pallas as pl
from jax.experimental.pallas import tpu as pltpu
from jax.sharding import PartitionSpec as P

MESH = pl.DeviceIdType.MESH
NX = 4
NY = 4
BL = 128
BLK = 8
SLOTS = 12


def remote(src, dst, send, recv, device):
    return pltpu.make_async_remote_copy(
        src_ref=src, dst_ref=dst, send_sem=send, recv_sem=recv, device_id=device, device_id_type=MESH
    )


def diffuse_kernel(
    nz, expr, aff, lists, out, x0, x1, x2, w, lv, ls,
    loc, xs_s, xs_r, li_s, li_r, wx_s, wx_r, wf_s, wf_r, wy_s, wy_r,
    z_s, z_r, p_s, p_r, o_s, o_r,
):
    flow_len = 4 * (nz // 2) - 2
    me = lax.axis_index("cells")
    y = lax.axis_index("genes")
    core = lax.rem(me, 2)
    x = lax.rem(me // 2, NX)
    z = me // (2 * NX)
    half = lax.rem(y, 2)

    def cell(zz, xx, kk):
        return (zz * NX + xx) * 2 + kk

    def wrap(v, n):
        return lax.rem(v + n, n)

    def x_dev(d):
        return (cell(z, wrap(x + d, NX), core), y)

    right = (cell(wrap(z + 1, nz), x, core), y)
    left = (cell(wrap(z - 1, nz), x, core), y)
    partner = (cell(z, x, 1 - core), y)
    up = (me, wrap(y + 1, NY))
    down = (me, wrap(y - 1, NY))

    barrier = pltpu.get_barrier_semaphore()
    peers = [x_dev(1), x_dev(2), x_dev(3), right, left, partner, up, down]
    for peer in peers:
        pl.semaphore_signal(barrier, inc=1, device_id=peer, device_id_type=MESH)
    pl.semaphore_wait(barrier, len(peers))

    def piece(buf, shard):
        return buf.at[pl.ds(shard * BLK, BLK)]

    def columns(ref, xx):
        return ref.at[:, :, pl.ds(pl.multiple_of(xx * BL, BL), BL)]

    def deal(d):
        return remote(
            columns(expr, wrap(x + d, NX)), piece(x0, me), xs_s.at[d - 1], xs_r.at[d - 1], x_dev(d)
        )

    own_in = pltpu.make_async_copy(columns(expr, x), piece(x0, me), loc.at[0])
    own_in.start()
    for d in (1, 3, 2):
        deal(d).start()

    def names(d):
        return remote(lists, lv.at[x], li_s.at[d - 1], li_r.at[d - 1], x_dev(d))

    own_names = pltpu.make_async_copy(lists, lv.at[x], loc.at[1])
    own_names.start()
    for d in (1, 2, 3):
        names(d).start()

    own_w = pltpu.make_async_copy(aff, w.at[x], loc.at[2])

    def wsub(xx, hh, u):
        return w.at[xx, pl.ds(4 * hh + 2 * u, 2)]

    def w_first(way, u):
        return remote(
            aff.at[pl.ds(4 * half + 2 * u, 2)], wsub(x, half, u),
            wx_s.at[way, u], wx_r.at[way, u], x_dev(1 if way == 0 else 3),
        )

    def w_forward(way):
        ref = wsub(wrap(x - 1, NX), half, 0) if way == 0 else wsub(wrap(x + 1, NX), half, 1)
        return remote(ref, ref, wf_s.at[way], wf_r.at[way], x_dev(1 if way == 0 else 3))

    def w_across(e, u):
        ref = wsub(wrap(x + (3, 1, 2)[e], NX), half, u)
        return remote(ref, ref, wy_s.at[u, e], wy_r.at[u, e], up if u == 0 else down)

    for way, u in ((0, 0), (1, 1), (0, 1), (1, 0)):
        w_first(way, u).start()
    own_w.start()

    def w_serve(stage):
        if stage == 0:
            w_first(0, 0).wait_recv()
            w_forward(0).start()
            w_across(0, 0).start()
            w_first(1, 1).wait_recv()
            w_forward(1).start()
            w_across(1, 1).start()
        elif stage == 1:
            w_first(0, 1).wait_recv()
            w_across(0, 1).start()
            w_first(1, 0).wait_recv()
            w_across(1, 0).start()
        else:
            w_forward(0).wait_recv()
            w_across(2, 0).start()
            w_forward(1).wait_recv()
            w_across(2, 1).start()

    def shard_of(zz, j, kk):
        return cell(wrap(zz, nz), wrap(x - j, NX), kk)

    def z_copy(n, buf, way, s, shard):
        return remote(
            piece(buf, shard), piece(buf, shard), z_s.at[n, way, s], z_r.at[n, way, s],
            right if way == 0 else left,
        )

    def p_copy(n, buf, q, shard):
        return remote(piece(buf, shard), piece(buf, shard), p_s.at[n, q], p_r.at[n, q], partner)

    def from_left(r, kk):
        return shard_of(z - 1 - r // 4, lax.rem(r, 4), kk)

    def from_right(r, kk):
        j = lax.rem(r, 4) + jnp.where(r < flow_len - 2, 0, 2)
        return shard_of(z + 1 + r // 4, j, kk)

    def send_own(n, buf, j):
        shard = shard_of(z, j, core)
        z_copy(n, buf, 0, j, shard).start()
        z_copy(n, buf, 1, j, shard).start()
        p_copy(n, buf, j, shard).start()

    def pass_on(n, buf, first, last):
        @pl.loop(first, last)
        def _(r):
            shard = from_left(r, core)
            z_copy(n, buf, 0, r, shard).wait_recv()

            @pl.when(r + 4 < flow_len)
            def _():
                z_copy(n, buf, 0, r + 4, shard).start()

            p_copy(n, buf, 4 + r, shard).start()
            other = from_right(r, core)
            z_copy(n, buf, 1, r, other).wait_recv()

            @pl.when(r < flow_len - 6)
            def _():
                z_copy(n, buf, 1, r + 4, other).start()

            @pl.when((r >= flow_len - 4) & (r < flow_len - 2))
            def _():
                z_copy(n, buf, 1, r + 2, other).start()

            p_copy(n, buf, 4 + flow_len + r, other).start()

    def partner_done(n, buf):
        @pl.loop(0, 4)
        def _(j):
            p_copy(n, buf, j, shard_of(z, j, 1 - core)).wait_recv()

        @pl.loop(0, flow_len)
        def _(r):
            p_copy(n, buf, 4 + r, from_left(r, 1 - core)).wait_recv()
            p_copy(n, buf, 4 + flow_len + r, from_right(r, 1 - core)).wait_recv()

    def sends_done(n, buf):
        shard = shard_of(z, 0, core)

        @pl.loop(0, flow_len)
        def _(s):
            z_copy(n, buf, 0, s, shard).wait_send()
            z_copy(n, buf, 1, s, shard).wait_send()

        @pl.loop(0, 4 + 2 * flow_len)
        def _(q):
            p_copy(n, buf, q, shard).wait_send()

    def block_sum(buf, xs, b):
        total = None
        for pair in range(SLOTS // 2):
            rows = [buf[ls[xs, b, 2 * pair + i]] for i in range(2)]
            mats = [w[xs, b, 2 * pair + i] for i in range(2)]
            term = jnp.dot(
                jnp.concatenate(mats, axis=1), jnp.concatenate(rows, axis=0),
                preferred_element_type=jnp.float32,
            )
            total = term if total is None else total + term
        return total.astype(jnp.bfloat16)

    zeros = jnp.zeros((BL, BL), jnp.bfloat16)
    x0[nz * 2 * NX * BLK] = zeros
    x1[nz * 2 * NX * BLK] = zeros

    own_in.wait()
    send_own(0, x0, 0)
    for j in (1, 3, 2):
        deal(j).wait_recv()
        send_own(0, x0, j)
    cuts = (0, flow_len // 2 - 1, flow_len // 2 + 2, flow_len - 1, flow_len)
    for part in range(4):
        pass_on(0, x0, cuts[part], cuts[part + 1])
        if part < 3:
            w_serve(part)

    own_names.wait()
    for d in (1, 2, 3):
        names(d).wait_recv()
    to_smem = pltpu.make_async_copy(lv, ls, loc.at[1])
    to_smem.start()
    to_smem.wait()
    own_w.wait()
    partner_done(0, x0)
    for e in range(3):
        for u in range(2):
            w_across(e, u).wait_recv()

    @pl.loop(0, NX)
    def _(j):
        xs = wrap(x - j, NX)
        base = shard_of(z, j, core) * BLK

        @pl.loop(0, BLK)
        def _(b):
            x1[base + b] = block_sum(x0, xs, b)

        send_own(1, x1, j)

    pass_on(1, x1, 0, flow_len)
    partner_done(1, x1)

    def give(j):
        return remote(
            x2.at[j], columns(out, x), o_s.at[j - 1], o_r.at[j - 1],
            (cell(z, wrap(x - j, NX), core), y),
        )

    @pl.loop(0, NX)
    def _(j):
        xs = wrap(x - j, NX)

        @pl.loop(0, BLK)
        def _(b):
            x2[j, b] = block_sum(x1, xs, b)

        @pl.when(j > 0)
        def _():
            give(j).start()

    own_out = pltpu.make_async_copy(x2.at[0], columns(out, x), loc.at[0])
    own_out.start()

    for d in (1, 2, 3):
        deal(d).wait_send()
        names(d).wait_send()
        for u in range(2):
            w_across(d - 1, u).wait_send()
    for way in range(2):
        w_forward(way).wait_send()
        for u in range(2):
            w_first(way, u).wait_send()
    sends_done(0, x0)
    sends_done(1, x1)
    own_out.wait()
    for j in (1, 2, 3):
        give(j).wait()


def diffuse(expression, affinity, lists, nz):
    shards = nz * 2 * NX
    flow_len = 4 * (nz // 2) - 2
    dma = pltpu.SemaphoreType.DMA
    any_spec = pl.BlockSpec(memory_space=pl.ANY)
    return pl.pallas_call(
        functools.partial(diffuse_kernel, nz),
        out_shape=jax.ShapeDtypeStruct(expression.shape, jnp.bfloat16),
        in_specs=[any_spec] * 3,
        out_specs=any_spec,
        scratch_shapes=[
            pltpu.VMEM((shards * BLK + 1, BL, BL), jnp.bfloat16),
            pltpu.VMEM((shards * BLK + 1, BL, BL), jnp.bfloat16),
            pltpu.VMEM((NX, BLK, BL, BL), jnp.bfloat16),
            pltpu.VMEM((NX, BLK, SLOTS, BL, BL), jnp.bfloat16),
            pltpu.VMEM((NX, BLK, BL), jnp.int32),
            pltpu.SMEM((NX, BLK, BL), jnp.int32),
            dma((3,)),
            dma((3,)), dma((3,)),
            dma((3,)), dma((3,)),
            dma((2, 2)), dma((2, 2)),
            dma((2,)), dma((2,)),
            dma((2, 3)), dma((2, 3)),
            dma((2, 2, flow_len)), dma((2, 2, flow_len)),
            dma((2, 4 + 2 * flow_len)), dma((2, 4 + 2 * flow_len)),
            dma((3,)), dma((3,)),
        ],
        compiler_params=pltpu.CompilerParams(
            collective_id=0, has_side_effects=True, vmem_limit_bytes=56 * 2**20
        ),
    )(expression, affinity, lists)


def body(nz, expression, affinity, near_blocks, far_blocks, far_count):
    cell_rows = expression.shape[0]
    shard_total = nz * 2 * NX
    live = jnp.arange(far_blocks.shape[1], dtype=jnp.int32)[None, :] < far_count[:, None]
    far = jnp.where(live, far_blocks, shard_total * BLK)
    lists = jnp.concatenate([near_blocks, far], axis=1)
    lists = jnp.pad(lists, ((0, 0), (0, BL - SLOTS)))
    blocks = expression.reshape(BLK, BL, expression.shape[1])
    current = diffuse(blocks, affinity, lists, nz).reshape(expression.shape)
    whole = lax.all_gather(current, "genes", axis=1, tiled=True)
    summed = lax.psum_scatter(
        lax.dot_general(
            whole, current, (((0,), (0,)), ((), ())), preferred_element_type=jnp.float32
        ),
        "cells",
        scatter_dimension=0,
        tiled=True,
    )
    covariance = summed / (cell_rows * shard_total)
    return (current, covariance)


def solution(mesh):
    nz = mesh.shape["cells"] // (2 * NX)
    return jax.shard_map(
        functools.partial(body, nz),
        mesh=mesh,
        in_specs=(
            P("cells", "genes"),
            P("cells", None, None, None),
            P("cells", None),
            P("cells", None),
            P("cells"),
        ),
        out_specs=(P("cells", "genes"), P("cells", "genes")),
        check_vma=False,
    )
```

```python
import functools

import jax
import jax.numpy as jnp
from jax import lax
from jax.experimental import pallas as pl
from jax.experimental.pallas import tpu as pltpu
from jax.sharding import PartitionSpec as P

MESH = pl.DeviceIdType.MESH
NX = 4
NY = 4
BL = 128
BLK = 8
SLOTS = 12


def remote(src, dst, send, recv, device):
    return pltpu.make_async_remote_copy(
        src_ref=src, dst_ref=dst, send_sem=send, recv_sem=recv, device_id=device, device_id_type=MESH
    )


def diffuse_kernel(
    nz, scale, expr, aff, lists, out, cov, x0, x1, x2, w, lv, ls, s, st, gram, r1, r2, t, r3,
    loc, xs_s, xs_r, li_s, li_r, wx_s, wx_r, wf_s, wf_r, wy_s, wy_r,
    z_s, z_r, p_s, p_r, o_s, o_r, y_s, y_r, a_s, a_r, b_s, b_r, c_s, c_r,
):
    flow_len = 4 * (nz // 2) - 2
    me = lax.axis_index("cells")
    y = lax.axis_index("genes")
    core = lax.rem(me, 2)
    x = lax.rem(me // 2, NX)
    z = me // (2 * NX)
    half = lax.rem(y, 2)

    def cell(zz, xx, kk):
        return (zz * NX + xx) * 2 + kk

    def wrap(v, n):
        return lax.rem(v + n, n)

    def x_dev(d):
        return (cell(z, wrap(x + d, NX), core), y)

    def z_dev(d):
        return (cell(wrap(z + d, nz), x, core), y)

    right, left = z_dev(1), z_dev(nz - 1)
    partner = (cell(z, x, 1 - core), y)
    up = (me, wrap(y + 1, NY))
    down = (me, wrap(y - 1, NY))

    barrier = pltpu.get_barrier_semaphore()
    peers = [x_dev(d) for d in range(1, NX)] + [z_dev(d) for d in range(1, nz)]
    peers += [partner, up, down]
    for peer in peers:
        pl.semaphore_signal(barrier, inc=1, device_id=peer, device_id_type=MESH)
    pl.semaphore_wait(barrier, len(peers))

    def piece(buf, shard):
        return buf.at[pl.ds(shard * BLK, BLK)]

    def columns(ref, xx):
        return ref.at[:, :, pl.ds(pl.multiple_of(xx * BL, BL), BL)]

    def deal(d):
        return remote(
            columns(expr, wrap(x + d, NX)), piece(x0, me), xs_s.at[d - 1], xs_r.at[d - 1], x_dev(d)
        )

    own_in = pltpu.make_async_copy(columns(expr, x), piece(x0, me), loc.at[0])
    own_in.start()
    for d in (1, 3, 2):
        deal(d).start()

    def names(d):
        return remote(lists, lv.at[x], li_s.at[d - 1], li_r.at[d - 1], x_dev(d))

    own_names = pltpu.make_async_copy(lists, lv.at[x], loc.at[1])
    own_names.start()
    for d in (1, 2, 3):
        names(d).start()

    own_w = pltpu.make_async_copy(aff, w.at[x], loc.at[2])

    def wsub(xx, hh, u):
        return w.at[xx, pl.ds(4 * hh + 2 * u, 2)]

    def w_first(way, u):
        return remote(
            aff.at[pl.ds(4 * half + 2 * u, 2)], wsub(x, half, u),
            wx_s.at[way, u], wx_r.at[way, u], x_dev(1 if way == 0 else 3),
        )

    def w_forward(way):
        ref = wsub(wrap(x - 1, NX), half, 0) if way == 0 else wsub(wrap(x + 1, NX), half, 1)
        return remote(ref, ref, wf_s.at[way], wf_r.at[way], x_dev(1 if way == 0 else 3))

    def w_across(e, u):
        ref = wsub(wrap(x + (3, 1, 2)[e], NX), half, u)
        return remote(ref, ref, wy_s.at[u, e], wy_r.at[u, e], up if u == 0 else down)

    for way, u in ((0, 0), (1, 1), (0, 1), (1, 0)):
        w_first(way, u).start()
    own_w.start()

    def w_serve(stage):
        if stage == 0:
            w_first(0, 0).wait_recv()
            w_forward(0).start()
            w_across(0, 0).start()
            w_first(1, 1).wait_recv()
            w_forward(1).start()
            w_across(1, 1).start()
        elif stage == 1:
            w_first(0, 1).wait_recv()
            w_across(0, 1).start()
            w_first(1, 0).wait_recv()
            w_across(1, 0).start()
        else:
            w_forward(0).wait_recv()
            w_across(2, 0).start()
            w_forward(1).wait_recv()
            w_across(2, 1).start()

    def shard_of(zz, j, kk):
        return cell(wrap(zz, nz), wrap(x - j, NX), kk)

    def z_copy(n, buf, way, s, shard):
        return remote(
            piece(buf, shard), piece(buf, shard), z_s.at[n, way, s], z_r.at[n, way, s],
            right if way == 0 else left,
        )

    def p_copy(n, buf, q, shard):
        return remote(piece(buf, shard), piece(buf, shard), p_s.at[n, q], p_r.at[n, q], partner)

    def from_left(r, kk):
        return shard_of(z - 1 - r // 4, lax.rem(r, 4), kk)

    def from_right(r, kk):
        j = lax.rem(r, 4) + jnp.where(r < flow_len - 2, 0, 2)
        return shard_of(z + 1 + r // 4, j, kk)

    def send_own(n, buf, j):
        shard = shard_of(z, j, core)
        z_copy(n, buf, 0, j, shard).start()
        z_copy(n, buf, 1, j, shard).start()
        p_copy(n, buf, j, shard).start()

    def pass_on(n, buf, first, last):
        @pl.loop(first, last)
        def _(r):
            shard = from_left(r, core)
            z_copy(n, buf, 0, r, shard).wait_recv()

            @pl.when(r + 4 < flow_len)
            def _():
                z_copy(n, buf, 0, r + 4, shard).start()

            p_copy(n, buf, 4 + r, shard).start()
            other = from_right(r, core)
            z_copy(n, buf, 1, r, other).wait_recv()

            @pl.when(r < flow_len - 6)
            def _():
                z_copy(n, buf, 1, r + 4, other).start()

            @pl.when((r >= flow_len - 4) & (r < flow_len - 2))
            def _():
                z_copy(n, buf, 1, r + 2, other).start()

            p_copy(n, buf, 4 + flow_len + r, other).start()

    def partner_done(n, buf):
        @pl.loop(0, 4)
        def _(j):
            p_copy(n, buf, j, shard_of(z, j, 1 - core)).wait_recv()

        @pl.loop(0, flow_len)
        def _(r):
            p_copy(n, buf, 4 + r, from_left(r, 1 - core)).wait_recv()
            p_copy(n, buf, 4 + flow_len + r, from_right(r, 1 - core)).wait_recv()

    def sends_done(n, buf):
        shard = shard_of(z, 0, core)

        @pl.loop(0, flow_len)
        def _(s):
            z_copy(n, buf, 0, s, shard).wait_send()
            z_copy(n, buf, 1, s, shard).wait_send()

        @pl.loop(0, 4 + 2 * flow_len)
        def _(q):
            p_copy(n, buf, q, shard).wait_send()

    def block_sum(buf, xs, b):
        total = None
        for pair in range(SLOTS // 2):
            rows = [buf[ls[xs, b, 2 * pair + i]] for i in range(2)]
            mats = [w[xs, b, 2 * pair + i] for i in range(2)]
            term = jnp.dot(
                jnp.concatenate(mats, axis=1), jnp.concatenate(rows, axis=0),
                preferred_element_type=jnp.float32,
            )
            total = term if total is None else total + term
        return total.astype(jnp.bfloat16)

    zeros = jnp.zeros((BL, BL), jnp.bfloat16)
    x0[nz * 2 * NX * BLK] = zeros
    x1[nz * 2 * NX * BLK] = zeros

    own_in.wait()
    send_own(0, x0, 0)
    for j in (1, 3, 2):
        deal(j).wait_recv()
        send_own(0, x0, j)
    cuts = (0, flow_len // 2 - 1, flow_len // 2 + 2, flow_len - 1, flow_len)
    for part in range(4):
        pass_on(0, x0, cuts[part], cuts[part + 1])
        if part < 3:
            w_serve(part)

    own_names.wait()
    for d in (1, 2, 3):
        names(d).wait_recv()
    to_smem = pltpu.make_async_copy(lv, ls, loc.at[1])
    to_smem.start()
    to_smem.wait()
    own_w.wait()
    partner_done(0, x0)
    for e in range(3):
        for u in range(2):
            w_across(e, u).wait_recv()

    @pl.loop(0, NX)
    def _(j):
        xs = wrap(x - j, NX)
        base = shard_of(z, j, core) * BLK

        @pl.loop(0, BLK)
        def _(b):
            x1[base + b] = block_sum(x0, xs, b)

        send_own(1, x1, j)

    pass_on(1, x1, 0, flow_len)
    partner_done(1, x1)

    def give(j):
        return remote(
            x2.at[j], columns(s, x), o_s.at[j - 1], o_r.at[j - 1],
            (cell(z, wrap(x - j, NX), core), y),
        )

    @pl.loop(0, NX)
    def _(j):
        xs = wrap(x - j, NX)

        @pl.loop(0, BLK)
        def _(b):
            x2[j, b] = block_sum(x1, xs, b)

        @pl.when(j > 0)
        def _():
            give(j).start()

    def y_copy(way, n, p, j):
        ref = st.at[p, wrap(x + j, NX)]
        return remote(ref, ref, y_s.at[way, n], y_r.at[way, n], up if way == 0 else down)

    def turn(j):
        g = wrap(x + j, NX)
        for b in range(BLK):
            tile = s[b, :, pl.ds(pl.multiple_of(g * BL, BL), BL)]
            st[y, g, :, pl.ds(b * BL, BL)] = tile.T
        y_copy(0, j, y, j).start()
        y_copy(1, j, y, j).start()

    own_s = pltpu.make_async_copy(x2.at[0], columns(s, x), loc.at[0])
    own_s.start()
    own_s.wait()
    turn(0)
    for j in (1, 2, 3):
        give(j).wait_recv()
        turn(j)
    own_out = pltpu.make_async_copy(s, out, loc.at[0])
    own_out.start()

    def other_core(p, n):
        return remote(
            gram.at[pl.ds(2 * p, 2), :, 1 - core], r1.at[pl.ds(2 * p, 2)], a_s.at[n], a_r.at[n], partner
        )

    def along_x(p, n, d):
        return remote(
            r1.at[pl.ds(2 * p, 2), wrap(x + d, NX)], r2.at[d - 1, pl.ds(2 * p, 2)],
            b_s.at[n, d - 1], b_r.at[n, d - 1], x_dev(d),
        )

    def along_z(d):
        return remote(t.at[wrap(z + d, nz)], r3.at[d - 1], c_s.at[d - 1], c_r.at[d - 1], z_dev(d))

    def panel(p, n):
        @pl.loop(0, 4)
        def _(g):
            rows = jnp.dot(
                st[p, g], s[...].reshape(BLK * BL, 4 * BL), preferred_element_type=jnp.float32
            )
            gram[2 * p + g // 2, pl.ds(2 * lax.rem(g, 2), 2)] = rows.reshape(2, 2, 32, 4 * BL)

        other_core(p, n).start()

    def panel_x(p, n):
        other_core(p, n).wait_recv()
        for i in range(2):
            for xx in range(NX):
                r1[2 * p + i, xx] += gram[2 * p + i, xx, core]
        for d in (1, 3, 2):
            along_x(p, n, d).start()

    def panel_sum(p, n):
        for d in (1, 3, 2):
            along_x(p, n, d).wait_recv()
        for i in range(2):
            k = 2 * p + i
            t[k] = (r1[k, x] + r2[0, k]) + (r2[1, k] + r2[2, k])

    order = [y, wrap(y - 1, NY), wrap(y + 1, NY), wrap(y + 2, NY)]
    panel(order[0], 0)
    for j in range(4):
        y_copy(0, j, order[1], j).wait_recv()
        if j < 2:
            y_copy(0, 4 + j, order[1], j).start()
        y_copy(1, j, order[2], j).wait_recv()
        if j >= 2:
            y_copy(1, 2 + j, order[2], j).start()
    panel(order[1], 1)
    panel(order[2], 2)
    panel_x(order[0], 0)
    panel_x(order[1], 1)
    panel_x(order[2], 2)
    panel_sum(order[0], 0)
    for j in range(2):
        y_copy(0, 4 + j, order[3], j).wait_recv()
        y_copy(1, 4 + j, order[3], 2 + j).wait_recv()
    panel(order[3], 3)
    panel_sum(order[1], 1)
    panel_sum(order[2], 2)
    panel_x(order[3], 3)
    panel_sum(order[3], 3)
    for d in range(1, nz):
        along_z(d).start()
    total = t[z]
    for d in range(1, nz):
        along_z(d).wait_recv()
        total += r3[d - 1]
    cov[...] = total * scale

    for d in (1, 2, 3):
        deal(d).wait_send()
        names(d).wait_send()
        give(d).wait_send()
        for u in range(2):
            w_across(d - 1, u).wait_send()
    for way in range(2):
        w_forward(way).wait_send()
        for u in range(2):
            w_first(way, u).wait_send()
        for n in range(6):
            y_copy(way, n, y, 0).wait_send()
    sends_done(0, x0)
    sends_done(1, x1)
    for n in range(4):
        other_core(y, n).wait_send()
        for d in (1, 2, 3):
            along_x(y, n, d).wait_send()
    for d in range(1, nz):
        along_z(d).wait_send()
    own_out.wait()


def diffuse(expression, affinity, lists, nz):
    shards = nz * 2 * NX
    flow_len = 4 * (nz // 2) - 2
    dma = pltpu.SemaphoreType.DMA
    any_spec = pl.BlockSpec(memory_space=pl.ANY)
    return pl.pallas_call(
        functools.partial(diffuse_kernel, nz, 1.0 / (shards * BLK * BL)),
        out_shape=(
            jax.ShapeDtypeStruct(expression.shape, jnp.bfloat16),
            jax.ShapeDtypeStruct((32, NX * BL), jnp.float32),
        ),
        in_specs=[any_spec] * 3,
        out_specs=(any_spec, pl.BlockSpec(memory_space=pltpu.VMEM)),
        scratch_shapes=[
            pltpu.VMEM((shards * BLK + 1, BL, BL), jnp.bfloat16),
            pltpu.VMEM((shards * BLK + 1, BL, BL), jnp.bfloat16),
            pltpu.VMEM((NX, BLK, BL, BL), jnp.bfloat16),
            pltpu.VMEM((NX, BLK, SLOTS, BL, BL), jnp.bfloat16),
            pltpu.VMEM((NX, BLK, BL), jnp.int32),
            pltpu.SMEM((NX, BLK, BL), jnp.int32),
            pltpu.VMEM((BLK, BL, NX * BL), jnp.bfloat16),
            pltpu.VMEM((NY, NX, BL, BLK * BL), jnp.bfloat16),
            pltpu.VMEM((nz, NX, 2, 32, NX * BL), jnp.float32),
            pltpu.VMEM((nz, NX, 32, NX * BL), jnp.float32),
            pltpu.VMEM((NX - 1, nz, 32, NX * BL), jnp.float32),
            pltpu.VMEM((nz, 32, NX * BL), jnp.float32),
            pltpu.VMEM((nz - 1, 32, NX * BL), jnp.float32),
            dma((3,)),
            dma((3,)), dma((3,)),
            dma((3,)), dma((3,)),
            dma((2, 2)), dma((2, 2)),
            dma((2,)), dma((2,)),
            dma((2, 3)), dma((2, 3)),
            dma((2, 2, flow_len)), dma((2, 2, flow_len)),
            dma((2, 4 + 2 * flow_len)), dma((2, 4 + 2 * flow_len)),
            dma((3,)), dma((3,)),
            dma((2, 6)), dma((2, 6)),
            dma((NY,)), dma((NY,)),
            dma((NY, NX - 1)), dma((NY, NX - 1)),
            dma((nz - 1,)), dma((nz - 1,)),
        ],
        compiler_params=pltpu.CompilerParams(
            collective_id=0, has_side_effects=True, vmem_limit_bytes=61 * 2**20
        ),
    )(expression, affinity, lists)


def body(nz, expression, affinity, near_blocks, far_blocks, far_count):
    shard_total = nz * 2 * NX
    live = jnp.arange(far_blocks.shape[1], dtype=jnp.int32)[None, :] < far_count[:, None]
    far = jnp.where(live, far_blocks, shard_total * BLK)
    lists = jnp.concatenate([near_blocks, far], axis=1)
    lists = jnp.pad(lists, ((0, 0), (0, BL - SLOTS)))
    blocks = expression.reshape(BLK, BL, expression.shape[1])
    current, covariance = diffuse(blocks, affinity, lists, nz)
    return (current.reshape(expression.shape), covariance)


def solution(mesh):
    nz = mesh.shape["cells"] // (2 * NX)
    return jax.shard_map(
        functools.partial(body, nz),
        mesh=mesh,
        in_specs=(
            P("cells", "genes"),
            P("cells", None, None, None),
            P("cells", None),
            P("cells", None),
            P("cells"),
        ),
        out_specs=(P("cells", "genes"), P("cells", "genes")),
        check_vma=False,
    )
```

```python
import functools

import jax
import jax.numpy as jnp
from jax import lax
from jax.experimental import pallas as pl
from jax.experimental.pallas import tpu as pltpu
from jax.sharding import PartitionSpec as P

MESH = pl.DeviceIdType.MESH
NX = 4
NY = 4
BL = 128
BLK = 8
SLOTS = 12


def remote(src, dst, send, recv, device):
    return pltpu.make_async_remote_copy(
        src_ref=src, dst_ref=dst, send_sem=send, recv_sem=recv, device_id=device, device_id_type=MESH
    )


def diffuse_kernel(
    nz, scale, expr, aff, lists, out, cov, x0, x1, w, lv, ls, sx, st, gram, r1, r3,
    loc, xs_s, xs_r, li_s, li_r, wx_s, wx_r, wf_s, wf_r, wy_s, wy_r,
    z_s, z_r, p_s, p_r, g_s, g_r, a_s, a_r, c_s, c_r,
):
    flow_len = 4 * (nz // 2) - 2
    me = lax.axis_index("cells")
    y = lax.axis_index("genes")
    core = lax.rem(me, 2)
    x = lax.rem(me // 2, NX)
    z = me // (2 * NX)
    half = lax.rem(y, 2)

    def cell(zz, xx, kk):
        return (zz * NX + xx) * 2 + kk

    def wrap(v, n):
        return lax.rem(v + n, n)

    def x_dev(d):
        return (cell(z, wrap(x + d, NX), core), y)

    right = (cell(wrap(z + 1, nz), x, core), y)
    left = (cell(wrap(z - 1, nz), x, core), y)
    partner = (cell(z, x, 1 - core), y)
    up = (me, wrap(y + 1, NY))
    down = (me, wrap(y - 1, NY))

    def sink(n):
        return cell(2 * (n // 2) + x // 2, 2 * lax.rem(x, 2) + n % 2, core)

    def source(zz):
        return cell(zz, 2 * lax.rem(z, 2) + x // 2, core)

    barrier = pltpu.get_barrier_semaphore()
    peers = [x_dev(1), x_dev(2), x_dev(3), right, left, partner, up, down]
    for peer in peers:
        pl.semaphore_signal(barrier, inc=1, device_id=peer, device_id_type=MESH)
    for zz in range(nz):
        @pl.when(source(zz) != me)
        def _():
            pl.semaphore_signal(barrier, inc=1, device_id=(source(zz), y), device_id_type=MESH)
    pl.semaphore_wait(barrier, len(peers) + nz - jnp.where(source(z) == me, 1, 0))

    def piece(buf, shard):
        return buf.at[pl.ds(shard * BLK, BLK)]

    def columns(ref, xx):
        return ref.at[:, :, pl.ds(pl.multiple_of(xx * BL, BL), BL)]

    def deal(d):
        return remote(
            columns(expr, wrap(x + d, NX)), piece(x0, me), xs_s.at[d - 1], xs_r.at[d - 1], x_dev(d)
        )

    own_in = pltpu.make_async_copy(columns(expr, x), piece(x0, me), loc.at[0])
    own_in.start()
    for d in (1, 3, 2):
        deal(d).start()

    def names(d):
        return remote(lists, lv.at[x], li_s.at[d - 1], li_r.at[d - 1], x_dev(d))

    own_names = pltpu.make_async_copy(lists, lv.at[x], loc.at[1])
    own_names.start()
    for d in (1, 2, 3):
        names(d).start()

    own_w = pltpu.make_async_copy(aff, w.at[x], loc.at[2])

    def wsub(xx, hh, u):
        return w.at[xx, pl.ds(4 * hh + 2 * u, 2)]

    def w_first(way, u):
        return remote(
            aff.at[pl.ds(4 * half + 2 * u, 2)], wsub(x, half, u),
            wx_s.at[way, u], wx_r.at[way, u], x_dev(1 if way == 0 else 3),
        )

    def w_forward(way):
        ref = wsub(wrap(x - 1, NX), half, 0) if way == 0 else wsub(wrap(x + 1, NX), half, 1)
        return remote(ref, ref, wf_s.at[way], wf_r.at[way], x_dev(1 if way == 0 else 3))

    def w_across(e, u):
        ref = wsub(wrap(x + (3, 1, 2)[e], NX), half, u)
        return remote(ref, ref, wy_s.at[u, e], wy_r.at[u, e], up if u == 0 else down)

    for way, u in ((0, 0), (1, 1), (0, 1), (1, 0)):
        w_first(way, u).start()
    own_w.start()

    def w_serve(stage):
        if stage == 0:
            w_first(0, 0).wait_recv()
            w_forward(0).start()
            w_across(0, 0).start()
            w_first(1, 1).wait_recv()
            w_forward(1).start()
            w_across(1, 1).start()
        elif stage == 1:
            w_first(0, 1).wait_recv()
            w_across(0, 1).start()
            w_first(1, 0).wait_recv()
            w_across(1, 0).start()
        else:
            w_forward(0).wait_recv()
            w_across(2, 0).start()
            w_forward(1).wait_recv()
            w_across(2, 1).start()

    def shard_of(zz, j, kk):
        return cell(wrap(zz, nz), wrap(x - j, NX), kk)

    def z_copy(n, buf, way, s, shard):
        return remote(
            piece(buf, shard), piece(buf, shard), z_s.at[n, way, s], z_r.at[n, way, s],
            right if way == 0 else left,
        )

    def p_copy(n, buf, q, shard):
        return remote(piece(buf, shard), piece(buf, shard), p_s.at[n, q], p_r.at[n, q], partner)

    def from_left(r, kk):
        return shard_of(z - 1 - r // 4, lax.rem(r, 4), kk)

    def from_right(r, kk):
        j = lax.rem(r, 4) + jnp.where(r < flow_len - 2, 0, 2)
        return shard_of(z + 1 + r // 4, j, kk)

    def send_own(n, buf, j):
        shard = shard_of(z, j, core)
        z_copy(n, buf, 0, j, shard).start()
        z_copy(n, buf, 1, j, shard).start()
        p_copy(n, buf, j, shard).start()

    def pass_on(n, buf, first, last):
        @pl.loop(first, last)
        def _(r):
            shard = from_left(r, core)
            z_copy(n, buf, 0, r, shard).wait_recv()

            @pl.when(r + 4 < flow_len)
            def _():
                z_copy(n, buf, 0, r + 4, shard).start()

            p_copy(n, buf, 4 + r, shard).start()
            other = from_right(r, core)
            z_copy(n, buf, 1, r, other).wait_recv()

            @pl.when(r < flow_len - 6)
            def _():
                z_copy(n, buf, 1, r + 4, other).start()

            @pl.when((r >= flow_len - 4) & (r < flow_len - 2))
            def _():
                z_copy(n, buf, 1, r + 2, other).start()

            p_copy(n, buf, 4 + flow_len + r, other).start()

    def partner_done(n, buf):
        @pl.loop(0, 4)
        def _(j):
            p_copy(n, buf, j, shard_of(z, j, 1 - core)).wait_recv()

        @pl.loop(0, flow_len)
        def _(r):
            p_copy(n, buf, 4 + r, from_left(r, 1 - core)).wait_recv()
            p_copy(n, buf, 4 + flow_len + r, from_right(r, 1 - core)).wait_recv()

    def sends_done(n, buf):
        shard = shard_of(z, 0, core)

        @pl.loop(0, flow_len)
        def _(s):
            z_copy(n, buf, 0, s, shard).wait_send()
            z_copy(n, buf, 1, s, shard).wait_send()

        @pl.loop(0, 4 + 2 * flow_len)
        def _(q):
            p_copy(n, buf, q, shard).wait_send()

    def block_sum(buf, xs, b):
        total = None
        for pair in range(SLOTS // 2):
            rows = [buf[ls[xs, b, 2 * pair + i]] for i in range(2)]
            mats = [w[xs, b, 2 * pair + i] for i in range(2)]
            term = jnp.dot(
                jnp.concatenate(mats, axis=1), jnp.concatenate(rows, axis=0),
                preferred_element_type=jnp.float32,
            )
            total = term if total is None else total + term
        return total.astype(jnp.bfloat16)

    zeros = jnp.zeros((BL, BL), jnp.bfloat16)
    x0[nz * 2 * NX * BLK] = zeros
    x1[nz * 2 * NX * BLK] = zeros

    own_in.wait()
    send_own(0, x0, 0)
    for j in (1, 3, 2):
        deal(j).wait_recv()
        send_own(0, x0, j)
    cuts = (0, flow_len // 2 - 1, flow_len // 2 + 2, flow_len - 1, flow_len)
    for part in range(4):
        pass_on(0, x0, cuts[part], cuts[part + 1])
        if part < 3:
            w_serve(part)

    own_names.wait()
    for d in (1, 2, 3):
        names(d).wait_recv()
    to_smem = pltpu.make_async_copy(lv, ls, loc.at[1])
    to_smem.start()
    to_smem.wait()
    own_w.wait()
    partner_done(0, x0)
    for e in range(3):
        for u in range(2):
            w_across(e, u).wait_recv()

    @pl.loop(0, NX)
    def _(j):
        xs = wrap(x - j, NX)
        base = shard_of(z, j, core) * BLK

        @pl.loop(0, BLK)
        def _(b):
            x1[base + b] = block_sum(x0, xs, b)

        send_own(1, x1, j)

    pass_on(1, x1, 0, flow_len)
    partner_done(1, x1)

    def turn_x(way, n, xt, xc):
        ref = sx.at[xt, xc]
        return remote(ref, ref, g_s.at[0, way, n], g_r.at[0, way, n], x_dev(1 if way == 0 else 3))

    def turn_y(way, n, yt, xc):
        ref = st.at[yt, xc]
        return remote(ref, ref, g_s.at[1, way, n], g_r.at[1, way, n], up if way == 0 else down)

    @pl.loop(0, NX)
    def _(j):
        xc = wrap(x - j, NX)

        @pl.loop(0, BLK)
        def _(b):
            value = block_sum(x1, xc, b)
            sx[x, xc, b] = value
            st[y, xc, :, pl.ds(pl.multiple_of(b * BL, BL), BL)] = value.T

        for way in range(2):
            turn_x(way, j, x, xc).start()
            turn_y(way, j, y, xc).start()

    xl, xr, xo = wrap(x - 1, NX), wrap(x + 1, NX), wrap(x + 2, NX)
    yd, yu, yo = wrap(y - 1, NY), wrap(y + 1, NY), wrap(y + 2, NY)
    for j in range(NX):
        turn_x(0, j, xl, wrap(xl - j, NX)).wait_recv()
        turn_y(0, j, yd, wrap(x - j, NX)).wait_recv()
        if j < 2:
            turn_x(0, 4 + j, xl, wrap(xl - j, NX)).start()
            turn_y(0, 4 + j, yd, wrap(x - j, NX)).start()
        turn_x(1, j, xr, wrap(xr - j, NX)).wait_recv()
        turn_y(1, j, yu, wrap(x - j, NX)).wait_recv()
        if j >= 2:
            turn_x(1, 2 + j, xr, wrap(xr - j, NX)).start()
            turn_y(1, 2 + j, yu, wrap(x - j, NX)).start()

    def product(yts, xts):
        @pl.loop(0, NX)
        def _(xc):
            lhs = jnp.concatenate([st[yt, xc] for yt in yts], axis=0)
            rhs = jnp.concatenate(
                [sx[xt, xc].reshape(BLK * BL, BL) for xt in xts], axis=1
            )
            part = jnp.dot(lhs, rhs, preferred_element_type=jnp.float32)
            for i, yt in enumerate(yts):
                for k, xt in enumerate(xts):
                    cols = pl.ds(pl.multiple_of(xt * BL, BL), BL)
                    tile = part[i * BL:(i + 1) * BL, k * BL:(k + 1) * BL].reshape(2, 2, 32, BL)

                    @pl.when(xc == 0)
                    def _():
                        gram[yt, :, :, :, cols] = tile

                    @pl.when(xc > 0)
                    def _():
                        gram[yt, :, :, :, cols] += tile

    product([y, yd, yu], [x, xl])
    product([y, yd, yu], [xr])
    for j in range(2):
        turn_x(0, 4 + j, xo, wrap(xo - j, NX)).wait_recv()
        turn_y(0, 4 + j, yo, wrap(x - j, NX)).wait_recv()
        turn_x(1, 4 + j, xo, wrap(xo - 2 - j, NX)).wait_recv()
        turn_y(1, 4 + j, yo, wrap(x - 2 - j, NX)).wait_recv()
    product([y, yd, yu], [xo])
    product([yo], [x, xl])
    product([yo], [xr, xo])

    other = remote(gram.at[:, :, 1 - core], r1, a_s.at[0], a_r.at[0], partner)
    other.start()

    def write_out(xt):
        return pltpu.make_async_copy(sx.at[xt, x], columns(out, xt), loc.at[xt])

    for xt in range(NX):
        write_out(xt).start()

    def to_owner(n):
        return remote(r1.at[n // 2, n % 2], r3.at[z], c_s.at[n], c_r.at[z], (sink(n), y))

    other.wait_recv()
    for n in range(nz):
        r1[n // 2, n % 2] += gram[n // 2, n % 2, core]

        @pl.when(sink(n) != me)
        def _():
            to_owner(n).start()

    @pl.when(source(z) == me)
    def _():
        r3[z] = r1[z // 2, lax.rem(x, 2)]

    for zz in range(nz):
        @pl.when(source(zz) != me)
        def _():
            remote(r1.at[0, 0], r3.at[zz], c_s.at[0], c_r.at[zz], (source(zz), y)).wait_recv()

    total = r3[0]
    for zz in range(1, nz):
        total += r3[zz]
    cov[...] = total * scale

    for d in (1, 2, 3):
        deal(d).wait_send()
        names(d).wait_send()
        for u in range(2):
            w_across(d - 1, u).wait_send()
    for way in range(2):
        w_forward(way).wait_send()
        for u in range(2):
            w_first(way, u).wait_send()
        for n in range(6):
            turn_x(way, n, x, x).wait_send()
            turn_y(way, n, y, x).wait_send()
    sends_done(0, x0)
    sends_done(1, x1)
    other.wait_send()
    for n in range(nz):
        @pl.when(sink(n) != me)
        def _():
            to_owner(n).wait_send()
    for xt in range(NX):
        write_out(xt).wait()


def diffuse(expression, affinity, lists, nz):
    shards = nz * 2 * NX
    flow_len = 4 * (nz // 2) - 2
    dma = pltpu.SemaphoreType.DMA
    any_spec = pl.BlockSpec(memory_space=pl.ANY)
    return pl.pallas_call(
        functools.partial(diffuse_kernel, nz, 1.0 / (shards * BLK * BL)),
        out_shape=(
            jax.ShapeDtypeStruct(expression.shape, jnp.bfloat16),
            jax.ShapeDtypeStruct((32, NX * BL), jnp.float32),
        ),
        in_specs=[any_spec] * 3,
        out_specs=(any_spec, pl.BlockSpec(memory_space=pltpu.VMEM)),
        scratch_shapes=[
            pltpu.VMEM((shards * BLK + 1, BL, BL), jnp.bfloat16),
            pltpu.VMEM((shards * BLK + 1, BL, BL), jnp.bfloat16),
            pltpu.VMEM((NX, BLK, SLOTS, BL, BL), jnp.bfloat16),
            pltpu.VMEM((NX, BLK, BL), jnp.int32),
            pltpu.SMEM((NX, BLK, BL), jnp.int32),
            pltpu.VMEM((NX, NX, BLK, BL, BL), jnp.bfloat16),
            pltpu.VMEM((NY, NX, BL, BLK * BL), jnp.bfloat16),
            pltpu.VMEM((NY, 2, 2, 32, NX * BL), jnp.float32),
            pltpu.VMEM((NY, 2, 32, NX * BL), jnp.float32),
            pltpu.VMEM((nz, 32, NX * BL), jnp.float32),
            dma((4,)),
            dma((3,)), dma((3,)),
            dma((3,)), dma((3,)),
            dma((2, 2)), dma((2, 2)),
            dma((2,)), dma((2,)),
            dma((2, 3)), dma((2, 3)),
            dma((2, 2, flow_len)), dma((2, 2, flow_len)),
            dma((2, 4 + 2 * flow_len)), dma((2, 4 + 2 * flow_len)),
            dma((2, 2, 6)), dma((2, 2, 6)),
            dma((1,)), dma((1,)),
            dma((nz,)), dma((nz,)),
        ],
        compiler_params=pltpu.CompilerParams(
            collective_id=0, has_side_effects=True, vmem_limit_bytes=60 * 2**20
        ),
    )(expression, affinity, lists)


def body(nz, expression, affinity, near_blocks, far_blocks, far_count):
    shard_total = nz * 2 * NX
    live = jnp.arange(far_blocks.shape[1], dtype=jnp.int32)[None, :] < far_count[:, None]
    far = jnp.where(live, far_blocks, shard_total * BLK)
    lists = jnp.concatenate([near_blocks, far], axis=1)
    lists = jnp.pad(lists, ((0, 0), (0, BL - SLOTS)))
    blocks = expression.reshape(BLK, BL, expression.shape[1])
    current, covariance = diffuse(blocks, affinity, lists, nz)
    return (current.reshape(expression.shape), covariance)


def solution(mesh):
    nz = mesh.shape["cells"] // (2 * NX)
    return jax.shard_map(
        functools.partial(body, nz),
        mesh=mesh,
        in_specs=(
            P("cells", "genes"),
            P("cells", None, None, None),
            P("cells", None),
            P("cells", None),
            P("cells"),
        ),
        out_specs=(P("cells", "genes"), P("cells", "genes")),
        check_vma=False,
    )
```

```python
import functools

import jax
import jax.numpy as jnp
from jax import lax
from jax.experimental import pallas as pl
from jax.experimental.pallas import tpu as pltpu
from jax.sharding import PartitionSpec as P

MESH = pl.DeviceIdType.MESH
NX = 4
NY = 4
BL = 128
BLK = 8
SLOTS = 12
LOC = 4


def remote(src, dst, send, recv, device):
    return pltpu.make_async_remote_copy(
        src_ref=src, dst_ref=dst, send_sem=send, recv_sem=recv, device_id=device, device_id_type=MESH
    )


def diffuse_kernel(
    nz, scale, expr, aff, near, far, count, out, cov, x0, x1, w, lv, ls, sx, st, gram, r1, rz, r3,
    loc, xs_s, xs_r, li_s, li_r, wx_s, wx_r, wf_s, wf_r, wy_s, wy_r,
    z_s, z_r, p_s, p_r, g_s, g_r, a_s, a_r, c_s, c_r,
):
    flow_len = 4 * (nz // 2) - 2
    me = lax.axis_index("cells")
    y = lax.axis_index("genes")
    core = lax.rem(me, 2)
    x = lax.rem(me // 2, NX)
    z = me // (2 * NX)
    half = lax.rem(y, 2)

    def cell(zz, xx, kk):
        return (zz * NX + xx) * 2 + kk

    def wrap(v, n):
        return lax.rem(v + n, n)

    def x_dev(d):
        return (cell(z, wrap(x + d, NX), core), y)

    right = (cell(wrap(z + 1, nz), x, core), y)
    left = (cell(wrap(z - 1, nz), x, core), y)
    partner = (cell(z, x, 1 - core), y)
    up = (me, wrap(y + 1, NY))
    down = (me, wrap(y - 1, NY))

    def sink(n):
        return cell(2 * (n // 2) + x // 2, 2 * lax.rem(x, 2) + n % 2, core)

    def source(zz):
        return cell(zz, 2 * lax.rem(z, 2) + x // 2, core)

    barrier = pltpu.get_barrier_semaphore()
    peers = [x_dev(1), x_dev(2), x_dev(3), right, left, partner, up, down]
    for peer in peers:
        pl.semaphore_signal(barrier, inc=1, device_id=peer, device_id_type=MESH)
    for zz in range(nz):
        @pl.when(source(zz) != me)
        def _():
            pl.semaphore_signal(barrier, inc=1, device_id=(source(zz), y), device_id_type=MESH)
    pl.semaphore_wait(barrier, len(peers) + nz - jnp.where(source(z) == me, 1, 0))

    def piece(buf, shard):
        return buf.at[pl.ds(shard * BLK, BLK)]

    def columns(ref, xx):
        return ref.at[:, :, pl.ds(pl.multiple_of(xx * BL, BL), BL)]

    def deal(d):
        return remote(
            columns(expr, wrap(x + d, NX)), piece(x0, me), xs_s.at[d - 1], xs_r.at[d - 1], x_dev(d)
        )

    own_in = pltpu.make_async_copy(columns(expr, x), piece(x0, me), loc.at[0])
    own_in.start()
    for d in (1, 3, 2):
        deal(d).start()

    slot = lax.broadcasted_iota(jnp.int32, (1, BLK), 1)
    for b in range(BLK):
        lv[x, b:b + 1, 0:BLK] = jnp.where(slot < count[b], far[b:b + 1, :], nz * 2 * NX * BLK)
    lv[x, BLK:BLK + LOC, 0:BLK] = near[...]

    def names(d):
        return remote(lv.at[x], lv.at[x], li_s.at[d - 1], li_r.at[d - 1], x_dev(d))

    for d in (1, 2, 3):
        names(d).start()

    own_w = pltpu.make_async_copy(aff, w.at[x], loc.at[2])

    def wsub(xx, hh, i):
        return w.at[xx, 4 * hh + i]

    def w_first(way, n):
        i = n if way == 0 else 3 - n
        return remote(
            aff.at[4 * half + i], wsub(x, half, i), wx_s.at[way, n], wx_r.at[way, n],
            x_dev(1 if way == 0 else 3),
        )

    def w_forward(way, n):
        i = n if way == 0 else 3 - n
        ref = wsub(wrap(x - 1, NX) if way == 0 else wrap(x + 1, NX), half, i)
        return remote(ref, ref, wf_s.at[way, n], wf_r.at[way, n], x_dev(1 if way == 0 else 3))

    def w_across(e, i):
        ref = wsub(wrap(x + (3, 1, 2)[e], NX), half, i)
        return remote(ref, ref, wy_s.at[e, i], wy_r.at[e, i], up if i < 2 else down)

    for n in range(2):
        w_first(0, n).start()
        w_first(1, n).start()
    own_w.start()

    def w_serve(n):
        for way in range(2):
            i = n % 4 if way == 0 else 3 - n % 4
            if n < 4:
                w_first(way, n).wait_recv()
                if n < 2:
                    w_forward(way, n).start()
                w_across(way, i).start()
                if n < 2:
                    w_first(way, n + 2).start()
            else:
                w_forward(way, n - 4).wait_recv()
                w_across(2, i).start()

    def shard_of(zz, j, kk):
        return cell(wrap(zz, nz), wrap(x - j, NX), kk)

    def z_copy(n, buf, way, s, shard):
        return remote(
            piece(buf, shard), piece(buf, shard), z_s.at[n, way, s], z_r.at[n, way, s],
            right if way == 0 else left,
        )

    def p_copy(n, buf, q, shard):
        return remote(piece(buf, shard), piece(buf, shard), p_s.at[n, q], p_r.at[n, q], partner)

    def from_left(r, kk):
        return shard_of(z - 1 - r // 4, lax.rem(r, 4), kk)

    def from_right(r, kk):
        j = lax.rem(r, 4) + jnp.where(r < flow_len - 2, 0, 2)
        return shard_of(z + 1 + r // 4, j, kk)

    def send_own(n, buf, j):
        shard = shard_of(z, j, core)
        z_copy(n, buf, 0, j, shard).start()
        z_copy(n, buf, 1, j, shard).start()
        p_copy(n, buf, j, shard).start()

    def pass_on(n, buf, first, last):
        @pl.loop(first, last)
        def _(r):
            shard = from_left(r, core)
            z_copy(n, buf, 0, r, shard).wait_recv()

            @pl.when(r + 4 < flow_len)
            def _():
                z_copy(n, buf, 0, r + 4, shard).start()

            p_copy(n, buf, 4 + r, shard).start()
            other = from_right(r, core)
            z_copy(n, buf, 1, r, other).wait_recv()

            @pl.when(r < flow_len - 6)
            def _():
                z_copy(n, buf, 1, r + 4, other).start()

            @pl.when((r >= flow_len - 4) & (r < flow_len - 2))
            def _():
                z_copy(n, buf, 1, r + 2, other).start()

            p_copy(n, buf, 4 + flow_len + r, other).start()

    def partner_done(n, buf):
        @pl.loop(0, 4)
        def _(j):
            p_copy(n, buf, j, shard_of(z, j, 1 - core)).wait_recv()

        @pl.loop(0, flow_len)
        def _(r):
            p_copy(n, buf, 4 + r, from_left(r, 1 - core)).wait_recv()
            p_copy(n, buf, 4 + flow_len + r, from_right(r, 1 - core)).wait_recv()

    def sends_done(n, buf):
        shard = shard_of(z, 0, core)

        @pl.loop(0, flow_len)
        def _(s):
            z_copy(n, buf, 0, s, shard).wait_send()
            z_copy(n, buf, 1, s, shard).wait_send()

        @pl.loop(0, 4 + 2 * flow_len)
        def _(q):
            p_copy(n, buf, q, shard).wait_send()

    def name(xs, b, slot):
        return ls[xs, BLK + slot, b] if slot < LOC else ls[xs, b, slot - LOC]

    def block_sum(buf, xs, b):
        total = None
        for pair in range(SLOTS // 2):
            rows = [buf[name(xs, b, 2 * pair + i)] for i in range(2)]
            mats = [w[xs, b, 2 * pair + i] for i in range(2)]
            term = jnp.dot(
                jnp.concatenate(mats, axis=1), jnp.concatenate(rows, axis=0),
                preferred_element_type=jnp.float32,
            )
            total = term if total is None else total + term
        return total.astype(jnp.bfloat16)

    zeros = jnp.zeros((BL, BL), jnp.bfloat16)
    x0[nz * 2 * NX * BLK] = zeros
    x1[nz * 2 * NX * BLK] = zeros

    own_in.wait()
    send_own(0, x0, 0)
    for j in (1, 3, 2):
        deal(j).wait_recv()
        send_own(0, x0, j)
    cuts = (0, 3, 4, 6, 7, 8, 9, flow_len)
    for part in range(7):
        pass_on(0, x0, cuts[part], cuts[part + 1])
        if part < 6:
            w_serve(part)

    for d in (1, 2, 3):
        names(d).wait_recv()
    to_smem = pltpu.make_async_copy(lv, ls, loc.at[1])
    to_smem.start()
    to_smem.wait()
    own_w.wait()
    partner_done(0, x0)
    for e in range(3):
        for i in range(4):
            w_across(e, i).wait_recv()

    @pl.loop(0, NX)
    def _(j):
        xs = wrap(x - j, NX)
        base = shard_of(z, j, core) * BLK

        @pl.loop(0, BLK)
        def _(b):
            x1[base + b] = block_sum(x0, xs, b)

        send_own(1, x1, j)

    pass_on(1, x1, 0, flow_len)
    partner_done(1, x1)

    def turn_x(way, n, xt, xc):
        ref = sx.at[xt, xc]
        return remote(ref, ref, g_s.at[0, way, n], g_r.at[0, way, n], x_dev(1 if way == 0 else 3))

    def turn_y(way, n, yt, xc):
        ref = st.at[yt, xc]
        return remote(ref, ref, g_s.at[1, way, n], g_r.at[1, way, n], up if way == 0 else down)

    @pl.loop(0, NX)
    def _(j):
        xc = wrap(x - j, NX)

        @pl.loop(0, BLK)
        def _(b):
            value = block_sum(x1, xc, b)
            sx[x, xc, b] = value
            st[y, xc, :, pl.ds(pl.multiple_of(b * BL, BL), BL)] = value.T

        for way in range(2):
            turn_x(way, j, x, xc).start()
            turn_y(way, j, y, xc).start()

    xl, xr, xo = wrap(x - 1, NX), wrap(x + 1, NX), wrap(x + 2, NX)
    yd, yu, yo = wrap(y - 1, NY), wrap(y + 1, NY), wrap(y + 2, NY)
    for j in range(NX):
        turn_x(0, j, xl, wrap(xl - j, NX)).wait_recv()
        turn_y(0, j, yd, wrap(x - j, NX)).wait_recv()
        if j < 2:
            turn_x(0, 4 + j, xl, wrap(xl - j, NX)).start()
            turn_y(0, 4 + j, yd, wrap(x - j, NX)).start()
        turn_x(1, j, xr, wrap(xr - j, NX)).wait_recv()
        turn_y(1, j, yu, wrap(x - j, NX)).wait_recv()
        if j >= 2:
            turn_x(1, 2 + j, xr, wrap(xr - j, NX)).start()
            turn_y(1, 2 + j, yu, wrap(x - j, NX)).start()

    def product(yts, xts):
        @pl.loop(0, NX)
        def _(xc):
            lhs = jnp.concatenate([st[yt, xc] for yt in yts], axis=0)
            rhs = jnp.concatenate(
                [sx[xt, xc].reshape(BLK * BL, BL) for xt in xts], axis=1
            )
            part = jnp.dot(lhs, rhs, preferred_element_type=jnp.float32)
            for i, yt in enumerate(yts):
                for k, xt in enumerate(xts):
                    cols = pl.ds(pl.multiple_of(xt * BL, BL), BL)
                    tile = part[i * BL:(i + 1) * BL, k * BL:(k + 1) * BL].reshape(2, 2, 32, BL)

                    @pl.when(xc == 0)
                    def _():
                        gram[yt, :, :, :, cols] = tile

                    @pl.when(xc > 0)
                    def _():
                        gram[yt, :, :, :, cols] += tile

    product([y, yd, yu], [x, xl])
    product([y, yd, yu], [xr])
    for j in range(2):
        turn_x(0, 4 + j, xo, wrap(xo - j, NX)).wait_recv()
        turn_y(0, 4 + j, yo, wrap(x - j, NX)).wait_recv()
        turn_x(1, 4 + j, xo, wrap(xo - 2 - j, NX)).wait_recv()
        turn_y(1, 4 + j, yo, wrap(x - 2 - j, NX)).wait_recv()
    product([y, yd, yu], [xo])
    product([yo], [x, xl])
    product([yo], [xr, xo])

    other = remote(gram.at[:, :, 1 - core], r1, a_s.at[0], a_r.at[0], partner)
    other.start()

    def write_out(xt):
        return pltpu.make_async_copy(sx.at[xt, x], columns(out, xt), loc.at[xt])

    for xt in range(NX):
        write_out(xt).start()

    def to_owner(n):
        return remote(rz.at[n // 2, n % 2], r3.at[z], c_s.at[n], c_r.at[z], (sink(n), y))

    other.wait_recv()
    for n in range(nz):
        both = r1[n // 2, n % 2] + gram[n // 2, n % 2, core]
        rz[n // 2, n % 2] = both.astype(jnp.bfloat16)

        @pl.when(sink(n) != me)
        def _():
            to_owner(n).start()

    @pl.when(source(z) == me)
    def _():
        r3[z] = rz[z // 2, lax.rem(x, 2)]

    for zz in range(nz):
        @pl.when(source(zz) != me)
        def _():
            remote(rz.at[0, 0], r3.at[zz], c_s.at[0], c_r.at[zz], (source(zz), y)).wait_recv()

    total = r3[0].astype(jnp.float32)
    for zz in range(1, nz):
        total += r3[zz].astype(jnp.float32)
    cov[...] = total * scale

    for d in (1, 2, 3):
        deal(d).wait_send()
        names(d).wait_send()
        for i in range(4):
            w_across(d - 1, i).wait_send()
    for way in range(2):
        for n in range(2):
            w_forward(way, n).wait_send()
        for n in range(4):
            w_first(way, n).wait_send()
        for n in range(6):
            turn_x(way, n, x, x).wait_send()
            turn_y(way, n, y, x).wait_send()
    sends_done(0, x0)
    sends_done(1, x1)
    other.wait_send()
    for n in range(nz):
        @pl.when(sink(n) != me)
        def _():
            to_owner(n).wait_send()
    for xt in range(NX):
        write_out(xt).wait()


def diffuse(expression, affinity, near, far, count, nz):
    shards = nz * 2 * NX
    flow_len = 4 * (nz // 2) - 2
    dma = pltpu.SemaphoreType.DMA
    any_spec = pl.BlockSpec(memory_space=pl.ANY)
    return pl.pallas_call(
        functools.partial(diffuse_kernel, nz, 1.0 / (shards * BLK * BL)),
        out_shape=(
            jax.ShapeDtypeStruct(expression.shape, jnp.bfloat16),
            jax.ShapeDtypeStruct((32, NX * BL), jnp.float32),
        ),
        in_specs=[
            any_spec,
            any_spec,
            pl.BlockSpec(memory_space=pltpu.VMEM),
            pl.BlockSpec(memory_space=pltpu.VMEM),
            pl.BlockSpec(memory_space=pltpu.SMEM),
        ],
        out_specs=(any_spec, pl.BlockSpec(memory_space=pltpu.VMEM)),
        scratch_shapes=[
            pltpu.VMEM((shards * BLK + 1, BL, BL), jnp.bfloat16),
            pltpu.VMEM((shards * BLK + 1, BL, BL), jnp.bfloat16),
            pltpu.VMEM((NX, BLK, SLOTS, BL, BL), jnp.bfloat16),
            pltpu.VMEM((NX, 2 * BLK, BL), jnp.int32),
            pltpu.SMEM((NX, 2 * BLK, BL), jnp.int32),
            pltpu.VMEM((NX, NX, BLK, BL, BL), jnp.bfloat16),
            pltpu.VMEM((NY, NX, BL, BLK * BL), jnp.bfloat16),
            pltpu.VMEM((NY, 2, 2, 32, NX * BL), jnp.float32),
            pltpu.VMEM((NY, 2, 32, NX * BL), jnp.float32),
            pltpu.VMEM((NY, 2, 32, NX * BL), jnp.bfloat16),
            pltpu.VMEM((nz, 32, NX * BL), jnp.bfloat16),
            dma((4,)),
            dma((3,)), dma((3,)),
            dma((3,)), dma((3,)),
            dma((2, 4)), dma((2, 4)),
            dma((2, 2)), dma((2, 2)),
            dma((3, 4)), dma((3, 4)),
            dma((2, 2, flow_len)), dma((2, 2, flow_len)),
            dma((2, 4 + 2 * flow_len)), dma((2, 4 + 2 * flow_len)),
            dma((2, 2, 6)), dma((2, 2, 6)),
            dma((1,)), dma((1,)),
            dma((nz,)), dma((nz,)),
        ],
        compiler_params=pltpu.CompilerParams(
            collective_id=0, has_side_effects=True, vmem_limit_bytes=60 * 2**20
        ),
    )(expression, affinity, near, far, count)


def body(nz, expression, affinity, near_blocks, far_blocks, far_count):
    blocks = expression.reshape(BLK, BL, expression.shape[1])
    current, covariance = diffuse(
        blocks, affinity, near_blocks.T, far_blocks, far_count, nz
    )
    return (current.reshape(expression.shape), covariance)


def solution(mesh):
    nz = mesh.shape["cells"] // (2 * NX)
    return jax.shard_map(
        functools.partial(body, nz),
        mesh=mesh,
        in_specs=(
            P("cells", "genes"),
            P("cells", None, None, None),
            P("cells", None),
            P("cells", None),
            P("cells"),
        ),
        out_specs=(P("cells", "genes"), P("cells", "genes")),
        check_vma=False,
    )
```

```python
import functools

import jax
import jax.numpy as jnp
from jax import lax
from jax.experimental import pallas as pl
from jax.experimental.pallas import tpu as pltpu
from jax.sharding import PartitionSpec as P

MESH = pl.DeviceIdType.MESH
NX = 4
NY = 4
BL = 128
BLK = 8
SLOTS = 12
LOC = 4


def remote(src, dst, send, recv, device):
    return pltpu.make_async_remote_copy(
        src_ref=src, dst_ref=dst, send_sem=send, recv_sem=recv, device_id=device, device_id_type=MESH
    )


def diffuse_kernel(
    nz, scale, expr, aff, near, far, count, out, cov, x0, x1, w, lv, ls, sx, st, gram, r1, rz, r3,
    loc, xs_s, xs_r, li_s, li_r, wx_s, wx_r, wf_s, wf_r, wy_s, wy_r,
    z_s, z_r, p_s, p_r, g_s, g_r, a_s, a_r, c_s, c_r,
):
    flow_len = 4 * (nz // 2) - 2
    me = lax.axis_index("cells")
    y = lax.axis_index("genes")
    core = lax.rem(me, 2)
    x = lax.rem(me // 2, NX)
    z = me // (2 * NX)
    half = lax.rem(y, 2)

    def cell(zz, xx, kk):
        return (zz * NX + xx) * 2 + kk

    def wrap(v, n):
        return lax.rem(v + n, n)

    def x_dev(d):
        return (cell(z, wrap(x + d, NX), core), y)

    right = (cell(wrap(z + 1, nz), x, core), y)
    left = (cell(wrap(z - 1, nz), x, core), y)
    partner = (cell(z, x, 1 - core), y)
    up = (me, wrap(y + 1, NY))
    down = (me, wrap(y - 1, NY))

    def sink(n):
        return cell(2 * (n // 2) + x // 2, 2 * lax.rem(x, 2) + n % 2, core)

    def source(zz):
        return cell(zz, 2 * lax.rem(z, 2) + x // 2, core)

    barrier = pltpu.get_barrier_semaphore()
    peers = [x_dev(1), x_dev(2), x_dev(3), right, left, partner, up, down]
    for peer in peers:
        pl.semaphore_signal(barrier, inc=1, device_id=peer, device_id_type=MESH)
    for zz in range(nz):
        @pl.when(source(zz) != me)
        def _():
            pl.semaphore_signal(barrier, inc=1, device_id=(source(zz), y), device_id_type=MESH)
    pl.semaphore_wait(barrier, len(peers) + nz - jnp.where(source(z) == me, 1, 0))

    def piece(buf, shard):
        return buf.at[pl.ds(shard * BLK, BLK)]

    def columns(ref, xx):
        return ref.at[:, :, pl.ds(pl.multiple_of(xx * BL, BL), BL)]

    def deal(d):
        return remote(
            columns(expr, wrap(x + d, NX)), piece(x0, me), xs_s.at[d - 1], xs_r.at[d - 1], x_dev(d)
        )

    own_in = pltpu.make_async_copy(columns(expr, x), piece(x0, me), loc.at[0])
    own_in.start()
    for d in (1, 3, 2):
        deal(d).start()

    slot = lax.broadcasted_iota(jnp.int32, (1, BLK), 1)
    for b in range(BLK):
        lv[x, b:b + 1, 0:BLK] = jnp.where(slot < count[b], far[b:b + 1, :], nz * 2 * NX * BLK)
    lv[x, BLK:BLK + LOC, 0:BLK] = near[...]

    def names(d):
        return remote(lv.at[x], lv.at[x], li_s.at[d - 1], li_r.at[d - 1], x_dev(d))

    for d in (1, 2, 3):
        names(d).start()

    own_w = pltpu.make_async_copy(aff, w.at[x], loc.at[2])

    def wsub(xx, hh, i):
        return w.at[xx, 4 * hh + i]

    def w_first(way, n):
        i = n if way == 0 else 3 - n
        return remote(
            aff.at[4 * half + i], wsub(x, half, i), wx_s.at[way, n], wx_r.at[way, n],
            x_dev(1 if way == 0 else 3),
        )

    def w_forward(way, n):
        i = n if way == 0 else 3 - n
        ref = wsub(wrap(x - 1, NX) if way == 0 else wrap(x + 1, NX), half, i)
        return remote(ref, ref, wf_s.at[way, n], wf_r.at[way, n], x_dev(1 if way == 0 else 3))

    def w_across(e, i):
        ref = wsub(wrap(x + (3, 1, 2)[e], NX), half, i)
        return remote(ref, ref, wy_s.at[e, i], wy_r.at[e, i], up if i < 2 else down)

    for n in range(4):
        w_first(0, n).start()
        w_first(1, n).start()
    own_w.start()

    def w_serve(n):
        for way in range(2):
            i = n % 4 if way == 0 else 3 - n % 4
            if n < 4:
                w_first(way, n).wait_recv()
                if n < 2:
                    w_forward(way, n).start()
                w_across(way, i).start()
            else:
                w_forward(way, n - 4).wait_recv()
                w_across(2, i).start()

    def shard_of(zz, j, kk):
        return cell(wrap(zz, nz), wrap(x - j, NX), kk)

    def z_copy(n, buf, way, s, shard):
        return remote(
            piece(buf, shard), piece(buf, shard), z_s.at[n, way, s], z_r.at[n, way, s],
            right if way == 0 else left,
        )

    def p_copy(n, buf, q, shard):
        return remote(piece(buf, shard), piece(buf, shard), p_s.at[n, q], p_r.at[n, q], partner)

    def from_left(r, kk):
        return shard_of(z - 1 - r // 4, lax.rem(r, 4), kk)

    def from_right(r, kk):
        j = lax.rem(r, 4) + jnp.where(r < flow_len - 2, 0, 2)
        return shard_of(z + 1 + r // 4, j, kk)

    def send_own(n, buf, j):
        shard = shard_of(z, j, core)
        z_copy(n, buf, 0, j, shard).start()
        z_copy(n, buf, 1, j, shard).start()
        p_copy(n, buf, j, shard).start()

    def pass_on(n, buf, first, last):
        @pl.loop(first, last)
        def _(r):
            shard = from_left(r, core)
            z_copy(n, buf, 0, r, shard).wait_recv()

            @pl.when(r + 4 < flow_len)
            def _():
                z_copy(n, buf, 0, r + 4, shard).start()

            p_copy(n, buf, 4 + r, shard).start()
            other = from_right(r, core)
            z_copy(n, buf, 1, r, other).wait_recv()

            @pl.when(r < flow_len - 6)
            def _():
                z_copy(n, buf, 1, r + 4, other).start()

            @pl.when((r >= flow_len - 4) & (r < flow_len - 2))
            def _():
                z_copy(n, buf, 1, r + 2, other).start()

            p_copy(n, buf, 4 + flow_len + r, other).start()

    def partner_own(n, buf):
        @pl.loop(0, 4)
        def _(j):
            p_copy(n, buf, j, shard_of(z, j, 1 - core)).wait_recv()

    def partner_done(n, buf, first, last):
        @pl.loop(first, last)
        def _(r):
            p_copy(n, buf, 4 + r, from_left(r, 1 - core)).wait_recv()
            p_copy(n, buf, 4 + flow_len + r, from_right(r, 1 - core)).wait_recv()

    def sends_done(n, buf):
        shard = shard_of(z, 0, core)

        @pl.loop(0, flow_len)
        def _(s):
            z_copy(n, buf, 0, s, shard).wait_send()
            z_copy(n, buf, 1, s, shard).wait_send()

        @pl.loop(0, 4 + 2 * flow_len)
        def _(q):
            p_copy(n, buf, q, shard).wait_send()

    def name(xs, b, slot):
        return ls[xs, BLK + slot, b] if slot < LOC else ls[xs, b, slot - LOC]

    def block_sum(buf, xs, b):
        total = None
        for pair in range(SLOTS // 2):
            rows = [buf[name(xs, b, 2 * pair + i)] for i in range(2)]
            mats = [w[xs, b, 2 * pair + i] for i in range(2)]
            term = jnp.dot(
                jnp.concatenate(mats, axis=1), jnp.concatenate(rows, axis=0),
                preferred_element_type=jnp.float32,
            )
            total = term if total is None else total + term
        return total.astype(jnp.bfloat16)

    zeros = jnp.zeros((BL, BL), jnp.bfloat16)
    x0[nz * 2 * NX * BLK] = zeros
    x1[nz * 2 * NX * BLK] = zeros

    own_in.wait()
    send_own(0, x0, 0)
    for j in (1, 3, 2):
        deal(j).wait_recv()
        send_own(0, x0, j)
    cuts = (0, 4, 6, 8, 9, 11, 12)
    for part in range(6):
        pass_on(0, x0, cuts[part], cuts[part + 1])
        w_serve(part)
    for d in (1, 2, 3):
        names(d).wait_recv()
    to_smem = pltpu.make_async_copy(lv, ls, loc.at[1])
    to_smem.start()
    partner_own(0, x0)
    partner_done(0, x0, 0, 9)
    to_smem.wait()
    own_w.wait()
    pass_on(0, x0, 12, flow_len)
    for e in range(3):
        for i in range(4):
            w_across(e, i).wait_recv()
    partner_done(0, x0, 9, flow_len)

    @pl.loop(0, NX)
    def _(j):
        xs = wrap(x - j, NX)
        base = shard_of(z, j, core) * BLK

        @pl.loop(0, BLK)
        def _(b):
            x1[base + b] = block_sum(x0, xs, b)

        send_own(1, x1, j)

    pass_on(1, x1, 0, 8)
    for d in (1, 2, 3):
        deal(d).wait_send()
        names(d).wait_send()
        for i in range(4):
            w_across(d - 1, i).wait_send()
    for way in range(2):
        for n in range(2):
            w_forward(way, n).wait_send()
        for n in range(4):
            w_first(way, n).wait_send()
    sends_done(0, x0)
    pass_on(1, x1, 8, 12)
    partner_own(1, x1)
    partner_done(1, x1, 0, 9)
    pass_on(1, x1, 12, flow_len)
    partner_done(1, x1, 9, flow_len)

    def turn_x(way, n, xt, xc):
        ref = sx.at[xt, xc]
        return remote(ref, ref, g_s.at[0, way, n], g_r.at[0, way, n], x_dev(1 if way == 0 else 3))

    def turn_y(way, n, yt, xc):
        ref = st.at[yt, xc]
        return remote(ref, ref, g_s.at[1, way, n], g_r.at[1, way, n], up if way == 0 else down)

    @pl.loop(0, NX)
    def _(j):
        xc = wrap(x - j, NX)

        @pl.loop(0, BLK)
        def _(b):
            value = block_sum(x1, xc, b)
            sx[x, xc, b] = value
            st[y, xc, :, pl.ds(pl.multiple_of(b * BL, BL), BL)] = value.T

        for way in range(2):
            turn_x(way, j, x, xc).start()
            turn_y(way, j, y, xc).start()

    xl, xr, xo = wrap(x - 1, NX), wrap(x + 1, NX), wrap(x + 2, NX)
    yd, yu, yo = wrap(y - 1, NY), wrap(y + 1, NY), wrap(y + 2, NY)
    for j in range(NX):
        turn_x(0, j, xl, wrap(xl - j, NX)).wait_recv()
        turn_y(0, j, yd, wrap(x - j, NX)).wait_recv()
        if j < 2:
            turn_x(0, 4 + j, xl, wrap(xl - j, NX)).start()
            turn_y(0, 4 + j, yd, wrap(x - j, NX)).start()
        turn_x(1, j, xr, wrap(xr - j, NX)).wait_recv()
        turn_y(1, j, yu, wrap(x - j, NX)).wait_recv()
        if j >= 2:
            turn_x(1, 2 + j, xr, wrap(xr - j, NX)).start()
            turn_y(1, 2 + j, yu, wrap(x - j, NX)).start()

    def product(yts, xts):
        @pl.loop(0, NX)
        def _(xc):
            lhs = jnp.concatenate([st[yt, xc] for yt in yts], axis=0)
            rhs = jnp.concatenate(
                [sx[xt, xc].reshape(BLK * BL, BL) for xt in xts], axis=1
            )
            part = jnp.dot(lhs, rhs, preferred_element_type=jnp.float32)
            for i, yt in enumerate(yts):
                for k, xt in enumerate(xts):
                    cols = pl.ds(pl.multiple_of(xt * BL, BL), BL)
                    tile = part[i * BL:(i + 1) * BL, k * BL:(k + 1) * BL].reshape(2, 2, 32, BL)

                    @pl.when(xc == 0)
                    def _():
                        gram[yt, :, :, :, cols] = tile

                    @pl.when(xc > 0)
                    def _():
                        gram[yt, :, :, :, cols] += tile

    product([y, yd, yu], [x, xl])
    product([y, yd, yu], [xr])
    sends_done(1, x1)
    for j in range(2):
        turn_x(0, 4 + j, xo, wrap(xo - j, NX)).wait_recv()
        turn_y(0, 4 + j, yo, wrap(x - j, NX)).wait_recv()
        turn_x(1, 4 + j, xo, wrap(xo - 2 - j, NX)).wait_recv()
        turn_y(1, 4 + j, yo, wrap(x - 2 - j, NX)).wait_recv()
    product([y, yd, yu], [xo])
    product([yo], [x, xl])
    product([yo], [xr, xo])

    other = remote(gram.at[:, :, 1 - core], r1, a_s.at[0], a_r.at[0], partner)
    other.start()

    def write_out(xt):
        return pltpu.make_async_copy(sx.at[xt, x], columns(out, xt), loc.at[xt])

    for xt in range(NX):
        write_out(xt).start()

    def to_owner(n):
        return remote(rz.at[n // 2, n % 2], r3.at[z], c_s.at[n], c_r.at[z], (sink(n), y))

    other.wait_recv()
    for n in range(nz):
        both = r1[n // 2, n % 2] + gram[n // 2, n % 2, core]
        rz[n // 2, n % 2] = both.astype(jnp.bfloat16)

        @pl.when(sink(n) != me)
        def _():
            to_owner(n).start()

    for way in range(2):
        for n in range(6):
            turn_x(way, n, x, x).wait_send()
            turn_y(way, n, y, x).wait_send()
    for xt in range(NX):
        write_out(xt).wait()
    other.wait_send()

    @pl.when(source(z) == me)
    def _():
        r3[z] = rz[z // 2, lax.rem(x, 2)]

    for zz in range(nz):
        @pl.when(source(zz) != me)
        def _():
            remote(rz.at[0, 0], r3.at[zz], c_s.at[0], c_r.at[zz], (source(zz), y)).wait_recv()

    total = r3[0].astype(jnp.float32)
    for zz in range(1, nz):
        total += r3[zz].astype(jnp.float32)
    cov[...] = total * scale
    for n in range(nz):
        @pl.when(sink(n) != me)
        def _():
            to_owner(n).wait_send()


def diffuse(expression, affinity, near, far, count, nz):
    shards = nz * 2 * NX
    flow_len = 4 * (nz // 2) - 2
    dma = pltpu.SemaphoreType.DMA
    any_spec = pl.BlockSpec(memory_space=pl.ANY)
    return pl.pallas_call(
        functools.partial(diffuse_kernel, nz, 1.0 / (shards * BLK * BL)),
        out_shape=(
            jax.ShapeDtypeStruct(expression.shape, jnp.bfloat16),
            jax.ShapeDtypeStruct((32, NX * BL), jnp.float32),
        ),
        in_specs=[
            any_spec,
            any_spec,
            pl.BlockSpec(memory_space=pltpu.VMEM),
            pl.BlockSpec(memory_space=pltpu.VMEM),
            pl.BlockSpec(memory_space=pltpu.SMEM),
        ],
        out_specs=(any_spec, pl.BlockSpec(memory_space=pltpu.VMEM)),
        scratch_shapes=[
            pltpu.VMEM((shards * BLK + 1, BL, BL), jnp.bfloat16),
            pltpu.VMEM((shards * BLK + 1, BL, BL), jnp.bfloat16),
            pltpu.VMEM((NX, BLK, SLOTS, BL, BL), jnp.bfloat16),
            pltpu.VMEM((NX, 2 * BLK, BL), jnp.int32),
            pltpu.SMEM((NX, 2 * BLK, BL), jnp.int32),
            pltpu.VMEM((NX, NX, BLK, BL, BL), jnp.bfloat16),
            pltpu.VMEM((NY, NX, BL, BLK * BL), jnp.bfloat16),
            pltpu.VMEM((NY, 2, 2, 32, NX * BL), jnp.float32),
            pltpu.VMEM((NY, 2, 32, NX * BL), jnp.float32),
            pltpu.VMEM((NY, 2, 32, NX * BL), jnp.bfloat16),
            pltpu.VMEM((nz, 32, NX * BL), jnp.bfloat16),
            dma((4,)),
            dma((3,)), dma((3,)),
            dma((3,)), dma((3,)),
            dma((2, 4)), dma((2, 4)),
            dma((2, 2)), dma((2, 2)),
            dma((3, 4)), dma((3, 4)),
            dma((2, 2, flow_len)), dma((2, 2, flow_len)),
            dma((2, 4 + 2 * flow_len)), dma((2, 4 + 2 * flow_len)),
            dma((2, 2, 6)), dma((2, 2, 6)),
            dma((1,)), dma((1,)),
            dma((nz,)), dma((nz,)),
        ],
        compiler_params=pltpu.CompilerParams(
            collective_id=0, has_side_effects=True, vmem_limit_bytes=60 * 2**20
        ),
    )(expression, affinity, near, far, count)


def body(nz, expression, affinity, near_blocks, far_blocks, far_count):
    blocks = expression.reshape(BLK, BL, expression.shape[1])
    current, covariance = diffuse(
        blocks, affinity, near_blocks.T, far_blocks, far_count, nz
    )
    return (current.reshape(expression.shape), covariance)


def solution(mesh):
    nz = mesh.shape["cells"] // (2 * NX)
    return jax.shard_map(
        functools.partial(body, nz),
        mesh=mesh,
        in_specs=(
            P("cells", "genes"),
            P("cells", None, None, None),
            P("cells", None),
            P("cells", None),
            P("cells"),
        ),
        out_specs=(P("cells", "genes"), P("cells", "genes")),
        check_vma=False,
    )
```

```python
import functools

import jax
import jax.numpy as jnp
from jax import lax
from jax.experimental import pallas as pl
from jax.experimental.pallas import tpu as pltpu
from jax.sharding import PartitionSpec as P

MESH = pl.DeviceIdType.MESH
NX = 4
NY = 4
BL = 128
BLK = 8
SLOTS = 12
LOC = 4
HALF = BLK // 2


def remote(src, dst, send, recv, device):
    return pltpu.make_async_remote_copy(
        src_ref=src, dst_ref=dst, send_sem=send, recv_sem=recv, device_id=device, device_id_type=MESH
    )


def diffuse_kernel(
    nz, scale, expr, aff, near, far, count, out, cov, x0, x1a, x1b, w, lv, ls,
    lanes, sx, st, whole, gram, r1, rz, r3,
    loc, xs_s, xs_r, li_s, li_r, wx_s, wx_r, wf_s, wf_r, wy_s, wy_r,
    z_s, z_r, p_s, p_r, g_s, g_r, a_s, a_r, c_s, c_r,
):
    flow_len = 4 * (nz // 2) - 2
    me = lax.axis_index("cells")
    y = lax.axis_index("genes")
    core = lax.rem(me, 2)
    x = lax.rem(me // 2, NX)
    z = me // (2 * NX)
    half = lax.rem(y, 2)

    def cell(zz, xx, kk):
        return (zz * NX + xx) * 2 + kk

    def wrap(v, n):
        return lax.rem(v + n, n)

    def x_dev(d):
        return (cell(z, wrap(x + d, NX), core), y)

    right = (cell(wrap(z + 1, nz), x, core), y)
    left = (cell(wrap(z - 1, nz), x, core), y)
    partner = (cell(z, x, 1 - core), y)
    up = (me, wrap(y + 1, NY))
    down = (me, wrap(y - 1, NY))

    def sink(n):
        return cell(2 * (n // 2) + x // 2, 2 * lax.rem(x, 2) + n % 2, core)

    def source(zz):
        return cell(zz, 2 * lax.rem(z, 2) + x // 2, core)

    barrier = pltpu.get_barrier_semaphore()
    peers = [x_dev(1), x_dev(2), x_dev(3), right, left, partner, up, down]
    for peer in peers:
        pl.semaphore_signal(barrier, inc=1, device_id=peer, device_id_type=MESH)
    for zz in range(nz):
        @pl.when(source(zz) != me)
        def _():
            pl.semaphore_signal(barrier, inc=1, device_id=(source(zz), y), device_id_type=MESH)
    pl.semaphore_wait(barrier, len(peers) + nz - jnp.where(source(z) == me, 1, 0))

    def piece(buf, shard, size=BLK):
        return buf.at[pl.ds(shard * size, size)]

    def columns(ref, xx):
        return ref.at[:, :, pl.ds(pl.multiple_of(xx * BL, BL), BL)]

    def deal(d):
        return remote(
            columns(expr, wrap(x + d, NX)), piece(x0, me), xs_s.at[d - 1], xs_r.at[d - 1], x_dev(d)
        )

    own_in = pltpu.make_async_copy(columns(expr, x), piece(x0, me), loc.at[0])
    own_in.start()
    for d in (1, 3, 2):
        deal(d).start()

    slot = lax.broadcasted_iota(jnp.int32, (1, BLK), 1)
    lv[x] = jnp.zeros((6 * BLK, BL), jnp.int32)
    for b in range(BLK):
        lv[x, b:b + 1, 0:BLK] = jnp.where(slot < count[b], far[b:b + 1, :], nz * 2 * NX * BLK)
    lv[x, BLK:BLK + LOC, 0:BLK] = near[...]
    block = lv[x, 0:2 * BLK, :]
    lv[x, 2 * BLK:4 * BLK, :] = (block >> 3) * HALF + (block & (HALF - 1))
    lv[x, 4 * BLK:6 * BLK, :] = (block >> 2) & 1

    def names(d):
        return remote(lv.at[x], lv.at[x], li_s.at[d - 1], li_r.at[d - 1], x_dev(d))

    for d in (1, 2, 3):
        names(d).start()

    own_w = pltpu.make_async_copy(aff, w.at[x], loc.at[2])

    def wsub(xx, hh, i):
        return w.at[xx, 4 * hh + i]

    def w_first(way, n):
        i = n if way == 0 else 3 - n
        return remote(
            aff.at[4 * half + i], wsub(x, half, i), wx_s.at[way, n], wx_r.at[way, n],
            x_dev(1 if way == 0 else 3),
        )

    def w_forward(way, n):
        i = n if way == 0 else 3 - n
        ref = wsub(wrap(x - 1, NX) if way == 0 else wrap(x + 1, NX), half, i)
        return remote(ref, ref, wf_s.at[way, n], wf_r.at[way, n], x_dev(1 if way == 0 else 3))

    def w_across(e, i):
        ref = wsub(wrap(x + (3, 1, 2)[e], NX), half, i)
        return remote(ref, ref, wy_s.at[e, i], wy_r.at[e, i], up if i < 2 else down)

    for n in range(4):
        w_first(0, n).start()
        w_first(1, n).start()
    own_w.start()

    def w_serve(n):
        for way in range(2):
            i = n % 4 if way == 0 else 3 - n % 4
            if n < 4:
                w_first(way, n).wait_recv()
                if n < 2:
                    w_forward(way, n).start()
                w_across(way, i).start()
            else:
                w_forward(way, n - 4).wait_recv()
                w_across(2, i).start()

    def shard_of(zz, j, kk):
        return cell(wrap(zz, nz), wrap(x - j, NX), kk)

    def z_copy(n, buf, way, s, shard):
        ref = piece(buf, shard, BLK if n == 0 else HALF)
        return remote(
            ref, ref, z_s.at[n, way, s], z_r.at[n, way, s], right if way == 0 else left
        )

    def p_copy(n, buf, q, shard):
        ref = piece(buf, shard, BLK if n == 0 else HALF)
        return remote(ref, ref, p_s.at[n, q], p_r.at[n, q], partner)

    def from_left(r, kk):
        return shard_of(z - 1 - r // 4, lax.rem(r, 4), kk)

    def from_right(r, kk):
        j = lax.rem(r, 4) + jnp.where(r < flow_len - 2, 0, 2)
        return shard_of(z + 1 + r // 4, j, kk)

    def send_own(n, buf, j):
        shard = shard_of(z, j, core)
        z_copy(n, buf, 0, j, shard).start()
        z_copy(n, buf, 1, j, shard).start()
        p_copy(n, buf, j, shard).start()

    def pass_step(n, buf, r):
        shard = from_left(r, core)
        z_copy(n, buf, 0, r, shard).wait_recv()

        @pl.when(r + 4 < flow_len)
        def _():
            z_copy(n, buf, 0, r + 4, shard).start()

        p_copy(n, buf, 4 + r, shard).start()
        other = from_right(r, core)
        z_copy(n, buf, 1, r, other).wait_recv()

        @pl.when(r < flow_len - 6)
        def _():
            z_copy(n, buf, 1, r + 4, other).start()

        @pl.when((r >= flow_len - 4) & (r < flow_len - 2))
        def _():
            z_copy(n, buf, 1, r + 2, other).start()

        p_copy(n, buf, 4 + flow_len + r, other).start()

    def pass_on(n, buf, first, last):
        @pl.loop(first, last)
        def _(r):
            pass_step(n, buf, r)

    def partner_own(n, buf):
        @pl.loop(0, 4)
        def _(j):
            p_copy(n, buf, j, shard_of(z, j, 1 - core)).wait_recv()

    def partner_done(n, buf, first, last):
        @pl.loop(first, last)
        def _(r):
            p_copy(n, buf, 4 + r, from_left(r, 1 - core)).wait_recv()
            p_copy(n, buf, 4 + flow_len + r, from_right(r, 1 - core)).wait_recv()

    def sends_done(n, buf):
        shard = shard_of(z, 0, core)

        @pl.loop(0, flow_len)
        def _(s):
            z_copy(n, buf, 0, s, shard).wait_send()
            z_copy(n, buf, 1, s, shard).wait_send()

        @pl.loop(0, 4 + 2 * flow_len)
        def _(q):
            p_copy(n, buf, q, shard).wait_send()

    def name(xs, b, slot, part=0):
        first = 2 * BLK * part
        return ls[xs, first + BLK + slot, b] if slot < LOC else ls[xs, first + b, slot - LOC]

    def weighted(xs, b, rows):
        total = None
        for pair in range(SLOTS // 2):
            mats = [w[xs, b, 2 * pair + i] for i in range(2)]
            term = jnp.dot(
                jnp.concatenate(mats, axis=1),
                jnp.concatenate([rows(2 * pair), rows(2 * pair + 1)], axis=0),
                preferred_element_type=jnp.float32,
            )
            total = term if total is None else total + term
        return total

    on_left = lax.broadcasted_iota(jnp.int32, (BL, BL), 1) < BL // 2

    def swap(tile):
        return pltpu.roll(tile, BL // 2, 1)

    def step_one(xs, p, shard):
        low, high = [weighted(xs, b, lambda slot: x0[name(xs, b, slot)]) for b in (p, p + HALF)]
        x1a[shard * HALF + p] = jnp.where(on_left, low, swap(high)).astype(jnp.bfloat16)
        x1b[shard * HALF + p] = jnp.where(on_left, swap(low), high).astype(jnp.bfloat16)

    def step_two(h, xs, p):
        buf = x1a if h == 0 else x1b

        def one(b):
            def rows(slot):
                tile = buf[name(xs, b, slot, 1)].reshape(BLK, BL // BLK, BL)
                return (tile * lanes[name(xs, b, slot, 2)][None]).reshape(BL, BL)

            both = weighted(xs, b, rows)
            return both + swap(both)

        tile = jnp.where(on_left, one(p), one(p + HALF)).astype(jnp.bfloat16)
        sx[h, x, xs, p] = tile
        st[h, y, :, pl.ds(pl.multiple_of((xs * HALF + p) * BL, BL), BL)] = tile.T

    zeros = jnp.zeros((BL, BL), jnp.bfloat16)
    x0[nz * 2 * NX * BLK] = zeros
    x1a[nz * 2 * NX * HALF] = zeros
    x1b[nz * 2 * NX * HALF] = zeros
    for i in range(2):
        keep = on_left if i == 0 else jnp.logical_not(on_left)
        lanes[i] = jnp.where(keep, 1.0, 0.0)[0:BL // BLK].astype(jnp.bfloat16)

    own_in.wait()
    send_own(0, x0, 0)
    for j in (1, 3, 2):
        deal(j).wait_recv()
        send_own(0, x0, j)
    cuts = (0, 4, 6, 8, 9, 11, 12)
    for part in range(6):
        pass_on(0, x0, cuts[part], cuts[part + 1])
        w_serve(part)
    for d in (1, 2, 3):
        names(d).wait_recv()
    to_smem = pltpu.make_async_copy(lv, ls, loc.at[1])
    to_smem.start()
    partner_own(0, x0)
    partner_done(0, x0, 0, 9)
    to_smem.wait()
    own_w.wait()
    pass_on(0, x0, 12, flow_len)
    for e in range(3):
        for i in range(4):
            w_across(e, i).wait_recv()
    partner_done(0, x0, 9, flow_len)

    @pl.loop(0, NX)
    def _(j):
        @pl.loop(0, HALF)
        def _(p):
            step_one(wrap(x - j, NX), p, shard_of(z, j, core))

        send_own(1, x1a, j)

    pass_on(1, x1a, 0, 8)
    for d in (1, 2, 3):
        deal(d).wait_send()
        names(d).wait_send()
        for i in range(4):
            w_across(d - 1, i).wait_send()
    for way in range(2):
        for n in range(2):
            w_forward(way, n).wait_send()
        for n in range(4):
            w_first(way, n).wait_send()
    sends_done(0, x0)
    pass_on(1, x1a, 8, 10)

    @pl.loop(10, flow_len)
    def _(r):
        pass_step(1, x1a, r)
        send_own(2, x1b, r - 10)

    partner_own(1, x1a)
    partner_done(1, x1a, 0, flow_len)

    def turn_x(h, way, n, xt, xc):
        ref = sx.at[h, xt, xc]
        return remote(
            ref, ref, g_s.at[h, 0, way, n], g_r.at[h, 0, way, n], x_dev(1 if way == 0 else 3)
        )

    def turn_y(h, way, n, yt, xc):
        ref = st.at[h, yt, :, pl.ds(pl.multiple_of(xc * HALF * BL, BL), HALF * BL)]
        return remote(
            ref, ref, g_s.at[h, 1, way, n], g_r.at[h, 1, way, n], up if way == 0 else down
        )

    xl, xr, xo = wrap(x - 1, NX), wrap(x + 1, NX), wrap(x + 2, NX)
    yd, yu, yo = wrap(y - 1, NY), wrap(y + 1, NY), wrap(y + 2, NY)

    def turn_own(h, j):
        xc = wrap(x - j, NX)
        for way in range(2):
            turn_x(h, way, j, x, xc).start()
            turn_y(h, way, j, y, xc).start()

    def turn_step(h, j):
        turn_x(h, 0, j, xl, wrap(xl - j, NX)).wait_recv()
        turn_y(h, 0, j, yd, wrap(x - j, NX)).wait_recv()
        if j < 2:
            turn_x(h, 0, 4 + j, xl, wrap(xl - j, NX)).start()
            turn_y(h, 0, 4 + j, yd, wrap(x - j, NX)).start()
        turn_x(h, 1, j, xr, wrap(xr - j, NX)).wait_recv()
        turn_y(h, 1, j, yu, wrap(x - j, NX)).wait_recv()
        if j >= 2:
            turn_x(h, 1, 2 + j, xr, wrap(xr - j, NX)).start()
            turn_y(h, 1, 2 + j, yu, wrap(x - j, NX)).start()

    def turn_end(h):
        for j in range(2):
            turn_x(h, 0, 4 + j, xo, wrap(xo - j, NX)).wait_recv()
            turn_y(h, 0, 4 + j, yo, wrap(x - j, NX)).wait_recv()
            turn_x(h, 1, 4 + j, xo, wrap(xo - 2 - j, NX)).wait_recv()
            turn_y(h, 1, 4 + j, yo, wrap(x - 2 - j, NX)).wait_recv()

    def product(hr, yts, hc, xts):
        lhs = jnp.concatenate([st[hr, yt] for yt in yts], axis=0)
        rhs = jnp.concatenate(
            [sx[hc, xt].reshape(NX * HALF * BL, BL) for xt in xts], axis=1
        )
        part = jnp.dot(lhs, rhs, preferred_element_type=jnp.float32)
        mid = BL // 2
        for i, yt in enumerate(yts):
            for k, xt in enumerate(xts):
                cols = pl.ds(xt * BL if isinstance(xt, int) else pl.multiple_of(xt * BL, BL), BL)
                upper = part[i * BL:i * BL + mid, k * BL:(k + 1) * BL]
                lower = part[i * BL + mid:(i + 1) * BL, k * BL:(k + 1) * BL]
                if hc == 0:
                    tile = (upper + swap(lower)).reshape(2, 32, BL)
                else:
                    tile = (swap(upper) + lower).reshape(2, 32, BL)
                    tile = jnp.where(on_left[0:mid].reshape(2, 32, BL), gram[yt, hr, :, :, cols], tile)
                gram[yt, hr, :, :, cols] = tile

    @pl.loop(0, 8)
    def _(r):
        pass_step(2, x1b, r)
        j = r // 2
        for i in range(2):
            step_two(0, wrap(x - j, NX), 2 * lax.rem(r, 2) + i)

        @pl.when(lax.rem(r, 2) == 1)
        def _():
            turn_own(0, j)

    pass_on(2, x1b, 8, 11)
    turn_step(0, 0)
    turn_step(0, 1)
    sends_done(1, x1a)
    pass_on(2, x1b, 11, 13)
    turn_step(0, 2)
    turn_step(0, 3)
    partner_own(2, x1b)
    partner_done(2, x1b, 0, 10)
    pass_on(2, x1b, 13, flow_len)
    partner_done(2, x1b, 10, flow_len)

    @pl.loop(0, NX)
    def _(j):
        @pl.loop(0, HALF)
        def _(p):
            step_two(1, wrap(x - j, NX), p)

        turn_own(1, j)

    turn_end(0)
    every = list(range(NY))
    product(0, every, 0, [0, 1])
    product(0, every, 0, [2, 3])
    for j in range(NX):
        turn_step(1, j)
    near_y = [y, yd, yu]
    product(1, near_y, 0, [0, 1])
    product(1, near_y, 0, [2, 3])
    product(0, every, 1, [x, xl])
    product(0, every, 1, [xr])
    product(1, near_y, 1, [x, xl])
    product(1, near_y, 1, [xr])
    turn_end(1)
    product(0, every, 1, [xo])
    product(1, near_y, 1, [xo])
    product(1, [yo], 0, [0, 1])
    product(1, [yo], 0, [2, 3])
    product(1, [yo], 1, [x, xl])
    product(1, [yo], 1, [xr, xo])

    other = remote(gram.at[:, :, 1 - core], r1, a_s.at[0], a_r.at[0], partner)
    other.start()

    def to_owner(n):
        return remote(rz.at[n // 2, n % 2], r3.at[z], c_s.at[n], c_r.at[z], (sink(n), y))

    other.wait_recv()
    for n in range(nz):
        both = r1[n // 2, n % 2] + gram[n // 2, n % 2, core]
        rz[n // 2, n % 2] = both.astype(jnp.bfloat16)

        @pl.when(sink(n) != me)
        def _():
            to_owner(n).start()

    for xt in range(NX):
        cols = pl.ds(xt * BL, BL)
        for p in range(HALF):
            half_a = sx[0, xt, x, p].astype(jnp.float32)
            half_b = sx[1, xt, x, p].astype(jnp.float32)
            whole[p, :, cols] = jnp.where(on_left, half_a, swap(half_b)).astype(jnp.bfloat16)
            whole[p + HALF, :, cols] = jnp.where(on_left, swap(half_a), half_b).astype(jnp.bfloat16)
    own_out = pltpu.make_async_copy(whole, out, loc.at[0])
    own_out.start()
    for h in range(2):
        for way in range(2):
            for n in range(6):
                turn_x(h, way, n, x, x).wait_send()
                turn_y(h, way, n, y, x).wait_send()
    sends_done(2, x1b)
    other.wait_send()

    @pl.when(source(z) == me)
    def _():
        r3[z] = rz[z // 2, lax.rem(x, 2)]

    for zz in range(nz):
        @pl.when(source(zz) != me)
        def _():
            remote(rz.at[0, 0], r3.at[zz], c_s.at[0], c_r.at[zz], (source(zz), y)).wait_recv()

    total = r3[0].astype(jnp.float32)
    for zz in range(1, nz):
        total += r3[zz].astype(jnp.float32)
    cov[...] = total * scale
    for n in range(nz):
        @pl.when(sink(n) != me)
        def _():
            to_owner(n).wait_send()
    own_out.wait()


def diffuse(expression, affinity, near, far, count, nz):
    shards = nz * 2 * NX
    flow_len = 4 * (nz // 2) - 2
    dma = pltpu.SemaphoreType.DMA
    any_spec = pl.BlockSpec(memory_space=pl.ANY)
    return pl.pallas_call(
        functools.partial(diffuse_kernel, nz, 1.0 / (shards * BLK * BL)),
        out_shape=(
            jax.ShapeDtypeStruct(expression.shape, jnp.bfloat16),
            jax.ShapeDtypeStruct((32, NX * BL), jnp.float32),
        ),
        in_specs=[
            any_spec,
            any_spec,
            pl.BlockSpec(memory_space=pltpu.VMEM),
            pl.BlockSpec(memory_space=pltpu.VMEM),
            pl.BlockSpec(memory_space=pltpu.SMEM),
        ],
        out_specs=(any_spec, pl.BlockSpec(memory_space=pltpu.VMEM)),
        scratch_shapes=[
            pltpu.VMEM((shards * BLK + 1, BL, BL), jnp.bfloat16),
            pltpu.VMEM((shards * HALF + 1, BL, BL), jnp.bfloat16),
            pltpu.VMEM((shards * HALF + 1, BL, BL), jnp.bfloat16),
            pltpu.VMEM((NX, BLK, SLOTS, BL, BL), jnp.bfloat16),
            pltpu.VMEM((NX, 6 * BLK, BL), jnp.int32),
            pltpu.SMEM((NX, 6 * BLK, BL), jnp.int32),
            pltpu.VMEM((2, BL // BLK, BL), jnp.bfloat16),
            pltpu.VMEM((2, NX, NX, HALF, BL, BL), jnp.bfloat16),
            pltpu.VMEM((2, NY, BL, NX * HALF * BL), jnp.bfloat16),
            pltpu.VMEM((BLK, BL, NX * BL), jnp.bfloat16),
            pltpu.VMEM((NY, 2, 2, 32, NX * BL), jnp.float32),
            pltpu.VMEM((NY, 2, 32, NX * BL), jnp.float32),
            pltpu.VMEM((NY, 2, 32, NX * BL), jnp.bfloat16),
            pltpu.VMEM((nz, 32, NX * BL), jnp.bfloat16),
            dma((4,)),
            dma((3,)), dma((3,)),
            dma((3,)), dma((3,)),
            dma((2, 4)), dma((2, 4)),
            dma((2, 2)), dma((2, 2)),
            dma((3, 4)), dma((3, 4)),
            dma((3, 2, flow_len)), dma((3, 2, flow_len)),
            dma((3, 4 + 2 * flow_len)), dma((3, 4 + 2 * flow_len)),
            dma((2, 2, 2, 6)), dma((2, 2, 2, 6)),
            dma((1,)), dma((1,)),
            dma((nz,)), dma((nz,)),
        ],
        compiler_params=pltpu.CompilerParams(
            collective_id=0, has_side_effects=True, vmem_limit_bytes=60 * 2**20
        ),
    )(expression, affinity, near, far, count)


def body(nz, expression, affinity, near_blocks, far_blocks, far_count):
    blocks = expression.reshape(BLK, BL, expression.shape[1])
    current, covariance = diffuse(
        blocks, affinity, near_blocks.T, far_blocks, far_count, nz
    )
    return (current.reshape(expression.shape), covariance)


def solution(mesh):
    nz = mesh.shape["cells"] // (2 * NX)
    return jax.shard_map(
        functools.partial(body, nz),
        mesh=mesh,
        in_specs=(
            P("cells", "genes"),
            P("cells", None, None, None),
            P("cells", None),
            P("cells", None),
            P("cells"),
        ),
        out_specs=(P("cells", "genes"), P("cells", "genes")),
        check_vma=False,
    )
```

```python
import functools

import jax
import jax.numpy as jnp
from jax import lax
from jax.experimental import pallas as pl
from jax.experimental.pallas import tpu as pltpu
from jax.sharding import PartitionSpec as P

MESH = pl.DeviceIdType.MESH
NX = 4
NY = 4
BL = 128
BLK = 8
SLOTS = 12
LOC = 4
HALF = BLK // 2


def remote(src, dst, send, recv, device):
    return pltpu.make_async_remote_copy(
        src_ref=src, dst_ref=dst, send_sem=send, recv_sem=recv, device_id=device, device_id_type=MESH
    )


def diffuse_kernel(
    nz, scale, expr, aff, near, far, count, out, cov, x0, x1a, x1b, w, lv, ls,
    near_v, far_v, count_s, lanes, sx, st, whole, gram, r1, rz, r3,
    loc, xs_s, xs_r, li_s, li_r, w_s, wx_r, wf_r, wy_r,
    z_s, z_r, p_s, p_r, g_s, g_r, a_s, a_r, c_s, c_r,
):
    flow_len = 4 * (nz // 2) - 2
    me = lax.axis_index("cells")
    y = lax.axis_index("genes")
    core = lax.rem(me, 2)
    x = lax.rem(me // 2, NX)
    z = me // (2 * NX)
    half = lax.rem(y, 2)

    def cell(zz, xx, kk):
        return (zz * NX + xx) * 2 + kk

    def wrap(v, n):
        return lax.rem(v + n, n)

    def x_dev(d):
        return (cell(z, wrap(x + d, NX), core), y)

    right = (cell(wrap(z + 1, nz), x, core), y)
    left = (cell(wrap(z - 1, nz), x, core), y)
    partner = (cell(z, x, 1 - core), y)
    up = (me, wrap(y + 1, NY))
    down = (me, wrap(y - 1, NY))

    def sink(n):
        return cell(2 * (n // 2) + x // 2, 2 * lax.rem(x, 2) + n % 2, core)

    def source(zz):
        return cell(zz, 2 * lax.rem(z, 2) + x // 2, core)

    barrier = pltpu.get_barrier_semaphore()
    peers = [x_dev(1), x_dev(2), x_dev(3), right, left, partner, up, down]
    for peer in peers:
        pl.semaphore_signal(barrier, inc=1, device_id=peer, device_id_type=MESH)
    for zz in range(nz):
        @pl.when(source(zz) != me)
        def _():
            pl.semaphore_signal(barrier, inc=1, device_id=(source(zz), y), device_id_type=MESH)

    def piece(buf, shard, size=BLK):
        return buf.at[pl.ds(shard * size, size)]

    def columns(ref, xx):
        return ref.at[:, :, pl.ds(pl.multiple_of(xx * BL, BL), BL)]

    def deal(d):
        return remote(
            columns(expr, wrap(x + d, NX)), piece(x0, me), xs_s.at[0], xs_r.at[d - 1], x_dev(d)
        )

    own_in = pltpu.make_async_copy(columns(expr, x), piece(x0, me), loc.at[0])
    def names(d):
        return remote(lv.at[x], lv.at[x], li_s.at[0], li_r.at[0], x_dev(d))

    own_w = pltpu.make_async_copy(aff, w.at[x], loc.at[2])

    def wsub(xx, hh, i):
        return w.at[xx, 4 * hh + i]

    def w_first(way, n):
        i = n if way == 0 else 3 - n
        return remote(
            aff.at[4 * half + i], wsub(x, half, i), w_s.at[0], wx_r.at[way, n],
            x_dev(1 if way == 0 else 3),
        )

    def w_forward(way, n):
        i = n if way == 0 else 3 - n
        ref = wsub(wrap(x - 1, NX) if way == 0 else wrap(x + 1, NX), half, i)
        return remote(ref, ref, w_s.at[0], wf_r.at[way, n], x_dev(1 if way == 0 else 3))

    def w_across(e, i):
        ref = wsub(wrap(x + (3, 1, 2)[e], NX), half, i)
        return remote(ref, ref, w_s.at[0], wy_r.at[0], up if i < 2 else down)

    def w_serve(n):
        for way in range(2):
            i = n % 4 if way == 0 else 3 - n % 4
            if n < 4:
                w_first(way, n).wait_recv()
                if n < 2:
                    w_forward(way, n).start()
                w_across(way, i).start()
            else:
                w_forward(way, n - 4).wait_recv()
                w_across(2, i).start()

    def shard_of(zz, j, kk):
        return cell(wrap(zz, nz), wrap(x - j, NX), kk)

    def z_copy(n, buf, way, s, shard):
        ref = piece(buf, shard, BLK if n == 0 else HALF)
        return remote(
            ref, ref, z_s.at[n], z_r.at[n % 2, way, s], right if way == 0 else left
        )

    def p_copy(n, buf, q, shard):
        ref = piece(buf, shard, BLK if n == 0 else HALF)
        return remote(ref, ref, p_s.at[n], p_r.at[n], partner)

    def from_left(r, kk):
        return shard_of(z - 1 - r // 4, lax.rem(r, 4), kk)

    def from_right(r, kk):
        j = lax.rem(r, 4) + jnp.where(r < flow_len - 2, 0, 2)
        return shard_of(z + 1 + r // 4, j, kk)

    def send_own(n, buf, j):
        shard = shard_of(z, j, core)
        z_copy(n, buf, 0, j, shard).start()
        z_copy(n, buf, 1, j, shard).start()
        p_copy(n, buf, j, shard).start()

    def pass_step(n, buf, r):
        shard = from_left(r, core)
        z_copy(n, buf, 0, r, shard).wait_recv()

        @pl.when(r + 4 < flow_len)
        def _():
            z_copy(n, buf, 0, r + 4, shard).start()

        p_copy(n, buf, 4 + r, shard).start()
        other = from_right(r, core)
        z_copy(n, buf, 1, r, other).wait_recv()

        @pl.when(r < flow_len - 6)
        def _():
            z_copy(n, buf, 1, r + 4, other).start()

        @pl.when((r >= flow_len - 4) & (r < flow_len - 2))
        def _():
            z_copy(n, buf, 1, r + 2, other).start()

        p_copy(n, buf, 4 + flow_len + r, other).start()

    def pass_on(n, buf, first, last):
        @pl.loop(first, last)
        def _(r):
            pass_step(n, buf, r)

    def several(ref, send, recv):
        return remote(ref, ref, send, recv, partner)

    def partner_done(n, buf):
        size = (BLK if n == 0 else HALF) * (4 + 2 * flow_len)
        several(buf.at[pl.ds(0, size)], p_s.at[n], p_r.at[n]).wait_recv()

    def sends_done(n, buf):
        size = BLK if n == 0 else HALF
        several(buf.at[pl.ds(0, size * 2 * flow_len)], z_s.at[n], p_r.at[n]).wait_send()
        several(buf.at[pl.ds(0, size * (4 + 2 * flow_len))], p_s.at[n], p_r.at[n]).wait_send()

    def name(xs, b, slot, part=0):
        first = 2 * BLK * part
        return ls[xs, first + BLK + slot, b] if slot < LOC else ls[xs, first + b, slot - LOC]

    def weighted(xs, b, rows):
        total = None
        for pair in range(SLOTS // 2):
            mats = [w[xs, b, 2 * pair + i] for i in range(2)]
            term = jnp.dot(
                jnp.concatenate(mats, axis=1),
                jnp.concatenate([rows(2 * pair), rows(2 * pair + 1)], axis=0),
                preferred_element_type=jnp.float32,
            )
            total = term if total is None else total + term
        return total

    on_left = lax.broadcasted_iota(jnp.int32, (BL, BL), 1) < BL // 2

    def swap(tile):
        return pltpu.roll(tile, BL // 2, 1)

    def step_one(xs, p, shard):
        low, high = [weighted(xs, b, lambda slot: x0[name(xs, b, slot)]) for b in (p, p + HALF)]
        x1a[shard * HALF + p] = jnp.where(on_left, low, swap(high)).astype(jnp.bfloat16)
        x1b[shard * HALF + p] = jnp.where(on_left, swap(low), high).astype(jnp.bfloat16)

    def step_two(h, xs, p):
        buf = x1a if h == 0 else x1b

        def one(b):
            def rows(slot):
                tile = buf[name(xs, b, slot, 1)].reshape(BLK, BL // BLK, BL)
                return (tile * lanes[name(xs, b, slot, 2)][None]).reshape(BL, BL)

            both = weighted(xs, b, rows)
            return both + swap(both)

        tile = jnp.where(on_left, one(p), one(p + HALF)).astype(jnp.bfloat16)
        sx[h, x, xs, p] = tile
        st[h, y, :, pl.ds(pl.multiple_of((xs * HALF + p) * BL, BL), BL)] = tile.T

    small = [
        pltpu.make_async_copy(near, near_v, loc.at[1]),
        pltpu.make_async_copy(far, far_v, loc.at[3]),
        pltpu.make_async_copy(count, count_s, loc.at[4]),
    ]
    for copy in small:
        copy.start()
    own_in.start()
    own_w.start()
    zeros = jnp.zeros((BL, BL), jnp.bfloat16)
    x0[nz * 2 * NX * BLK] = zeros
    x1a[nz * 2 * NX * HALF] = zeros
    x1b[nz * 2 * NX * HALF] = zeros
    for i in range(2):
        keep = on_left if i == 0 else jnp.logical_not(on_left)
        lanes[i] = jnp.where(keep, 1.0, 0.0)[0:BL // BLK].astype(jnp.bfloat16)
    for copy in small:
        copy.wait()
    slot = lax.broadcasted_iota(jnp.int32, (1, BLK), 1)
    lv[x] = jnp.zeros((6 * BLK, BL), jnp.int32)
    for b in range(BLK):
        lv[x, b:b + 1, 0:BLK] = jnp.where(slot < count_s[b], far_v[b:b + 1, :], nz * 2 * NX * BLK)
    lv[x, BLK:BLK + LOC, 0:BLK] = near_v[...]
    block = lv[x, 0:2 * BLK, :]
    lv[x, 2 * BLK:4 * BLK, :] = (block >> 3) * HALF + (block & (HALF - 1))
    lv[x, 4 * BLK:6 * BLK, :] = (block >> 2) & 1
    own_in.wait()
    pl.semaphore_wait(barrier, len(peers) + nz - jnp.where(source(z) == me, 1, 0))

    send_own(0, x0, 0)
    for d in (1, 3, 2):
        deal(d).start()
    for d in (1, 2, 3):
        names(d).start()
    for n in range(4):
        w_first(0, n).start()
        w_first(1, n).start()
    for j in (1, 3, 2):
        deal(j).wait_recv()
        send_own(0, x0, j)
    cuts = (0, 4, 6, 8, 9, 11, 12)
    for part in range(6):
        pass_on(0, x0, cuts[part], cuts[part + 1])
        w_serve(part)
    several(lv.at[pl.ds(0, NX - 1)], li_s.at[0], li_r.at[0]).wait_recv()
    to_smem = pltpu.make_async_copy(lv, ls, loc.at[1])
    to_smem.start()
    to_smem.wait()
    own_w.wait()
    pass_on(0, x0, 12, flow_len)
    several(w.at[pl.ds(0, 3), pl.ds(0, 4)], w_s.at[0], wy_r.at[0]).wait_recv()
    partner_done(0, x0)

    @pl.loop(0, NX)
    def _(j):
        @pl.loop(0, HALF)
        def _(p):
            step_one(wrap(x - j, NX), p, shard_of(z, j, core))

        send_own(1, x1a, j)

    pass_on(1, x1a, 0, 8)
    several(piece(x0, 0, 3 * BLK), xs_s.at[0], xs_r.at[0]).wait_send()
    several(lv.at[pl.ds(0, NX - 1)], li_s.at[0], li_r.at[0]).wait_send()
    several(w.at[pl.ds(0, 3)], w_s.at[0], wy_r.at[0]).wait_send()
    sends_done(0, x0)
    pass_on(1, x1a, 8, 10)

    @pl.loop(10, flow_len)
    def _(r):
        pass_step(1, x1a, r)
        send_own(2, x1b, r - 10)

    partner_done(1, x1a)

    def passed(n):
        return min(n, 4) if isinstance(n, int) else n

    def turn_x(h, way, n, xt, xc):
        ref = sx.at[h, xt, xc]
        return remote(
            ref, ref, g_s.at[h, 0], g_r.at[h, 0, way, passed(n)], x_dev(1 if way == 0 else 3)
        )

    def turn_y(h, way, n, yt, xc):
        ref = st.at[h, yt, :, pl.ds(pl.multiple_of(xc * HALF * BL, BL), HALF * BL)]
        return remote(
            ref, ref, g_s.at[h, 1], g_r.at[h, 1, way, passed(n)], up if way == 0 else down
        )

    xl, xr, xo = wrap(x - 1, NX), wrap(x + 1, NX), wrap(x + 2, NX)
    yd, yu, yo = wrap(y - 1, NY), wrap(y + 1, NY), wrap(y + 2, NY)

    def turn_own(h, j):
        xc = wrap(x - j, NX)
        for way in range(2):
            turn_x(h, way, j, x, xc).start()
            turn_y(h, way, j, y, xc).start()

    def turn_step(h, j):
        turn_x(h, 0, j, xl, wrap(xl - j, NX)).wait_recv()
        turn_y(h, 0, j, yd, wrap(x - j, NX)).wait_recv()
        if j < 2:
            turn_x(h, 0, 4 + j, xl, wrap(xl - j, NX)).start()
            turn_y(h, 0, 4 + j, yd, wrap(x - j, NX)).start()
        turn_x(h, 1, j, xr, wrap(xr - j, NX)).wait_recv()
        turn_y(h, 1, j, yu, wrap(x - j, NX)).wait_recv()
        if j >= 2:
            turn_x(h, 1, 2 + j, xr, wrap(xr - j, NX)).start()
            turn_y(h, 1, 2 + j, yu, wrap(x - j, NX)).start()

    def turn_end(h):
        for way in range(2):
            several(sx.at[h, 0, pl.ds(0, 2)], g_s.at[h, 0], g_r.at[h, 0, way, 4]).wait_recv()
            several(st.at[h, 0, :, pl.ds(0, 2 * HALF * BL)], g_s.at[h, 1], g_r.at[h, 1, way, 4]).wait_recv()

    def product(hr, yts, hc, xts):
        lhs = jnp.concatenate([st[hr, yt] for yt in yts], axis=0)
        rhs = jnp.concatenate(
            [sx[hc, xt].reshape(NX * HALF * BL, BL) for xt in xts], axis=1
        )
        part = jnp.dot(lhs, rhs, preferred_element_type=jnp.float32)
        mid = BL // 2
        for i, yt in enumerate(yts):
            for k, xt in enumerate(xts):
                cols = pl.ds(xt * BL if isinstance(xt, int) else pl.multiple_of(xt * BL, BL), BL)
                upper = part[i * BL:i * BL + mid, k * BL:(k + 1) * BL]
                lower = part[i * BL + mid:(i + 1) * BL, k * BL:(k + 1) * BL]
                if hc == 0:
                    tile = (upper + swap(lower)).reshape(2, 32, BL)
                else:
                    tile = (swap(upper) + lower).reshape(2, 32, BL)
                    tile = jnp.where(on_left[0:mid].reshape(2, 32, BL), gram[yt, hr, :, :, cols], tile)
                gram[yt, hr, :, :, cols] = tile

    @pl.loop(0, 8)
    def _(r):
        pass_step(2, x1b, r)
        j = r // 2
        for i in range(2):
            step_two(0, wrap(x - j, NX), 2 * lax.rem(r, 2) + i)

        @pl.when(lax.rem(r, 2) == 1)
        def _():
            turn_own(0, j)

    pass_on(2, x1b, 8, 11)
    turn_step(0, 0)
    turn_step(0, 1)
    sends_done(1, x1a)
    pass_on(2, x1b, 11, 13)
    turn_step(0, 2)
    turn_step(0, 3)
    pass_on(2, x1b, 13, flow_len)
    partner_done(2, x1b)

    @pl.loop(0, NX)
    def _(j):
        @pl.loop(0, HALF)
        def _(p):
            step_two(1, wrap(x - j, NX), p)

        turn_own(1, j)

    turn_end(0)
    every = list(range(NY))
    product(0, every, 0, [0, 1])
    product(0, every, 0, [2, 3])
    for j in range(NX):
        turn_step(1, j)
    near_y = [y, yd, yu]
    product(1, near_y, 0, [0, 1])
    product(1, near_y, 0, [2, 3])
    product(0, every, 1, [x, xl])
    product(0, every, 1, [xr])
    product(1, near_y, 1, [x, xl])
    product(1, near_y, 1, [xr])
    turn_end(1)
    product(0, every, 1, [xo])
    product(1, near_y, 1, [xo])
    product(1, [yo], 0, [0, 1])
    product(1, [yo], 0, [2, 3])
    product(1, [yo], 1, [x, xl])
    product(1, [yo], 1, [xr, xo])

    other = remote(gram.at[:, :, 1 - core], r1, a_s.at[0], a_r.at[0], partner)
    other.start()

    def to_owner(n):
        return remote(rz.at[n // 2, n % 2], r3.at[z], c_s.at[0], c_r.at[0], (sink(n), y))

    other.wait_recv()
    for n in range(nz):
        both = r1[n // 2, n % 2] + gram[n // 2, n % 2, core]
        rz[n // 2, n % 2] = both.astype(jnp.bfloat16)

        @pl.when(sink(n) != me)
        def _():
            to_owner(n).start()

    for xt in range(NX):
        cols = pl.ds(xt * BL, BL)
        for p in range(HALF):
            half_a = sx[0, xt, x, p].astype(jnp.float32)
            half_b = sx[1, xt, x, p].astype(jnp.float32)
            whole[p, :, cols] = jnp.where(on_left, half_a, swap(half_b)).astype(jnp.bfloat16)
            whole[p + HALF, :, cols] = jnp.where(on_left, swap(half_a), half_b).astype(jnp.bfloat16)
    own_out = pltpu.make_async_copy(whole, out, loc.at[0])
    own_out.start()
    for h in range(2):
        several(sx.at[h, pl.ds(0, 3)], g_s.at[h, 0], g_r.at[h, 0, 0, 4]).wait_send()
        several(st.at[h, pl.ds(0, 3)], g_s.at[h, 1], g_r.at[h, 1, 0, 4]).wait_send()
    sends_done(2, x1b)
    other.wait_send()

    @pl.when(source(z) == me)
    def _():
        r3[z] = rz[z // 2, lax.rem(x, 2)]

    def all_sums(do):
        @pl.when(source(z) == me)
        def _():
            do(several(r3.at[pl.ds(0, nz - 1)], c_s.at[0], c_r.at[0]))

        @pl.when(source(z) != me)
        def _():
            do(several(r3, c_s.at[0], c_r.at[0]))

    all_sums(lambda copies: copies.wait_recv())
    total = r3[0].astype(jnp.float32)
    for zz in range(1, nz):
        total += r3[zz].astype(jnp.float32)
    cov[...] = total * scale
    all_sums(lambda copies: copies.wait_send())
    own_out.wait()


def diffuse(expression, affinity, near, far, count, nz):
    shards = nz * 2 * NX
    flow_len = 4 * (nz // 2) - 2
    dma = pltpu.SemaphoreType.DMA
    any_spec = pl.BlockSpec(memory_space=pl.ANY)
    return pl.pallas_call(
        functools.partial(diffuse_kernel, nz, 1.0 / (shards * BLK * BL)),
        out_shape=(
            jax.ShapeDtypeStruct(expression.shape, jnp.bfloat16),
            jax.ShapeDtypeStruct((32, NX * BL), jnp.float32),
        ),
        in_specs=[any_spec] * 5,
        out_specs=(any_spec, pl.BlockSpec(memory_space=pltpu.VMEM)),
        scratch_shapes=[
            pltpu.VMEM((shards * BLK + 1, BL, BL), jnp.bfloat16),
            pltpu.VMEM((shards * HALF + 1, BL, BL), jnp.bfloat16),
            pltpu.VMEM((shards * HALF + 1, BL, BL), jnp.bfloat16),
            pltpu.VMEM((NX, BLK, SLOTS, BL, BL), jnp.bfloat16),
            pltpu.VMEM((NX, 6 * BLK, BL), jnp.int32),
            pltpu.SMEM((NX, 6 * BLK, BL), jnp.int32),
            pltpu.VMEM((LOC, BLK), jnp.int32),
            pltpu.VMEM((BLK, BLK), jnp.int32),
            pltpu.SMEM((BLK,), jnp.int32),
            pltpu.VMEM((2, BL // BLK, BL), jnp.bfloat16),
            pltpu.VMEM((2, NX, NX, HALF, BL, BL), jnp.bfloat16),
            pltpu.VMEM((2, NY, BL, NX * HALF * BL), jnp.bfloat16),
            pltpu.VMEM((BLK, BL, NX * BL), jnp.bfloat16),
            pltpu.VMEM((NY, 2, 2, 32, NX * BL), jnp.float32),
            pltpu.VMEM((NY, 2, 32, NX * BL), jnp.float32),
            pltpu.VMEM((NY, 2, 32, NX * BL), jnp.bfloat16),
            pltpu.VMEM((nz, 32, NX * BL), jnp.bfloat16),
            dma((5,)),
            dma((1,)), dma((3,)),
            dma((1,)), dma((1,)),
            dma((1,)), dma((2, 4)), dma((2, 2)), dma((1,)),
            dma((3,)), dma((2, 2, flow_len)),
            dma((3,)), dma((3,)),
            dma((2, 2)), dma((2, 2, 2, 5)),
            dma((1,)), dma((1,)),
            dma((1,)), dma((1,)),
        ],
        compiler_params=pltpu.CompilerParams(
            collective_id=0, has_side_effects=True, vmem_limit_bytes=60 * 2**20
        ),
    )(expression, affinity, near, far, count)


def body(nz, expression, affinity, near_blocks, far_blocks, far_count):
    blocks = expression.reshape(BLK, BL, expression.shape[1])
    current, covariance = diffuse(
        blocks, affinity, near_blocks.T, far_blocks, far_count, nz
    )
    return (current.reshape(expression.shape), covariance)


def solution(mesh):
    nz = mesh.shape["cells"] // (2 * NX)
    return jax.shard_map(
        functools.partial(body, nz),
        mesh=mesh,
        in_specs=(
            P("cells", "genes"),
            P("cells", None, None, None),
            P("cells", None),
            P("cells", None),
            P("cells"),
        ),
        out_specs=(P("cells", "genes"), P("cells", "genes")),
        check_vma=False,
    )
```

```python
import functools

import jax
import jax.numpy as jnp
from jax import lax
from jax.experimental import pallas as pl
from jax.experimental.pallas import tpu as pltpu
from jax.sharding import PartitionSpec as P

MESH = pl.DeviceIdType.MESH
NX = 4
NY = 4
BL = 128
BLK = 8
SLOTS = 12
LOC = 4
HALF = BLK // 2


def remote(src, dst, send, recv, device):
    return pltpu.make_async_remote_copy(
        src_ref=src, dst_ref=dst, send_sem=send, recv_sem=recv, device_id=device, device_id_type=MESH
    )


def diffuse_kernel(
    nz, scale, expr, aff, near, far, count, out, cov, x0, x1a, x1b, w, lv, ls,
    near_v, far_v, count_s, lanes, sx, st, whole, gram, r1, rz, r3,
    loc, xs_s, xs_r, li_s, li_r, w_s, wx_r, wf_r, wy_r,
    z_s, z_r, p_s, p_r, g_s, g_r, a_s, a_r, c_s, c_r,
):
    me = lax.axis_index("cells")
    y = lax.axis_index("genes")
    core = lax.rem(me, 2)
    x = lax.rem(me // 2, NX)
    z = me // (2 * NX)
    half = lax.rem(y, 2)

    def cell(zz, xx, kk):
        return (zz * NX + xx) * 2 + kk

    def wrap(v, n):
        return lax.rem(v + n, n)

    def x_dev(d):
        return (cell(z, wrap(x + d, NX), core), y)

    right = (cell(wrap(z + 1, nz), x, core), y)
    left = (cell(wrap(z - 1, nz), x, core), y)
    partner = (cell(z, x, 1 - core), y)
    up = (me, wrap(y + 1, NY))
    down = (me, wrap(y - 1, NY))

    def sink(n):
        return cell(2 * (n // 2) + x // 2, 2 * lax.rem(x, 2) + n % 2, core)

    def source(zz):
        return cell(zz, 2 * lax.rem(z, 2) + x // 2, core)

    barrier = pltpu.get_barrier_semaphore()
    peers = [x_dev(1), x_dev(2), x_dev(3), right, left, partner, up, down]
    for peer in peers:
        pl.semaphore_signal(barrier, inc=1, device_id=peer, device_id_type=MESH)
    for zz in range(nz):
        @pl.when(source(zz) != me)
        def _():
            pl.semaphore_signal(barrier, inc=1, device_id=(source(zz), y), device_id_type=MESH)

    def piece(buf, shard, size=BLK):
        return buf.at[pl.ds(shard * size, size)]

    def columns(ref, xx):
        return ref.at[:, :, pl.ds(pl.multiple_of(xx * BL, BL), BL)]

    def deal(d):
        return remote(
            columns(expr, wrap(x + d, NX)), piece(x0, me), xs_s.at[0], xs_r.at[d - 1], x_dev(d)
        )

    own_in = pltpu.make_async_copy(columns(expr, x), piece(x0, me), loc.at[0])
    def names(d):
        return remote(lv.at[x], lv.at[x], li_s.at[0], li_r.at[0], x_dev(d))

    own_w = pltpu.make_async_copy(aff, w.at[x], loc.at[2])

    def wsub(xx, hh, i):
        return w.at[xx, 4 * hh + i]

    def w_first(way, n):
        i = n if way == 0 else 3 - n
        return remote(
            aff.at[4 * half + i], wsub(x, half, i), w_s.at[0], wx_r.at[way, n],
            x_dev(1 if way == 0 else 3),
        )

    def w_forward(way, n):
        i = n if way == 0 else 3 - n
        ref = wsub(wrap(x - 1, NX) if way == 0 else wrap(x + 1, NX), half, i)
        return remote(ref, ref, w_s.at[0], wf_r.at[way, n], x_dev(1 if way == 0 else 3))

    def w_across(e, i):
        ref = wsub(wrap(x + (3, 1, 2)[e], NX), half, i)
        return remote(ref, ref, w_s.at[0], wy_r.at[0], up if i < 2 else down)

    def w_serve(n):
        for way in range(2):
            i = n % 4 if way == 0 else 3 - n % 4
            if n < 4:
                w_first(way, n).wait_recv()
                if n < 2:
                    w_forward(way, n).start()
                w_across(way, i).start()
            else:
                w_forward(way, n - 4).wait_recv()
                w_across(2, i).start()

    def unit(n):
        return NX if n == 0 else 2 * NX

    def flow_len(n):
        return unit(n) * (nz // 2) - unit(n) // 2

    def shard_of(zz, j, kk):
        return cell(wrap(zz, nz), wrap(x - j, NX), kk)

    def place(n, zz, q, kk):
        if n == 0:
            return shard_of(zz, q, kk) * BLK
        return shard_of(zz, q // 2, kk) * HALF + 2 * lax.rem(q, 2)

    def part_of(n, buf, first):
        return buf.at[pl.ds(first, BLK if n == 0 else 2)]

    def z_copy(n, buf, way, s, first):
        ref = part_of(n, buf, first)
        return remote(
            ref, ref, z_s.at[n], z_r.at[n % 2, way, s], right if way == 0 else left
        )

    def p_copy(n, buf, first):
        ref = part_of(n, buf, first)
        return remote(ref, ref, p_s.at[n], p_r.at[n], partner)

    def from_left(n, r, kk):
        return place(n, z - 1 - r // unit(n), lax.rem(r, unit(n)), kk)

    def from_right(n, r, kk):
        half_unit = unit(n) // 2
        q = lax.rem(r, unit(n)) + jnp.where(r < flow_len(n) - half_unit, 0, half_unit)
        return place(n, z + 1 + r // unit(n), q, kk)

    def send_own(n, buf, q):
        first = place(n, z, q, core)
        z_copy(n, buf, 0, q, first).start()
        z_copy(n, buf, 1, q, first).start()
        p_copy(n, buf, first).start()

    def pass_step(n, buf, r):
        size, last = unit(n), flow_len(n)
        first = from_left(n, r, core)
        z_copy(n, buf, 0, r, first).wait_recv()

        @pl.when(r + size < last)
        def _():
            z_copy(n, buf, 0, r + size, first).start()

        p_copy(n, buf, first).start()
        other = from_right(n, r, core)
        z_copy(n, buf, 1, r, other).wait_recv()

        @pl.when(r < last - size - size // 2)
        def _():
            z_copy(n, buf, 1, r + size, other).start()

        @pl.when((r >= last - size) & (r < last - size // 2))
        def _():
            z_copy(n, buf, 1, r + size // 2, other).start()

        p_copy(n, buf, other).start()

    def pass_on(n, buf, first, last):
        @pl.loop(first, last)
        def _(r):
            pass_step(n, buf, r)

    def several(ref, send, recv):
        return remote(ref, ref, send, recv, partner)

    def partner_done(n, buf):
        size = (BLK if n == 0 else 2) * (unit(n) + 2 * flow_len(n))
        several(buf.at[pl.ds(0, size)], p_s.at[n], p_r.at[n]).wait_recv()

    def sends_done(n, buf):
        size = BLK if n == 0 else 2
        z_all, p_all = size * 2 * flow_len(n), size * (unit(n) + 2 * flow_len(n))
        several(buf.at[pl.ds(0, z_all)], z_s.at[n], p_r.at[n]).wait_send()
        several(buf.at[pl.ds(0, p_all)], p_s.at[n], p_r.at[n]).wait_send()

    def name(xs, b, slot, part=0):
        first = 2 * BLK * part
        return ls[xs, first + BLK + slot, b] if slot < LOC else ls[xs, first + b, slot - LOC]

    def weighted(xs, b, rows):
        return jnp.dot(
            jnp.concatenate([w[xs, b, slot] for slot in range(SLOTS)], axis=1),
            jnp.concatenate([rows(slot) for slot in range(SLOTS)], axis=0),
            preferred_element_type=jnp.float32,
        )

    on_left = lax.broadcasted_iota(jnp.int32, (BL, BL), 1) < BL // 2

    def swap(tile):
        return pltpu.roll(tile, BL // 2, 1)

    def step_one(xs, p, shard):
        low, high = [weighted(xs, b, lambda slot: x0[name(xs, b, slot)]) for b in (p, p + HALF)]
        x1a[shard * HALF + p] = jnp.where(on_left, low, swap(high)).astype(jnp.bfloat16)
        x1b[shard * HALF + p] = jnp.where(on_left, swap(low), high).astype(jnp.bfloat16)

    def step_two(h, xs, p):
        buf = x1a if h == 0 else x1b

        def one(b):
            def rows(slot):
                tile = buf[name(xs, b, slot, 1)].reshape(BLK, BL // BLK, BL)
                return (tile * lanes[name(xs, b, slot, 2)][None]).reshape(BL, BL)

            both = weighted(xs, b, rows)
            return both + swap(both)

        tile = jnp.where(on_left, one(p), one(p + HALF)).astype(jnp.bfloat16)
        sx[h, x, xs, p] = tile
        st[h, y, :, pl.ds(pl.multiple_of((xs * HALF + p) * BL, BL), BL)] = tile.T

    small = [
        pltpu.make_async_copy(near, near_v, loc.at[1]),
        pltpu.make_async_copy(far, far_v, loc.at[3]),
        pltpu.make_async_copy(count, count_s, loc.at[4]),
    ]
    for copy in small:
        copy.start()
    own_in.start()
    own_w.start()
    zeros = jnp.zeros((BL, BL), jnp.bfloat16)
    x0[nz * 2 * NX * BLK] = zeros
    x1a[nz * 2 * NX * HALF] = zeros
    x1b[nz * 2 * NX * HALF] = zeros
    for i in range(2):
        keep = on_left if i == 0 else jnp.logical_not(on_left)
        lanes[i] = jnp.where(keep, 1.0, 0.0)[0:BL // BLK].astype(jnp.bfloat16)
    for copy in small:
        copy.wait()
    slot = lax.broadcasted_iota(jnp.int32, (1, BLK), 1)
    lv[x] = jnp.zeros((6 * BLK, BL), jnp.int32)
    for b in range(BLK):
        lv[x, b:b + 1, 0:BLK] = jnp.where(slot < count_s[b], far_v[b:b + 1, :], nz * 2 * NX * BLK)
    lv[x, BLK:BLK + LOC, 0:BLK] = near_v[...]
    block = lv[x, 0:2 * BLK, :]
    lv[x, 2 * BLK:4 * BLK, :] = (block >> 3) * HALF + (block & (HALF - 1))
    lv[x, 4 * BLK:6 * BLK, :] = (block >> 2) & 1
    own_in.wait()
    pl.semaphore_wait(barrier, len(peers) + nz - jnp.where(source(z) == me, 1, 0))

    send_own(0, x0, 0)
    for d in (1, 3, 2):
        deal(d).start()
    for d in (1, 2, 3):
        names(d).start()
    for n in range(4):
        w_first(0, n).start()
        w_first(1, n).start()
    for j in (1, 3, 2):
        deal(j).wait_recv()
        send_own(0, x0, j)
    cuts = (0, 4, 6, 8, 9, 11, 12)
    for part in range(6):
        pass_on(0, x0, cuts[part], cuts[part + 1])
        w_serve(part)
    several(lv.at[pl.ds(0, NX - 1)], li_s.at[0], li_r.at[0]).wait_recv()
    to_smem = pltpu.make_async_copy(lv, ls, loc.at[1])
    to_smem.start()
    to_smem.wait()
    own_w.wait()
    pass_on(0, x0, 12, flow_len(0))
    several(w.at[pl.ds(0, 3), pl.ds(0, 4)], w_s.at[0], wy_r.at[0]).wait_recv()
    partner_done(0, x0)

    @pl.loop(0, 2 * NX)
    def _(q):
        j = q // 2
        for i in range(2):
            step_one(wrap(x - j, NX), 2 * lax.rem(q, 2) + i, shard_of(z, j, core))
        send_own(1, x1a, q)

    pass_on(1, x1a, 0, 16)
    several(piece(x0, 0, 3 * BLK), xs_s.at[0], xs_r.at[0]).wait_send()
    several(lv.at[pl.ds(0, NX - 1)], li_s.at[0], li_r.at[0]).wait_send()
    several(w.at[pl.ds(0, 3)], w_s.at[0], wy_r.at[0]).wait_send()
    sends_done(0, x0)
    pass_on(1, x1a, 16, 20)

    @pl.loop(20, flow_len(1))
    def _(r):
        pass_step(1, x1a, r)
        send_own(2, x1b, r - 20)

    partner_done(1, x1a)

    def passed(n):
        return min(n, 8) if isinstance(n, int) else n

    def turn_x(h, way, n, xt, q):
        ref = sx.at[h, xt, wrap(xt - q // 2, NX), pl.ds(2 * (q % 2), 2)]
        return remote(
            ref, ref, g_s.at[h, 0], g_r.at[h, 0, way, passed(n)], x_dev(1 if way == 0 else 3)
        )

    def turn_y(h, way, n, yt, q):
        first = wrap(x - q // 2, NX) * 2 + q % 2
        ref = st.at[h, yt, :, pl.ds(pl.multiple_of(first * 2 * BL, 2 * BL), 2 * BL)]
        return remote(
            ref, ref, g_s.at[h, 1], g_r.at[h, 1, way, passed(n)], up if way == 0 else down
        )

    xl, xr, xo = wrap(x - 1, NX), wrap(x + 1, NX), wrap(x + 2, NX)
    yd, yu, yo = wrap(y - 1, NY), wrap(y + 1, NY), wrap(y + 2, NY)

    def turn_own(h, q):
        for way in range(2):
            turn_x(h, way, q, x, q).start()
            turn_y(h, way, q, y, q).start()

    def turn_step(h, q):
        turn_x(h, 0, q, xl, q).wait_recv()
        turn_y(h, 0, q, yd, q).wait_recv()
        if q < 4:
            turn_x(h, 0, 8 + q, xl, q).start()
            turn_y(h, 0, 8 + q, yd, q).start()
        turn_x(h, 1, q, xr, q).wait_recv()
        turn_y(h, 1, q, yu, q).wait_recv()
        if q >= 4:
            turn_x(h, 1, 4 + q, xr, q).start()
            turn_y(h, 1, 4 + q, yu, q).start()

    def turn_end(h):
        for way in range(2):
            several(sx.at[h, 0, pl.ds(0, 2)], g_s.at[h, 0], g_r.at[h, 0, way, 8]).wait_recv()
            several(st.at[h, 0, :, pl.ds(0, 2 * HALF * BL)], g_s.at[h, 1], g_r.at[h, 1, way, 8]).wait_recv()

    def product(hr, yts, hc, xts):
        lhs = jnp.concatenate([st[hr, yt] for yt in yts], axis=0)
        rhs = jnp.concatenate(
            [sx[hc, xt].reshape(NX * HALF * BL, BL) for xt in xts], axis=1
        )
        part = jnp.dot(lhs, rhs, preferred_element_type=jnp.float32)
        mid = BL // 2
        for i, yt in enumerate(yts):
            for k, xt in enumerate(xts):
                cols = pl.ds(xt * BL if isinstance(xt, int) else pl.multiple_of(xt * BL, BL), BL)
                upper = part[i * BL:i * BL + mid, k * BL:(k + 1) * BL]
                lower = part[i * BL + mid:(i + 1) * BL, k * BL:(k + 1) * BL]
                if hc == 0:
                    tile = (upper + swap(lower)).reshape(2, 32, BL)
                else:
                    tile = (swap(upper) + lower).reshape(2, 32, BL)
                    tile = jnp.where(on_left[0:mid].reshape(2, 32, BL), gram[yt, hr, :, :, cols], tile)
                gram[yt, hr, :, :, cols] = tile

    @pl.loop(0, 16)
    def _(r):
        pass_step(2, x1b, r)
        step_two(0, wrap(x - r // 4, NX), lax.rem(r, 4))

        @pl.when(lax.rem(r, 2) == 1)
        def _():
            turn_own(0, r // 2)

    pass_on(2, x1b, 16, 22)
    for q in range(4):
        turn_step(0, q)
    sends_done(1, x1a)
    pass_on(2, x1b, 22, 26)
    for q in range(4, 8):
        turn_step(0, q)
    pass_on(2, x1b, 26, flow_len(2))
    partner_done(2, x1b)

    @pl.loop(0, 2 * NX)
    def _(q):
        for i in range(2):
            step_two(1, wrap(x - q // 2, NX), 2 * lax.rem(q, 2) + i)
        turn_own(1, q)

    turn_end(0)
    every = list(range(NY))
    product(0, every, 0, [0, 1])
    product(0, every, 0, [2, 3])
    for q in range(2 * NX):
        turn_step(1, q)
    near_y = [y, yd, yu]
    product(1, near_y, 0, [0, 1])
    product(1, near_y, 0, [2, 3])
    product(0, every, 1, [x, xl])
    product(0, every, 1, [xr])
    product(1, near_y, 1, [x, xl])
    product(1, near_y, 1, [xr])
    turn_end(1)
    product(0, every, 1, [xo])

    def other_core(e):
        return remote(gram.at[:, e, 1 - core], r1.at[e], a_s.at[e], a_r.at[e], partner)

    def to_owner(n):
        return remote(rz.at[n % 2, n // 2], r3.at[z], c_s.at[0], c_r.at[0], (sink(n), y))

    def to_owners(e):
        other_core(e).wait_recv()
        for yt in range(NY):
            n = 2 * yt + e
            rz[e, yt] = (r1[e, yt] + gram[yt, e, core]).astype(jnp.bfloat16)

            @pl.when(sink(n) != me)
            def _():
                to_owner(n).start()

    other_core(0).start()
    product(1, near_y, 1, [xo])
    product(1, [yo], 0, [0, 1])
    product(1, [yo], 0, [2, 3])
    to_owners(0)
    product(1, [yo], 1, [x, xl])
    product(1, [yo], 1, [xr, xo])
    other_core(1).start()
    to_owners(1)

    for xt in range(NX):
        cols = pl.ds(xt * BL, BL)
        for p in range(HALF):
            half_a = sx[0, xt, x, p].astype(jnp.float32)
            half_b = sx[1, xt, x, p].astype(jnp.float32)
            whole[p, :, cols] = jnp.where(on_left, half_a, swap(half_b)).astype(jnp.bfloat16)
            whole[p + HALF, :, cols] = jnp.where(on_left, swap(half_a), half_b).astype(jnp.bfloat16)
    own_out = pltpu.make_async_copy(whole, out, loc.at[0])
    own_out.start()
    for h in range(2):
        several(sx.at[h, pl.ds(0, 3)], g_s.at[h, 0], g_r.at[h, 0, 0, 8]).wait_send()
        several(st.at[h, pl.ds(0, 3)], g_s.at[h, 1], g_r.at[h, 1, 0, 8]).wait_send()
    sends_done(2, x1b)
    for e in range(2):
        other_core(e).wait_send()

    @pl.when(source(z) == me)
    def _():
        r3[z] = rz[lax.rem(x, 2), z // 2]

    def all_sums(do):
        @pl.when(source(z) == me)
        def _():
            do(several(r3.at[pl.ds(0, nz - 1)], c_s.at[0], c_r.at[0]))

        @pl.when(source(z) != me)
        def _():
            do(several(r3, c_s.at[0], c_r.at[0]))

    all_sums(lambda copies: copies.wait_recv())
    total = r3[0].astype(jnp.float32)
    for zz in range(1, nz):
        total += r3[zz].astype(jnp.float32)
    cov[...] = total * scale
    all_sums(lambda copies: copies.wait_send())
    own_out.wait()


def diffuse(expression, affinity, near, far, count, nz):
    shards = nz * 2 * NX
    flow_len = 4 * (nz // 2) - 2
    dma = pltpu.SemaphoreType.DMA
    any_spec = pl.BlockSpec(memory_space=pl.ANY)
    return pl.pallas_call(
        functools.partial(diffuse_kernel, nz, 1.0 / (shards * BLK * BL)),
        out_shape=(
            jax.ShapeDtypeStruct(expression.shape, jnp.bfloat16),
            jax.ShapeDtypeStruct((32, NX * BL), jnp.float32),
        ),
        in_specs=[any_spec] * 5,
        out_specs=(any_spec, pl.BlockSpec(memory_space=pltpu.VMEM)),
        scratch_shapes=[
            pltpu.VMEM((shards * BLK + 1, BL, BL), jnp.bfloat16),
            pltpu.VMEM((shards * HALF + 1, BL, BL), jnp.bfloat16),
            pltpu.VMEM((shards * HALF + 1, BL, BL), jnp.bfloat16),
            pltpu.VMEM((NX, BLK, SLOTS, BL, BL), jnp.bfloat16),
            pltpu.VMEM((NX, 6 * BLK, BL), jnp.int32),
            pltpu.SMEM((NX, 6 * BLK, BL), jnp.int32),
            pltpu.VMEM((LOC, BLK), jnp.int32),
            pltpu.VMEM((BLK, BLK), jnp.int32),
            pltpu.SMEM((BLK,), jnp.int32),
            pltpu.VMEM((2, BL // BLK, BL), jnp.bfloat16),
            pltpu.VMEM((2, NX, NX, HALF, BL, BL), jnp.bfloat16),
            pltpu.VMEM((2, NY, BL, NX * HALF * BL), jnp.bfloat16),
            pltpu.VMEM((BLK, BL, NX * BL), jnp.bfloat16),
            pltpu.VMEM((NY, 2, 2, 32, NX * BL), jnp.float32),
            pltpu.VMEM((2, NY, 32, NX * BL), jnp.float32),
            pltpu.VMEM((2, NY, 32, NX * BL), jnp.bfloat16),
            pltpu.VMEM((nz, 32, NX * BL), jnp.bfloat16),
            dma((5,)),
            dma((1,)), dma((3,)),
            dma((1,)), dma((1,)),
            dma((1,)), dma((2, 4)), dma((2, 2)), dma((1,)),
            dma((3,)), dma((2, 2, 2 * flow_len)),
            dma((3,)), dma((3,)),
            dma((2, 2)), dma((2, 2, 2, 9)),
            dma((2,)), dma((2,)),
            dma((1,)), dma((1,)),
        ],
        compiler_params=pltpu.CompilerParams(
            collective_id=0, has_side_effects=True, vmem_limit_bytes=60 * 2**20
        ),
    )(expression, affinity, near, far, count)


def last_kernel(smoothed, covariance, smoothed_out, covariance_out):
    smoothed_out[...] = smoothed[...]
    covariance_out[...] = covariance[...]


def hand_over(smoothed, covariance):
    vmem = pl.BlockSpec(memory_space=pltpu.VMEM)
    return pl.pallas_call(
        last_kernel,
        out_shape=(
            jax.ShapeDtypeStruct(smoothed.shape, smoothed.dtype),
            jax.ShapeDtypeStruct(covariance.shape, covariance.dtype),
        ),
        in_specs=[vmem, vmem],
        out_specs=(vmem, vmem),
    )(smoothed, covariance)


def body(nz, expression, affinity, near_blocks, far_blocks, far_count):
    blocks = expression.reshape(BLK, BL, expression.shape[1])
    current, covariance = hand_over(*diffuse(
        blocks, affinity, near_blocks.T, far_blocks, far_count, nz
    ))
    return (current.reshape(expression.shape), covariance)


def solution(mesh):
    nz = mesh.shape["cells"] // (2 * NX)
    return jax.shard_map(
        functools.partial(body, nz),
        mesh=mesh,
        in_specs=(
            P("cells", "genes"),
            P("cells", None, None, None),
            P("cells", None),
            P("cells", None),
            P("cells"),
        ),
        out_specs=(P("cells", "genes"), P("cells", "genes")),
        check_vma=False,
    )
```

```python
import functools

import jax
import jax.numpy as jnp
from jax import lax
from jax.experimental import pallas as pl
from jax.experimental.pallas import tpu as pltpu
from jax.sharding import PartitionSpec as P

MESH = pl.DeviceIdType.MESH
NX = 4
NY = 4
BL = 128
BLK = 8
SLOTS = 12
LOC = 4
HALF = BLK // 2


def remote(src, dst, send, recv, device):
    return pltpu.make_async_remote_copy(
        src_ref=src, dst_ref=dst, send_sem=send, recv_sem=recv, device_id=device, device_id_type=MESH
    )


def diffuse_kernel(
    nz, scale, expr, aff, near, far, count, out, cov, x0, x1a, x1b, w, lv, ls,
    near_v, far_v, count_s, lanes, sx, st, whole, gram, r1, rz, r3,
    loc, xs_s, xs_r, li_s, li_r, w_s, wx_r, wf_r, wy_r,
    z_s, z_r, p_s, p_r, g_s, g_r, a_s, a_r, c_s, c_r,
):
    me = lax.axis_index("cells")
    y = lax.axis_index("genes")
    core = lax.rem(me, 2)
    x = lax.rem(me // 2, NX)
    z = me // (2 * NX)
    half = lax.rem(y, 2)

    def cell(zz, xx, kk):
        return (zz * NX + xx) * 2 + kk

    def wrap(v, n):
        return lax.rem(v + n, n)

    def x_dev(d):
        return (cell(z, wrap(x + d, NX), core), y)

    right = (cell(wrap(z + 1, nz), x, core), y)
    left = (cell(wrap(z - 1, nz), x, core), y)
    partner = (cell(z, x, 1 - core), y)
    up = (me, wrap(y + 1, NY))
    down = (me, wrap(y - 1, NY))

    def sink(yt, e):
        return cell(2 * yt + x // 2, 2 * lax.rem(x, 2) + e, core)

    def source(zz):
        return cell(zz, 2 * lax.rem(z, 2) + x // 2, core)

    barrier = pltpu.get_barrier_semaphore()
    peers = [x_dev(1), x_dev(2), x_dev(3), right, left, partner, up, down]
    for peer in peers:
        pl.semaphore_signal(barrier, inc=1, device_id=peer, device_id_type=MESH)
    for zz in range(nz):
        @pl.when(source(zz) != me)
        def _():
            pl.semaphore_signal(barrier, inc=1, device_id=(source(zz), y), device_id_type=MESH)

    def piece(buf, shard, size=BLK):
        return buf.at[pl.ds(shard * size, size)]

    def columns(ref, xx):
        return ref.at[:, :, pl.ds(pl.multiple_of(xx * BL, BL), BL)]

    def deal(d, u):
        rows = pl.ds(HALF * u, HALF)
        return remote(
            columns(expr, wrap(x + d, NX)).at[rows], piece(x0, me).at[rows],
            xs_s.at[0], xs_r.at[d - 1, u], x_dev(d),
        )

    own_in = pltpu.make_async_copy(columns(expr, x), piece(x0, me), loc.at[0])
    def names(d):
        return remote(lv.at[x], lv.at[x], li_s.at[0], li_r.at[0], x_dev(d))

    own_w = pltpu.make_async_copy(aff, w.at[x], loc.at[2])

    def wsub(xx, hh, i):
        return w.at[xx, 4 * hh + i]

    def w_first(way, n):
        i = n if way == 0 else 3 - n
        return remote(
            aff.at[4 * half + i], wsub(x, half, i), w_s.at[0], wx_r.at[way, n],
            x_dev(1 if way == 0 else 3),
        )

    def w_forward(way, n):
        i = n if way == 0 else 3 - n
        ref = wsub(wrap(x - 1, NX) if way == 0 else wrap(x + 1, NX), half, i)
        return remote(ref, ref, w_s.at[0], wf_r.at[way, n], x_dev(1 if way == 0 else 3))

    def w_across(e, i):
        ref = wsub(wrap(x + (3, 1, 2)[e], NX), half, i)
        return remote(ref, ref, w_s.at[0], wy_r.at[0], up if i < 2 else down)

    def w_serve(n):
        for way in range(2):
            i = n % 4 if way == 0 else 3 - n % 4
            if n < 4:
                w_first(way, n).wait_recv()
                if n < 2:
                    w_forward(way, n).start()
                w_across(way, i).start()
            else:
                w_forward(way, n - 4).wait_recv()
                w_across(2, i).start()

    unit = 2 * NX
    flow_len = unit * (nz // 2) - unit // 2

    def shard_of(zz, j, kk):
        return cell(wrap(zz, nz), wrap(x - j, NX), kk)

    def place(n, zz, q, kk):
        shard, upper = shard_of(zz, q // 2, kk), lax.rem(q, 2)
        return shard * BLK + HALF * upper if n == 0 else shard * HALF + 2 * upper

    def part_of(n, buf, first):
        return buf.at[pl.ds(first, HALF if n == 0 else 2)]

    def z_copy(n, buf, way, s, first):
        ref = part_of(n, buf, first)
        return remote(
            ref, ref, z_s.at[n], z_r.at[n % 2, way, s], right if way == 0 else left
        )

    def p_copy(n, buf, first):
        ref = part_of(n, buf, first)
        return remote(ref, ref, p_s.at[n], p_r.at[n], partner)

    def from_left(n, r, kk):
        return place(n, z - 1 - r // unit, lax.rem(r, unit), kk)

    def from_right(n, r, kk):
        half_unit = unit // 2
        q = lax.rem(r, unit) + jnp.where(r < flow_len - half_unit, 0, half_unit)
        return place(n, z + 1 + r // unit, q, kk)

    def send_own(n, buf, q):
        first = place(n, z, q, core)
        z_copy(n, buf, 0, q, first).start()
        z_copy(n, buf, 1, q, first).start()
        p_copy(n, buf, first).start()

    def pass_step(n, buf, r):
        size, last = unit, flow_len
        first = from_left(n, r, core)
        z_copy(n, buf, 0, r, first).wait_recv()

        @pl.when(r + size < last)
        def _():
            z_copy(n, buf, 0, r + size, first).start()

        p_copy(n, buf, first).start()
        other = from_right(n, r, core)
        z_copy(n, buf, 1, r, other).wait_recv()

        @pl.when(r < last - size - size // 2)
        def _():
            z_copy(n, buf, 1, r + size, other).start()

        @pl.when((r >= last - size) & (r < last - size // 2))
        def _():
            z_copy(n, buf, 1, r + size // 2, other).start()

        p_copy(n, buf, other).start()

    def pass_on(n, buf, first, last):
        @pl.loop(first, last)
        def _(r):
            pass_step(n, buf, r)

    def several(ref, send, recv):
        return remote(ref, ref, send, recv, partner)

    def partner_done(n, buf):
        size = (HALF if n == 0 else 2) * (unit + 2 * flow_len)
        several(buf.at[pl.ds(0, size)], p_s.at[n], p_r.at[n]).wait_recv()

    def sends_done(n, buf):
        size = HALF if n == 0 else 2
        z_all, p_all = size * 2 * flow_len, size * (unit + 2 * flow_len)
        several(buf.at[pl.ds(0, z_all)], z_s.at[n], p_r.at[n]).wait_send()
        several(buf.at[pl.ds(0, p_all)], p_s.at[n], p_r.at[n]).wait_send()

    def name(xs, b, slot, part=0):
        first = 2 * BLK * part
        return ls[xs, first + BLK + slot, b] if slot < LOC else ls[xs, first + b, slot - LOC]

    def weighted(xs, b, rows):
        return jnp.dot(
            jnp.concatenate([w[xs, b, slot] for slot in range(SLOTS)], axis=1),
            jnp.concatenate([rows(slot) for slot in range(SLOTS)], axis=0),
            preferred_element_type=jnp.float32,
        )

    on_left = lax.broadcasted_iota(jnp.int32, (BL, BL), 1) < BL // 2

    def swap(tile):
        return pltpu.roll(tile, BL // 2, 1)

    def step_one(xs, p, shard):
        low, high = [weighted(xs, b, lambda slot: x0[name(xs, b, slot)]) for b in (p, p + HALF)]
        x1a[shard * HALF + p] = jnp.where(on_left, low, swap(high)).astype(jnp.bfloat16)
        x1b[shard * HALF + p] = jnp.where(on_left, swap(low), high).astype(jnp.bfloat16)

    def step_two(h, xs, p):
        buf = x1a if h == 0 else x1b

        def one(b):
            def rows(slot):
                tile = buf[name(xs, b, slot, 1)].reshape(BLK, BL // BLK, BL)
                return (tile * lanes[name(xs, b, slot, 2)][None]).reshape(BL, BL)

            both = weighted(xs, b, rows)
            return both + swap(both)

        tile = jnp.where(on_left, one(p), one(p + HALF)).astype(jnp.bfloat16)
        sx[h, x, xs, p] = tile
        st[h, y, :, pl.ds(pl.multiple_of((xs * HALF + p) * BL, BL), BL)] = tile.T

    small = [
        pltpu.make_async_copy(near, near_v, loc.at[1]),
        pltpu.make_async_copy(far, far_v, loc.at[3]),
        pltpu.make_async_copy(count, count_s, loc.at[4]),
    ]
    for copy in small:
        copy.start()
    own_in.start()
    own_w.start()
    zeros = jnp.zeros((BL, BL), jnp.bfloat16)
    x0[nz * 2 * NX * BLK] = zeros
    x1a[nz * 2 * NX * HALF] = zeros
    x1b[nz * 2 * NX * HALF] = zeros
    for i in range(2):
        keep = on_left if i == 0 else jnp.logical_not(on_left)
        lanes[i] = jnp.where(keep, 1.0, 0.0)[0:BL // BLK].astype(jnp.bfloat16)
    for copy in small:
        copy.wait()
    slot = lax.broadcasted_iota(jnp.int32, (1, BLK), 1)
    lv[x] = jnp.zeros((6 * BLK, BL), jnp.int32)
    for b in range(BLK):
        lv[x, b:b + 1, 0:BLK] = jnp.where(slot < count_s[b], far_v[b:b + 1, :], nz * 2 * NX * BLK)
    lv[x, BLK:BLK + LOC, 0:BLK] = near_v[...]
    block = lv[x, 0:2 * BLK, :]
    lv[x, 2 * BLK:4 * BLK, :] = (block >> 3) * HALF + (block & (HALF - 1))
    lv[x, 4 * BLK:6 * BLK, :] = (block >> 2) & 1
    own_in.wait()
    pl.semaphore_wait(barrier, len(peers) + nz - jnp.where(source(z) == me, 1, 0))

    send_own(0, x0, 0)
    send_own(0, x0, 1)
    for u in range(2):
        for d in (1, 3, 2):
            deal(d, u).start()
    for d in (1, 2, 3):
        names(d).start()
    for n in range(4):
        w_first(0, n).start()
        w_first(1, n).start()
    for j, u in ((1, 0), (3, 0), (1, 1), (3, 1), (2, 0), (2, 1)):
        deal(j, u).wait_recv()
        send_own(0, x0, 2 * j + u)
    cuts = (0, 8, 12, 16, 18, 22, 24)
    for part in range(6):
        pass_on(0, x0, cuts[part], cuts[part + 1])
        w_serve(part)
    several(lv.at[pl.ds(0, NX - 1)], li_s.at[0], li_r.at[0]).wait_recv()
    to_smem = pltpu.make_async_copy(lv, ls, loc.at[1])
    to_smem.start()
    to_smem.wait()
    own_w.wait()
    pass_on(0, x0, 24, flow_len)
    several(w.at[pl.ds(0, 3), pl.ds(0, 4)], w_s.at[0], wy_r.at[0]).wait_recv()
    partner_done(0, x0)

    @pl.loop(0, 2 * NX)
    def _(q):
        j = q // 2
        for i in range(2):
            step_one(wrap(x - j, NX), 2 * lax.rem(q, 2) + i, shard_of(z, j, core))
        send_own(1, x1a, q)

    pass_on(1, x1a, 0, 16)
    several(piece(x0, 0, 3 * BLK), xs_s.at[0], xs_r.at[0]).wait_send()
    several(lv.at[pl.ds(0, NX - 1)], li_s.at[0], li_r.at[0]).wait_send()
    several(w.at[pl.ds(0, 3)], w_s.at[0], wy_r.at[0]).wait_send()
    sends_done(0, x0)
    pass_on(1, x1a, 16, 20)

    @pl.loop(20, flow_len)
    def _(r):
        pass_step(1, x1a, r)
        send_own(2, x1b, r - 20)

    partner_done(1, x1a)

    def passed(n):
        return min(n, 8) if isinstance(n, int) else n

    def turn_x(h, way, n, xt, q):
        ref = sx.at[h, xt, q // 2, pl.ds(2 * (q % 2), 2)]
        return remote(
            ref, ref, g_s.at[h, 0], g_r.at[h, 0, way, passed(n)], x_dev(1 if way == 0 else 3)
        )

    def turn_y(h, way, n, yt, q):
        cells = pl.ds(q * 2 * BL if isinstance(q, int) else pl.multiple_of(q * 2 * BL, 2 * BL), 2 * BL)
        ref = st.at[h, yt, :, cells]
        return remote(
            ref, ref, g_s.at[h, 1], g_r.at[h, 1, way, passed(n)], up if way == 0 else down
        )

    xl, xr, xo = wrap(x - 1, NX), wrap(x + 1, NX), wrap(x + 2, NX)
    yd, yu, yo = wrap(y - 1, NY), wrap(y + 1, NY), wrap(y + 2, NY)

    def turn_own(h, q):
        for way in range(2):
            turn_x(h, way, q, x, q).start()
            turn_y(h, way, q, y, q).start()

    def turn_step(h, q):
        turn_x(h, 0, q, xl, q).wait_recv()
        turn_y(h, 0, q, yd, q).wait_recv()
        if q < 4:
            turn_x(h, 0, 8 + q, xl, q).start()
            turn_y(h, 0, 8 + q, yd, q).start()
        turn_x(h, 1, q, xr, q).wait_recv()
        turn_y(h, 1, q, yu, q).wait_recv()
        if q >= 4:
            turn_x(h, 1, 4 + q, xr, q).start()
            turn_y(h, 1, 4 + q, yu, q).start()

    def turn_end(h, way):
        several(sx.at[h, 0, pl.ds(0, 2)], g_s.at[h, 0], g_r.at[h, 0, way, 8]).wait_recv()
        several(st.at[h, 0, :, pl.ds(0, 2 * HALF * BL)], g_s.at[h, 1], g_r.at[h, 1, way, 8]).wait_recv()

    ys, xs_all = (y, yd, yu, yo), (x, xl, xr, xo)

    def product(part, hr, rows, hc, cols):
        cells = 2 * HALF * BL
        lhs = jnp.concatenate([st[hr, ys[r], :, pl.ds(part * cells, cells)] for r in rows], axis=0)
        rhs = jnp.concatenate(
            [sx[hc, xs_all[c], pl.ds(2 * part, 2)].reshape(cells, BL) for c in cols], axis=1
        )
        sums = jnp.dot(lhs, rhs, preferred_element_type=jnp.float32)
        mid = BL // 2
        mine = on_left[0:mid] if hc == 0 else jnp.logical_not(on_left[0:mid])
        for i, r in enumerate(rows):
            for k, c in enumerate(cols):
                at = pl.ds(c * BL, BL)
                upper = sums[i * BL:i * BL + mid, k * BL:(k + 1) * BL]
                lower = sums[i * BL + mid:(i + 1) * BL, k * BL:(k + 1) * BL]
                tile = upper + swap(lower) if hc == 0 else swap(upper) + lower
                if part == 0 and hc == 0:
                    gram[r, hr, :, :, at] = tile.reshape(2, 32, BL)
                else:
                    old = gram[r, hr, :, :, at].reshape(mid, BL)
                    new = tile if part == 0 else old + tile
                    gram[r, hr, :, :, at] = jnp.where(mine, new, old).reshape(2, 32, BL)

    @pl.loop(0, 16)
    def _(r):
        pass_step(2, x1b, r)
        step_two(0, r // 4, lax.rem(r, 4))

        @pl.when(lax.rem(r, 2) == 1)
        def _():
            turn_own(0, r // 2)

    pass_on(2, x1b, 16, 22)
    for q in range(4):
        turn_step(0, q)
    sends_done(1, x1a)
    pass_on(2, x1b, 22, 26)
    for q in range(4, 8):
        turn_step(0, q)
    pass_on(2, x1b, 26, flow_len)
    partner_done(2, x1b)

    @pl.loop(0, 2 * NX)
    def _(q):
        for i in range(2):
            step_two(1, q // 2, 2 * lax.rem(q, 2) + i)
        turn_own(1, q)

    turn_end(0, 0)
    turn_end(0, 1)
    every, near_y = [0, 1, 2, 3], [0, 1, 2]
    for part in range(2):
        product(part, 0, every, 0, [0, 1])
        product(part, 0, every, 0, [2, 3])

    def early(part):
        product(part, 1, near_y, 0, [0, 1])
        product(part, 1, near_y, 0, [2, 3])
        product(part, 0, every, 1, [0, 1])
        product(part, 0, every, 1, [2])
        product(part, 1, near_y, 1, [0, 1])
        product(part, 1, near_y, 1, [2])

    def late(part):
        product(part, 0, every, 1, [3])
        product(part, 1, near_y, 1, [3])
        product(part, 1, [3], 0, [0, 1])
        product(part, 1, [3], 0, [2, 3])
        product(part, 1, [3], 1, [0, 1])
        product(part, 1, [3], 1, [2, 3])

    old_cols, new_cols, all_cols = pl.ds(0, 3 * BL), pl.ds(3 * BL, BL), pl.ds(0, NX * BL)
    rounds = (
        ((0, 0, 4, old_cols), (1, 0, 3, old_cols)),
        ((0, 0, 4, new_cols), (1, 0, 3, new_cols), (1, 3, 1, all_cols)),
    )

    def other_core(i, k):
        e, first, size, at = rounds[i][k]
        rows = pl.ds(first, size)
        return remote(
            gram.at[rows, e, 1 - core, :, at], r1.at[e, rows, :, at],
            a_s.at[2 * i + k], a_r.at[2 * i + k], partner,
        )

    def to_cores(i):
        for k in range(len(rounds[i])):
            other_core(i, k).start()

    def to_owners(i):
        for k, (e, first, size, at) in enumerate(rounds[i]):
            other_core(i, k).wait_recv()
            for r in range(first, first + size):
                rz[e, r, :, at] = (r1[e, r, :, at] + gram[r, e, core, :, at]).astype(jnp.bfloat16)
                owner = sink(ys[r], e)

                @pl.when(owner != me)
                def _():
                    remote(
                        rz.at[e, r, :, at], r3.at[z, :, at], c_s.at[0], c_r.at[0], (owner, y)
                    ).start()

    for q in range(2 * NX):
        turn_step(1, q)
    early(0)
    early(1)
    to_cores(0)
    turn_end(1, 0)
    late(0)
    to_owners(0)
    turn_end(1, 1)
    late(1)
    to_cores(1)
    to_owners(1)

    for xt in range(NX):
        cols = pl.ds(xt * BL, BL)
        for p in range(HALF):
            half_a = sx[0, xt, x, p].astype(jnp.float32)
            half_b = sx[1, xt, x, p].astype(jnp.float32)
            whole[p, :, cols] = jnp.where(on_left, half_a, swap(half_b)).astype(jnp.bfloat16)
            whole[p + HALF, :, cols] = jnp.where(on_left, swap(half_a), half_b).astype(jnp.bfloat16)
    own_out = pltpu.make_async_copy(whole, out, loc.at[0])
    own_out.start()
    for h in range(2):
        several(sx.at[h, pl.ds(0, 3)], g_s.at[h, 0], g_r.at[h, 0, 0, 8]).wait_send()
        several(st.at[h, pl.ds(0, 3)], g_s.at[h, 1], g_r.at[h, 1, 0, 8]).wait_send()
    sends_done(2, x1b)
    for i in range(2):
        for k in range(len(rounds[i])):
            other_core(i, k).wait_send()

    @pl.when(source(z) == me)
    def _():
        mine = z // 2
        r3[z] = rz[lax.rem(x, 2), jnp.where(mine == y, 0, jnp.where(mine == yd, 1, jnp.where(mine == yu, 2, 3)))]

    def all_sums(do):
        @pl.when(source(z) == me)
        def _():
            do(several(r3.at[pl.ds(0, nz - 1)], c_s.at[0], c_r.at[0]))

        @pl.when(source(z) != me)
        def _():
            do(several(r3, c_s.at[0], c_r.at[0]))

    all_sums(lambda copies: copies.wait_recv())
    total = r3[0].astype(jnp.float32)
    for zz in range(1, nz):
        total += r3[zz].astype(jnp.float32)
    total = total * scale
    from_x = 2 * lax.rem(z, 2) + x // 2
    for c, shift in enumerate((0, NX - 1, 1, 2)):
        cov[:, pl.ds(pl.multiple_of(lax.rem(from_x + shift, NX) * BL, BL), BL)] = total[:, c * BL:(c + 1) * BL]
    all_sums(lambda copies: copies.wait_send())
    own_out.wait()


def diffuse(expression, affinity, near, far, count, nz):
    shards = nz * 2 * NX
    flow_len = 2 * NX * (nz // 2) - NX
    dma = pltpu.SemaphoreType.DMA
    any_spec = pl.BlockSpec(memory_space=pl.ANY)
    return pl.pallas_call(
        functools.partial(diffuse_kernel, nz, 1.0 / (shards * BLK * BL)),
        out_shape=(
            jax.ShapeDtypeStruct(expression.shape, jnp.bfloat16),
            jax.ShapeDtypeStruct((32, NX * BL), jnp.float32),
        ),
        in_specs=[any_spec] * 5,
        out_specs=(any_spec, pl.BlockSpec(memory_space=pltpu.VMEM)),
        scratch_shapes=[
            pltpu.VMEM((shards * BLK + 1, BL, BL), jnp.bfloat16),
            pltpu.VMEM((shards * HALF + 1, BL, BL), jnp.bfloat16),
            pltpu.VMEM((shards * HALF + 1, BL, BL), jnp.bfloat16),
            pltpu.VMEM((NX, BLK, SLOTS, BL, BL), jnp.bfloat16),
            pltpu.VMEM((NX, 6 * BLK, BL), jnp.int32),
            pltpu.SMEM((NX, 6 * BLK, BL), jnp.int32),
            pltpu.VMEM((LOC, BLK), jnp.int32),
            pltpu.VMEM((BLK, BLK), jnp.int32),
            pltpu.SMEM((BLK,), jnp.int32),
            pltpu.VMEM((2, BL // BLK, BL), jnp.bfloat16),
            pltpu.VMEM((2, NX, NX, HALF, BL, BL), jnp.bfloat16),
            pltpu.VMEM((2, NY, BL, NX * HALF * BL), jnp.bfloat16),
            pltpu.VMEM((BLK, BL, NX * BL), jnp.bfloat16),
            pltpu.VMEM((NY, 2, 2, 32, NX * BL), jnp.float32),
            pltpu.VMEM((2, NY, 32, NX * BL), jnp.float32),
            pltpu.VMEM((2, NY, 32, NX * BL), jnp.bfloat16),
            pltpu.VMEM((nz, 32, NX * BL), jnp.bfloat16),
            dma((5,)),
            dma((1,)), dma((3, 2)),
            dma((1,)), dma((1,)),
            dma((1,)), dma((2, 4)), dma((2, 2)), dma((1,)),
            dma((3,)), dma((2, 2, flow_len)),
            dma((3,)), dma((3,)),
            dma((2, 2)), dma((2, 2, 2, 9)),
            dma((5,)), dma((5,)),
            dma((1,)), dma((1,)),
        ],
        compiler_params=pltpu.CompilerParams(
            collective_id=0, has_side_effects=True, vmem_limit_bytes=60 * 2**20
        ),
    )(expression, affinity, near, far, count)


def last_kernel(smoothed, covariance, smoothed_out, covariance_out):
    smoothed_out[...] = smoothed[...]
    covariance_out[...] = covariance[...]


def hand_over(smoothed, covariance):
    vmem = pl.BlockSpec(memory_space=pltpu.VMEM)
    return pl.pallas_call(
        last_kernel,
        out_shape=(
            jax.ShapeDtypeStruct(smoothed.shape, smoothed.dtype),
            jax.ShapeDtypeStruct(covariance.shape, covariance.dtype),
        ),
        in_specs=[vmem, vmem],
        out_specs=(vmem, vmem),
    )(smoothed, covariance)


def body(nz, expression, affinity, near_blocks, far_blocks, far_count):
    blocks = expression.reshape(BLK, BL, expression.shape[1])
    current, covariance = hand_over(*diffuse(
        blocks, affinity, near_blocks.T, far_blocks, far_count, nz
    ))
    return (current.reshape(expression.shape), covariance)


def solution(mesh):
    nz = mesh.shape["cells"] // (2 * NX)
    return jax.shard_map(
        functools.partial(body, nz),
        mesh=mesh,
        in_specs=(
            P("cells", "genes"),
            P("cells", None, None, None),
            P("cells", None),
            P("cells", None),
            P("cells"),
        ),
        out_specs=(P("cells", "genes"), P("cells", "genes")),
        check_vma=False,
    )
```

```python
import functools

import jax
import jax.numpy as jnp
from jax import lax
from jax.experimental import pallas as pl
from jax.experimental.pallas import tpu as pltpu
from jax.sharding import PartitionSpec as P

MESH = pl.DeviceIdType.MESH
NX = 4
NY = 4
BL = 128
BLK = 8
SLOTS = 12
CHUNKS = 4
LOC = 4
HALF = BLK // 2


def remote(src, dst, send, recv, device):
    return pltpu.make_async_remote_copy(
        src_ref=src, dst_ref=dst, send_sem=send, recv_sem=recv, device_id=device, device_id_type=MESH
    )


def diffuse_kernel(
    nz, scale, expr, aff, near, far, count, out, cov, x0, x1a, x1b, w, lv, ls,
    near_v, far_v, count_s, lanes, sx, st, whole, gram, r1, rz, r3,
    loc, xs_s, xs_r, li_s, li_r, w_s, wx_r, wf_r, wy_r,
    z_s, z_r, p_s, p_r, g_s, g_r, a_s, a_r, c_s, c_r,
):
    me = lax.axis_index("cells")
    y = lax.axis_index("genes")
    core = lax.rem(me, 2)
    x = lax.rem(me // 2, NX)
    z = me // (2 * NX)
    half = lax.rem(y, 2)

    def cell(zz, xx, kk):
        return (zz * NX + xx) * 2 + kk

    def wrap(v, n):
        return lax.rem(v + n, n)

    def x_dev(d):
        return (cell(z, wrap(x + d, NX), core), y)

    right = (cell(wrap(z + 1, nz), x, core), y)
    left = (cell(wrap(z - 1, nz), x, core), y)
    partner = (cell(z, x, 1 - core), y)
    up = (me, wrap(y + 1, NY))
    down = (me, wrap(y - 1, NY))

    def sink(yt, e):
        return cell(2 * yt + x // 2, 2 * lax.rem(x, 2) + e, core)

    def source(zz):
        return cell(zz, 2 * lax.rem(z, 2) + x // 2, core)

    barrier = pltpu.get_barrier_semaphore()
    peers = [x_dev(1), x_dev(2), x_dev(3), right, left, partner, up, down]
    for peer in peers:
        pl.semaphore_signal(barrier, inc=1, device_id=peer, device_id_type=MESH)
    for zz in range(nz):
        @pl.when(source(zz) != me)
        def _():
            pl.semaphore_signal(barrier, inc=1, device_id=(source(zz), y), device_id_type=MESH)

    def piece(buf, shard, size=BLK):
        return buf.at[pl.ds(shard * size, size)]

    def columns(ref, xx):
        return ref.at[:, :, pl.ds(pl.multiple_of(xx * BL, BL), BL)]

    def deal(d, u):
        rows = pl.ds(HALF * u, HALF)
        return remote(
            columns(expr, wrap(x + d, NX)).at[rows], piece(x0, me).at[rows],
            xs_s.at[0], xs_r.at[d - 1, u], x_dev(d),
        )

    own_in = pltpu.make_async_copy(columns(expr, x), piece(x0, me), loc.at[0])
    def names(d):
        return remote(lv.at[x], lv.at[x], li_s.at[0], li_r.at[0], x_dev(d))

    own_w = pltpu.make_async_copy(aff, w.at[x], loc.at[2])

    def wsub(xx, hh, i):
        return w.at[xx, 4 * hh + i]

    def w_first(way, n):
        i = n if way == 0 else 3 - n
        return remote(
            aff.at[4 * half + i], wsub(x, half, i), w_s.at[0], wx_r.at[way, n],
            x_dev(1 if way == 0 else 3),
        )

    def w_forward(way, n):
        i = n if way == 0 else 3 - n
        ref = wsub(wrap(x - 1, NX) if way == 0 else wrap(x + 1, NX), half, i)
        return remote(ref, ref, w_s.at[0], wf_r.at[way, n], x_dev(1 if way == 0 else 3))

    def w_across(e, i):
        ref = wsub(wrap(x + (3, 1, 2)[e], NX), half, i)
        return remote(ref, ref, w_s.at[0], wy_r.at[0], up if i < 2 else down)

    def w_serve(n):
        for way in range(2):
            i = n % 4 if way == 0 else 3 - n % 4
            if n < 4:
                w_first(way, n).wait_recv()
                if n < 2:
                    w_forward(way, n).start()
                w_across(way, i).start()
            else:
                w_forward(way, n - 4).wait_recv()
                w_across(2, i).start()

    unit = 2 * NX
    flow_len = unit * (nz // 2) - unit // 2

    def shard_of(zz, j, kk):
        return cell(wrap(zz, nz), wrap(x - j, NX), kk)

    def place(n, zz, q, kk):
        shard, upper = shard_of(zz, q // 2, kk), lax.rem(q, 2)
        return shard * BLK + HALF * upper if n == 0 else shard * HALF + 2 * upper

    def part_of(n, buf, first):
        return buf.at[pl.ds(first, HALF if n == 0 else 2)]

    def z_copy(n, buf, way, s, first):
        ref = part_of(n, buf, first)
        return remote(
            ref, ref, z_s.at[n], z_r.at[n % 2, way, s], right if way == 0 else left
        )

    def p_copy(n, buf, first):
        ref = part_of(n, buf, first)
        return remote(ref, ref, p_s.at[n], p_r.at[n], partner)

    def from_left(n, r, kk):
        return place(n, z - 1 - r // unit, lax.rem(r, unit), kk)

    def from_right(n, r, kk):
        half_unit = unit // 2
        q = lax.rem(r, unit) + jnp.where(r < flow_len - half_unit, 0, half_unit)
        return place(n, z + 1 + r // unit, q, kk)

    def send_own(n, buf, q):
        first = place(n, z, q, core)
        z_copy(n, buf, 0, q, first).start()
        z_copy(n, buf, 1, q, first).start()
        p_copy(n, buf, first).start()

    def pass_step(n, buf, r):
        size, last = unit, flow_len
        first = from_left(n, r, core)
        z_copy(n, buf, 0, r, first).wait_recv()

        @pl.when(r + size < last)
        def _():
            z_copy(n, buf, 0, r + size, first).start()

        p_copy(n, buf, first).start()
        other = from_right(n, r, core)
        z_copy(n, buf, 1, r, other).wait_recv()

        @pl.when(r < last - size - size // 2)
        def _():
            z_copy(n, buf, 1, r + size, other).start()

        @pl.when((r >= last - size) & (r < last - size // 2))
        def _():
            z_copy(n, buf, 1, r + size // 2, other).start()

        p_copy(n, buf, other).start()

    def pass_on(n, buf, first, last):
        @pl.loop(first, last)
        def _(r):
            pass_step(n, buf, r)

    def several(ref, send, recv):
        return remote(ref, ref, send, recv, partner)

    def partner_done(n, buf):
        size = (HALF if n == 0 else 2) * (unit + 2 * flow_len)
        several(buf.at[pl.ds(0, size)], p_s.at[n], p_r.at[n]).wait_recv()

    def sends_done(n, buf):
        size = HALF if n == 0 else 2
        z_all, p_all = size * 2 * flow_len, size * (unit + 2 * flow_len)
        several(buf.at[pl.ds(0, z_all)], z_s.at[n], p_r.at[n]).wait_send()
        several(buf.at[pl.ds(0, p_all)], p_s.at[n], p_r.at[n]).wait_send()

    def name(xs, b, slot, part=0):
        first = 2 * BLK * part
        return ls[xs, first + BLK + slot, b] if slot < LOC else ls[xs, first + b, slot - LOC]

    def weighted(xs, b, rows):
        return jnp.dot(
            jnp.concatenate([w[xs, b, slot] for slot in range(SLOTS)], axis=1),
            jnp.concatenate([rows(slot) for slot in range(SLOTS)], axis=0),
            preferred_element_type=jnp.float32,
        )

    on_left = lax.broadcasted_iota(jnp.int32, (BL, BL), 1) < BL // 2

    def swap(tile):
        return pltpu.roll(tile, BL // 2, 1)

    def step_one(xs, p, shard):
        low, high = [weighted(xs, b, lambda slot: x0[name(xs, b, slot)]) for b in (p, p + HALF)]
        x1a[shard * HALF + p] = jnp.where(on_left, low, swap(high)).astype(jnp.bfloat16)
        x1b[shard * HALF + p] = jnp.where(on_left, swap(low), high).astype(jnp.bfloat16)

    def step_two(h, xs, p):
        buf = x1a if h == 0 else x1b

        def one(b):
            def rows(slot):
                tile = buf[name(xs, b, slot, 1)].reshape(BLK, BL // BLK, BL)
                return (tile * lanes[name(xs, b, slot, 2)][None]).reshape(BL, BL)

            both = weighted(xs, b, rows)
            return both + swap(both)

        tile = jnp.where(on_left, one(p), one(p + HALF)).astype(jnp.bfloat16)
        sx[h, x, xs, p] = tile
        st[h, y, :, pl.ds(pl.multiple_of((xs * HALF + p) * BL, BL), BL)] = tile.T

    small = [
        pltpu.make_async_copy(near, near_v, loc.at[1]),
        pltpu.make_async_copy(far, far_v, loc.at[3]),
        pltpu.make_async_copy(count, count_s, loc.at[4]),
    ]
    for copy in small:
        copy.start()
    own_in.start()
    own_w.start()
    zeros = jnp.zeros((BL, BL), jnp.bfloat16)
    x0[nz * 2 * NX * BLK] = zeros
    x1a[nz * 2 * NX * HALF] = zeros
    x1b[nz * 2 * NX * HALF] = zeros
    for i in range(2):
        keep = on_left if i == 0 else jnp.logical_not(on_left)
        lanes[i] = jnp.where(keep, 1.0, 0.0)[0:BL // BLK].astype(jnp.bfloat16)
    for copy in small:
        copy.wait()
    slot = lax.broadcasted_iota(jnp.int32, (1, BLK), 1)
    lv[x] = jnp.zeros((6 * BLK, BL), jnp.int32)
    for b in range(BLK):
        lv[x, b:b + 1, 0:BLK] = jnp.where(slot < count_s[b], far_v[b:b + 1, :], nz * 2 * NX * BLK)
    lv[x, BLK:BLK + LOC, 0:BLK] = near_v[...]
    block = lv[x, 0:2 * BLK, :]
    lv[x, 2 * BLK:4 * BLK, :] = (block >> 3) * HALF + (block & (HALF - 1))
    lv[x, 4 * BLK:6 * BLK, :] = (block >> 2) & 1
    own_in.wait()
    pl.semaphore_wait(barrier, len(peers) + nz - jnp.where(source(z) == me, 1, 0))

    send_own(0, x0, 0)
    send_own(0, x0, 1)
    for u in range(2):
        for d in (1, 3, 2):
            deal(d, u).start()
    for d in (1, 2, 3):
        names(d).start()
    for n in range(4):
        w_first(0, n).start()
        w_first(1, n).start()
    for j, u in ((1, 0), (3, 0), (1, 1), (3, 1), (2, 0), (2, 1)):
        deal(j, u).wait_recv()
        send_own(0, x0, 2 * j + u)
    cuts = (0, 7, 11, 15, 17, 21, 24)
    for part in range(6):
        pass_on(0, x0, cuts[part], cuts[part + 1])
        w_serve(part)
    several(lv.at[pl.ds(0, NX - 1)], li_s.at[0], li_r.at[0]).wait_recv()
    to_smem = pltpu.make_async_copy(lv, ls, loc.at[1])
    to_smem.start()
    to_smem.wait()
    own_w.wait()
    pass_on(0, x0, 24, flow_len)
    several(w.at[pl.ds(0, 3), pl.ds(0, 4)], w_s.at[0], wy_r.at[0]).wait_recv()
    partner_done(0, x0)

    @pl.loop(0, 2 * NX)
    def _(q):
        j = q // 2
        for i in range(2):
            step_one(wrap(x - j, NX), 2 * lax.rem(q, 2) + i, shard_of(z, j, core))
        send_own(1, x1a, q)

    pass_on(1, x1a, 0, 16)
    several(piece(x0, 0, 3 * BLK), xs_s.at[0], xs_r.at[0]).wait_send()
    several(lv.at[pl.ds(0, NX - 1)], li_s.at[0], li_r.at[0]).wait_send()
    several(w.at[pl.ds(0, 3)], w_s.at[0], wy_r.at[0]).wait_send()
    sends_done(0, x0)
    pass_on(1, x1a, 16, 19)

    @pl.loop(19, flow_len - 1)
    def _(r):
        pass_step(1, x1a, r)
        send_own(2, x1b, r - 19)

    pass_on(1, x1a, flow_len - 1, flow_len)
    partner_done(1, x1a)

    def passed(n):
        return min(n, 8) if isinstance(n, int) else n

    def turn_x(h, way, n, xt, q):
        ref = sx.at[h, xt, q // 2, pl.ds(2 * (q % 2), 2)]
        return remote(
            ref, ref, g_s.at[h, 0], g_r.at[h, 0, way, passed(n)], x_dev(1 if way == 0 else 3)
        )

    def turn_y(h, way, n, yt, q):
        cells = pl.ds(q * 2 * BL if isinstance(q, int) else pl.multiple_of(q * 2 * BL, 2 * BL), 2 * BL)
        ref = st.at[h, yt, :, cells]
        return remote(
            ref, ref, g_s.at[h, 1], g_r.at[h, 1, way, passed(n)], up if way == 0 else down
        )

    xl, xr, xo = wrap(x - 1, NX), wrap(x + 1, NX), wrap(x + 2, NX)
    yd, yu, yo = wrap(y - 1, NY), wrap(y + 1, NY), wrap(y + 2, NY)

    def turn_own(h, q):
        for way in range(2):
            turn_x(h, way, q, x, q).start()
            turn_y(h, way, q, y, q).start()

    def turn_step(h, q):
        turn_x(h, 0, q, xl, q).wait_recv()
        turn_y(h, 0, q, yd, q).wait_recv()
        if q < 4:
            turn_x(h, 0, 8 + q, xl, q).start()
            turn_y(h, 0, 8 + q, yd, q).start()
        turn_x(h, 1, q, xr, q).wait_recv()
        turn_y(h, 1, q, yu, q).wait_recv()
        if q >= 4:
            turn_x(h, 1, 4 + q, xr, q).start()
            turn_y(h, 1, 4 + q, yu, q).start()

    def turn_end(h, way):
        several(sx.at[h, 0, pl.ds(0, 2)], g_s.at[h, 0], g_r.at[h, 0, way, 8]).wait_recv()
        several(st.at[h, 0, :, pl.ds(0, 2 * HALF * BL)], g_s.at[h, 1], g_r.at[h, 1, way, 8]).wait_recv()

    ys, xs_all = (y, yd, yu, yo), (x, xl, xr, xo)

    def product(hr, rows, hc, cols):
        lhs = jnp.concatenate([st[hr, ys[r]] for r in rows], axis=0)
        rhs = jnp.concatenate(
            [sx[hc, xs_all[c]].reshape(NX * HALF * BL, BL) for c in cols], axis=1
        )
        sums = jnp.dot(lhs, rhs, preferred_element_type=jnp.float32)
        mid = BL // 2
        for i, r in enumerate(rows):
            for k, c in enumerate(cols):
                at = pl.ds(c * BL, BL)
                upper = sums[i * BL:i * BL + mid, k * BL:(k + 1) * BL]
                lower = sums[i * BL + mid:(i + 1) * BL, k * BL:(k + 1) * BL]
                tile = upper + swap(lower) if hc == 0 else swap(upper) + lower
                if hc == 1:
                    tile = jnp.where(on_left[0:mid], gram[r, hr, :, :, at].reshape(mid, BL), tile)
                gram[r, hr, :, :, at] = tile.reshape(2, 32, BL)

    @pl.loop(0, 16)
    def _(r):
        pass_step(2, x1b, r)
        step_two(0, r // 4, lax.rem(r, 4))

        @pl.when(lax.rem(r, 2) == 1)
        def _():
            turn_own(0, r // 2)

    pass_on(2, x1b, 16, 22)
    for q in range(4):
        turn_step(0, q)
    sends_done(1, x1a)
    pass_on(2, x1b, 22, 26)
    for q in range(4, 8):
        turn_step(0, q)
    pass_on(2, x1b, 26, flow_len)
    partner_done(2, x1b)

    @pl.loop(0, 2 * NX)
    def _(q):
        for i in range(2):
            step_two(1, q // 2, 2 * lax.rem(q, 2) + i)
        turn_own(1, q)

    turn_end(0, 0)
    turn_end(0, 1)
    every, near_y = [0, 1, 2, 3], [0, 1, 2]
    product(0, every, 0, [0, 1])
    product(0, every, 0, [2, 3])

    def early():
        product(1, near_y, 0, [0, 1])
        product(1, near_y, 0, [2, 3])
        product(0, every, 1, [0, 1])
        product(0, every, 1, [2])
        product(1, near_y, 1, [0, 1])
        product(1, near_y, 1, [2])

    def late():
        product(0, every, 1, [3])
        product(1, near_y, 1, [3])
        product(1, [3], 0, [0, 1])
        product(1, [3], 0, [2, 3])
        product(1, [3], 1, [0, 1])
        product(1, [3], 1, [2, 3])

    old_cols, new_cols, all_cols = pl.ds(0, 3 * BL), pl.ds(3 * BL, BL), pl.ds(0, NX * BL)
    rounds = (
        ((0, 0, 4, old_cols), (1, 0, 3, old_cols)),
        ((0, 0, 4, new_cols), (1, 0, 3, new_cols), (1, 3, 1, all_cols)),
    )

    def other_core(i, k):
        e, first, size, at = rounds[i][k]
        rows = pl.ds(first, size)
        return remote(
            gram.at[rows, e, 1 - core, :, at], r1.at[e, rows, :, at],
            a_s.at[2 * i + k], a_r.at[2 * i + k], partner,
        )

    def to_cores(i):
        for k in range(len(rounds[i])):
            other_core(i, k).start()

    def to_owners(i):
        for k, (e, first, size, at) in enumerate(rounds[i]):
            other_core(i, k).wait_recv()
            for r in range(first, first + size):
                rz[e, r, :, at] = (r1[e, r, :, at] + gram[r, e, core, :, at]).astype(jnp.bfloat16)
                owner = sink(ys[r], e)

                @pl.when(owner != me)
                def _():
                    remote(
                        rz.at[e, r, :, at], r3.at[z, :, at], c_s.at[0], c_r.at[0], (owner, y)
                    ).start()

    for q in range(2 * NX):
        turn_step(1, q)
    early()
    to_cores(0)
    turn_end(1, 0)
    to_owners(0)
    turn_end(1, 1)
    late()
    to_cores(1)
    to_owners(1)

    for xt in range(NX):
        cols = pl.ds(xt * BL, BL)
        for p in range(HALF):
            half_a = sx[0, xt, x, p].astype(jnp.float32)
            half_b = sx[1, xt, x, p].astype(jnp.float32)
            whole[p, :, cols] = jnp.where(on_left, half_a, swap(half_b)).astype(jnp.bfloat16)
            whole[p + HALF, :, cols] = jnp.where(on_left, swap(half_a), half_b).astype(jnp.bfloat16)
    own_out = pltpu.make_async_copy(whole, out, loc.at[0])
    own_out.start()
    for h in range(2):
        several(sx.at[h, pl.ds(0, 3)], g_s.at[h, 0], g_r.at[h, 0, 0, 8]).wait_send()
        several(st.at[h, pl.ds(0, 3)], g_s.at[h, 1], g_r.at[h, 1, 0, 8]).wait_send()
    sends_done(2, x1b)
    for i in range(2):
        for k in range(len(rounds[i])):
            other_core(i, k).wait_send()

    @pl.when(source(z) == me)
    def _():
        mine = z // 2
        r3[z] = rz[lax.rem(x, 2), jnp.where(mine == y, 0, jnp.where(mine == yd, 1, jnp.where(mine == yu, 2, 3)))]

    def all_sums(do):
        @pl.when(source(z) == me)
        def _():
            do(several(r3.at[pl.ds(0, nz - 1)], c_s.at[0], c_r.at[0]))

        @pl.when(source(z) != me)
        def _():
            do(several(r3, c_s.at[0], c_r.at[0]))

    all_sums(lambda copies: copies.wait_recv())
    total = r3[0].astype(jnp.float32)
    for zz in range(1, nz):
        total += r3[zz].astype(jnp.float32)
    total = total * scale
    from_x = 2 * lax.rem(z, 2) + x // 2
    for c, shift in enumerate((0, NX - 1, 1, 2)):
        cov[:, pl.ds(pl.multiple_of(lax.rem(from_x + shift, NX) * BL, BL), BL)] = total[:, c * BL:(c + 1) * BL]
    all_sums(lambda copies: copies.wait_send())
    own_out.wait()


def diffuse(expression, affinity, near, far, count, nz):
    shards = nz * 2 * NX
    flow_len = 2 * NX * (nz // 2) - NX
    dma = pltpu.SemaphoreType.DMA
    any_spec = pl.BlockSpec(memory_space=pl.ANY)
    return pl.pallas_call(
        functools.partial(diffuse_kernel, nz, 1.0 / (shards * BLK * BL)),
        out_shape=(
            jax.ShapeDtypeStruct(expression.shape, jnp.bfloat16),
            jax.ShapeDtypeStruct((32, NX * BL), jnp.float32),
        ),
        in_specs=[any_spec] * 5,
        out_specs=(any_spec, pl.BlockSpec(memory_space=pltpu.VMEM)),
        scratch_shapes=[
            pltpu.VMEM((shards * BLK + 1, BL, BL), jnp.bfloat16),
            pltpu.VMEM((shards * HALF + 1, BL, BL), jnp.bfloat16),
            pltpu.VMEM((shards * HALF + 1, BL, BL), jnp.bfloat16),
            pltpu.VMEM((NX, BLK, SLOTS, BL, BL), jnp.bfloat16),
            pltpu.VMEM((NX, 6 * BLK, BL), jnp.int32),
            pltpu.SMEM((NX, 6 * BLK, BL), jnp.int32),
            pltpu.VMEM((LOC, BLK), jnp.int32),
            pltpu.VMEM((BLK, BLK), jnp.int32),
            pltpu.SMEM((BLK,), jnp.int32),
            pltpu.VMEM((2, BL // BLK, BL), jnp.bfloat16),
            pltpu.VMEM((2, NX, NX, HALF, BL, BL), jnp.bfloat16),
            pltpu.VMEM((2, NY, BL, NX * HALF * BL), jnp.bfloat16),
            pltpu.VMEM((BLK, BL, NX * BL), jnp.bfloat16),
            pltpu.VMEM((NY, 2, 2, 32, NX * BL), jnp.float32),
            pltpu.VMEM((2, NY, 32, NX * BL), jnp.float32),
            pltpu.VMEM((2, NY, 32, NX * BL), jnp.bfloat16),
            pltpu.VMEM((nz, 32, NX * BL), jnp.bfloat16),
            dma((5,)),
            dma((1,)), dma((3, 2)),
            dma((1,)), dma((1,)),
            dma((1,)), dma((2, 4)), dma((2, 2)), dma((1,)),
            dma((3,)), dma((2, 2, flow_len)),
            dma((3,)), dma((3,)),
            dma((2, 2)), dma((2, 2, 2, 9)),
            dma((5,)), dma((5,)),
            dma((1,)), dma((1,)),
        ],
        compiler_params=pltpu.CompilerParams(
            collective_id=0, has_side_effects=True, vmem_limit_bytes=60 * 2**20
        ),
    )(expression, affinity, near, far, count)


def last_kernel(smoothed, covariance, smoothed_out, covariance_out, held, held_too, sems):
    parts = [(covariance, held_too, covariance_out)]
    for i in range(CHUNKS):
        rows = pl.ds(i * (BLK // CHUNKS), BLK // CHUNKS)
        parts.append((smoothed.at[rows], held.at[rows], smoothed_out.at[rows]))
    ins = [pltpu.make_async_copy(p[0], p[1], sems.at[0, i]) for i, p in enumerate(parts)]
    outs = [pltpu.make_async_copy(p[1], p[2], sems.at[1, i]) for i, p in enumerate(parts)]
    for copy in ins:
        copy.start()
    for first, second in zip(ins, outs):
        first.wait()
        second.start()
    for copy in outs:
        copy.wait()


def hand_over(smoothed, covariance):
    any_spec = pl.BlockSpec(memory_space=pl.ANY)
    return pl.pallas_call(
        last_kernel,
        out_shape=(
            jax.ShapeDtypeStruct(smoothed.shape, smoothed.dtype),
            jax.ShapeDtypeStruct(covariance.shape, covariance.dtype),
        ),
        in_specs=[any_spec, any_spec],
        out_specs=(any_spec, any_spec),
        scratch_shapes=[
            pltpu.VMEM(smoothed.shape, smoothed.dtype),
            pltpu.VMEM(covariance.shape, covariance.dtype),
            pltpu.SemaphoreType.DMA((2, CHUNKS + 1)),
        ],
    )(smoothed, covariance)


def body(nz, expression, affinity, near_blocks, far_blocks, far_count):
    blocks = expression.reshape(BLK, BL, expression.shape[1])
    current, covariance = hand_over(*diffuse(
        blocks, affinity, near_blocks.T, far_blocks, far_count, nz
    ))
    return (current.reshape(expression.shape), covariance)


def solution(mesh):
    nz = mesh.shape["cells"] // (2 * NX)
    return jax.shard_map(
        functools.partial(body, nz),
        mesh=mesh,
        in_specs=(
            P("cells", "genes"),
            P("cells", None, None, None),
            P("cells", None),
            P("cells", None),
            P("cells"),
        ),
        out_specs=(P("cells", "genes"), P("cells", "genes")),
        check_vma=False,
    )
```
